32 devices in a mesh: dp: 8 (over z, core), comp: 4 (over y, x).
Axes of the slice: x: 2, y: 2, z: 4, core: 2. Of those that a mesh axis runs over, the one named last changes fastest.
Arguments:
- embeddings: float32 [8192, 768], P('dp'), may hold values from -6 to 6
- comp_means: float32 [2048, 768], P(('comp', 'dp')), may hold values from -1.2 to 1.2
- comp_variances: float32 [2048, 768], P(('comp', 'dp')), may hold values from 0.8 to 1.25
- comp_mass: float32 [2048], P(('comp', 'dp')), may hold values from 0.3 to 3
Outputs:
- new_means: float32 [2048, 768], P(('comp', 'dp'))
- new_variances: float32 [2048, 768], P(('comp', 'dp'))
- new_mass: float32 [2048], P(('comp', 'dp'))
The draws below stay inside these ranges and needn't reach their ends.
All inputs are finite; a program needn't handle non-finite values.
Results may differ from the reference program's by a relative error of at most 0.0003.
Values sent between devices are 32-bit elements; how exact they have to be, the bound alone decides.
No kernel may reach another device: no remote copies, remote signals or barrier semaphores. Data moves between devices by JAX's collectives and lax.ppermute only.
A program may use at most 64 MiB of HBM per device.

```python
import math
import jax
import jax.numpy as jnp
from jax import lax

D = 768
ROW_DEV = 1024
K = 2048
ROWS = 8192
N_DP = 8


def draw_embeddings(key, part):
    key_main = jax.random.fold_in(key, 11)
    values_drawn = jax.random.normal(key_main, (ROWS, D), jnp.float32)
    return jnp.clip(values_drawn, -6.0, 6.0)


def block_levels(key, extent, pieces, least, high):
    factor_of = 1.0
    for dim, shards_of in pieces:
        draws = jax.random.uniform(jax.random.fold_in(jax.random.fold_in(key, 6), dim), (shards_of,), jnp.float32, least / len(pieces), high / len(pieces))
        factor_of = factor_of * jnp.repeat(jnp.exp(draws), extent[dim] // shards_of).reshape((-1,) + (1,) * (len(extent) - 1 - dim))
    return factor_of


def bell_draw(own_key, shape, scale, bound, cuts=(), dtype=jnp.bfloat16):
    values = jax.random.normal(own_key, shape, jnp.float32) * scale
    if len(cuts) > 0:
        values = block_levels(own_key, shape, cuts, -0.22, 0.18) * values
    return jnp.clip(values, min=-bound, max=bound).astype(dtype)


def setup_inputs(seed: int = 0) -> dict:
    seeds = jax.random.split(jax.random.key(seed), 5)
    embeddings = draw_embeddings(jax.random.fold_in(seeds[4], 71), 0)
    comp_means = bell_draw(seeds[1], (K, D), 0.2, 1.2, ((0, 32),), jnp.float32)
    comp_variances = jnp.clip(jnp.exp(math.log(1.25) - 0.4462871 * jax.random.uniform(seeds[2], (K, D), jnp.float32) ** block_levels(seeds[2], (K, D), ((0, 32),), -0.2, 0.2)), 0.8, 1.25)
    comp_mass = jnp.clip(jnp.exp(math.log(3.0) - 2.3025851 * jax.random.uniform(seeds[3], (K,), jnp.float32) ** block_levels(seeds[3], (K,), ((0, 32),), -0.2, 0.2)), 0.3, 3.0)
    return {"embeddings": embeddings, "comp_means": comp_means, "comp_variances": comp_variances, "comp_mass": comp_mass}


def coefficients(comp_means, comp_variances, comp_mass):
    precision = 1.0 / comp_variances
    neg_half = -0.5 * precision
    mean_prec = comp_means * precision
    offset = jnp.log(comp_mass) - 0.5 * jnp.sum(jnp.log(comp_variances) + comp_means * mean_prec, axis=1)
    return neg_half, mean_prec, offset


def scores_of(row_block, squares, neg_half, mean_prec, offset):
    highest = lax.Precision.HIGHEST
    quad = jnp.dot(squares, neg_half.T, precision=highest, preferred_element_type=jnp.float32)
    linear = jnp.dot(row_block, mean_prec.T, precision=highest, preferred_element_type=jnp.float32)
    return quad + linear + offset[None, :]


def moments_of(responsibility, values):
    return lax.dot_general(responsibility, values, (((0,), (0,)), ((), ())), precision=lax.Precision.HIGHEST, preferred_element_type=jnp.float32)


def reference(embeddings, comp_means, comp_variances, comp_mass):
    neg_half, mean_prec, offset = coefficients(comp_means, comp_variances, comp_mass)
    blocks = embeddings.reshape(N_DP, ROW_DEV, D)

    def accumulate(running, row_block):
        squares = row_block * row_block
        scores = scores_of(row_block, squares, neg_half, mean_prec, offset)
        row_peak = jnp.max(scores, axis=1, keepdims=True)
        shifted = jnp.exp(scores - row_peak)
        row_total = jnp.sum(shifted, axis=1, keepdims=True)
        responsibility = shifted / row_total
        first_sums = running[0] + moments_of(responsibility, row_block)
        second_sums = running[1] + moments_of(responsibility, squares)
        counts = running[2] + jnp.sum(responsibility, axis=0)
        return (first_sums, second_sums, counts), None

    initial = (jnp.zeros((K, D), jnp.float32), jnp.zeros((K, D), jnp.float32), jnp.zeros((K,), jnp.float32))
    totals, unused = lax.scan(accumulate, initial, blocks)
    first_sums, second_sums, counts = totals
    mass_scale = K / ROWS
    new_mass = 0.4 * comp_mass + 0.6 * mass_scale * counts
    first_moment = 0.4 * comp_mass[:, None] * comp_means + 0.6 * mass_scale * first_sums
    second_moment = 0.4 * comp_mass[:, None] * (comp_variances + comp_means * comp_means) + 0.6 * mass_scale * second_sums
    new_means = first_moment / new_mass[:, None]
    new_variances = second_moment / new_mass[:, None] - new_means * new_means
    return (new_means, new_variances, new_mass)
```

```python
import jax
import jax.numpy as jnp
from jax import lax
from jax.sharding import PartitionSpec as P

HIGH = lax.Precision.HIGH


def swap(value, axis, bit):
    size = lax.axis_size(axis)
    return lax.ppermute(value, axis, [(i, i ^ bit) for i in range(size)])


def gather_planes(piece):
    planes = lax.axis_size("dp") // 2
    held = {0: piece}
    bit = planes // 2
    while bit:
        held.update({q ^ bit: swap(value, "dp", 2 * bit) for q, value in held.items()})
        bit //= 2
    return [held[q] for q in range(planes)]


def scatter_planes(parts):
    planes = lax.axis_size("dp") // 2
    held = dict(enumerate(parts))
    bit = 1
    while bit < planes:
        sent = sorted((q for q in held if q & bit), reverse=True)
        for q in sent:
            held[q ^ bit] = held[q ^ bit] + swap(held.pop(q), "dp", 2 * bit)
        bit *= 2
    return held[0]


def row_stats(scores):
    peak = jnp.max(scores, axis=0)
    return peak, jnp.sum(jnp.exp(scores - peak[None, :]), axis=0)


def merge(stats):
    stacked = jnp.stack(stats)
    peak = jnp.max(stacked[:, :, 0], axis=0)
    total = jnp.sum(stacked[:, :, 1] * jnp.exp(stacked[:, :, 0] - peak[None]), axis=0)
    return jnp.stack([peak, total], axis=1)


def per_device(embeddings, comp_means, comp_variances, comp_mass):
    f32 = jnp.float32
    variances = gather_planes(comp_variances)
    means = gather_planes(comp_means)
    masses = gather_planes(comp_mass)
    rows = [embeddings, swap(embeddings, "dp", 1)]
    squares = [block * block for block in rows]

    variances = jnp.concatenate(variances)
    means = jnp.concatenate(means)
    masses = jnp.concatenate(masses)
    precision = 1.0 / variances
    neg_half = -0.5 * precision
    mean_prec = means * precision
    offset = jnp.log(masses) - 0.5 * jnp.sum(jnp.log(variances) + means * mean_prec, axis=1)

    def score(block, square):
        across = (((1,), (1,)), ((), ()))
        quad = lax.dot_general(neg_half, square, across, precision=HIGH, preferred_element_type=f32)
        linear = lax.dot_general(mean_prec, block, across, precision=HIGH, preferred_element_type=f32)
        return quad + linear + offset[:, None]

    scores = [score(block, square) for block, square in zip(rows, squares)]
    stats = jnp.stack([jnp.stack(row_stats(s)) for s in scores])
    stats = merge([stats, swap(stats, "dp", 1)[::-1]])
    n_comp = lax.axis_size("comp")
    stats = merge([stats] + [swap(stats, "comp", q) for q in range(1, n_comp)])
    resp = [jnp.exp(s - stats[b, 0][None, :]) / stats[b, 1][None, :] for b, s in enumerate(scores)]

    def moments(values):
        within = (((1,), (0,)), ((), ()))
        return sum(
            lax.dot_general(r, v, within, precision=HIGH, preferred_element_type=f32)
            for r, v in zip(resp, values)
        )

    planes = lax.axis_size("dp") // 2
    counts = sum(jnp.sum(r, axis=1) for r in resp)
    first_sums = scatter_planes(jnp.split(moments(rows), planes))
    second_sums = scatter_planes(jnp.split(moments(squares), planes))
    counts = scatter_planes(jnp.split(counts, planes))

    total_comps = comp_means.shape[0] * lax.axis_size("dp") * lax.axis_size("comp")
    total_rows = embeddings.shape[0] * lax.axis_size("dp")
    mass_scale = total_comps / total_rows
    new_mass = 0.4 * comp_mass + 0.6 * mass_scale * counts
    first_moment = 0.4 * comp_mass[:, None] * comp_means + 0.6 * mass_scale * first_sums
    second_moment = (
        0.4 * comp_mass[:, None] * (comp_variances + comp_means * comp_means)
        + 0.6 * mass_scale * second_sums
    )
    new_means = first_moment / new_mass[:, None]
    new_variances = second_moment / new_mass[:, None] - new_means * new_means
    return (new_means, new_variances, new_mass)


def solution(mesh):
    placed = (P("dp", None), P(("comp", "dp"), None), P(("comp", "dp"), None), P(("comp", "dp")))
    return jax.shard_map(
        per_device,
        mesh=mesh,
        in_specs=placed,
        out_specs=(P(("comp", "dp"), None), P(("comp", "dp"), None), P(("comp", "dp"))),
        check_vma=False,
    )
```

```python
import functools

import jax
import jax.numpy as jnp
from jax import lax
from jax.experimental import pallas as pl
from jax.experimental.pallas import tpu as pltpu
from jax.sharding import PartitionSpec as P

F32 = jnp.float32
BF16 = jnp.bfloat16
LANES = 128
ACROSS = (((1,), (1,)), ((), ()))
WITHIN = (((1,), (0,)), ((), ()))


def params(megabytes):
    return pltpu.CompilerParams(vmem_limit_bytes=megabytes * 1024 * 1024)


def whole(shape):
    return pl.BlockSpec(shape, lambda *_: (0,) * len(shape))


def split(value):
    high = value.astype(BF16)
    return high, (value - high.astype(F32)).astype(BF16)


def diagonal(rows, columns):
    shape = (rows, columns)
    return lax.broadcasted_iota(jnp.int32, shape, 0) == lax.broadcasted_iota(jnp.int32, shape, 1)


def to_row(column, lanes):
    return jnp.sum(jnp.where(diagonal(column.shape[0], lanes), column, 0.0), axis=0, keepdims=True)


def to_column(row, rows):
    return jnp.sum(jnp.where(diagonal(rows, row.shape[1]), row, 0.0), axis=1, keepdims=True)


def coefficient_kernel(means_ref, variances_ref, mass_ref, quad_ref, linear_ref):
    n, width = means_ref.shape
    means, variances = means_ref[...], variances_ref[...]
    precision = 1.0 / variances
    neg_half = -0.5 * precision
    mean_prec = means * precision
    sums = jnp.sum(jnp.log(variances) + means * mean_prec, axis=1, keepdims=True)
    offset = to_column(jnp.log(mass_ref[...]), n) - 0.5 * sums
    for c in range(width // LANES):
        lanes = slice(c * LANES, (c + 1) * LANES)
        quad_ref[c * n : (c + 1) * n, :] = neg_half[:, lanes]
        linear_ref[c * n : (c + 1) * n, :] = mean_prec[:, lanes]
    quad_ref[width // LANES * n :, :] = jnp.broadcast_to(to_row(offset, LANES), (8, LANES))


def coefficients(means, variances, mass):
    n, width = means.shape
    tiles = width // LANES * n
    return pl.pallas_call(
        coefficient_kernel,
        out_shape=(
            jax.ShapeDtypeStruct((tiles + 8, LANES), F32),
            jax.ShapeDtypeStruct((tiles, LANES), F32),
        ),
        compiler_params=params(16),
        name="coefficients",
    )(means, variances, mass.reshape(1, n))


def halves_kernel(own_ref, other_ref, xh_ref, xl_ref, sh_ref, sl_ref):
    def put(block):
        xh_ref[...], xl_ref[...] = split(block)
        sh_ref[...], sl_ref[...] = split(block * block)

    first = pl.program_id(0) < pl.num_programs(0) // 2

    @pl.when(first)
    def _():
        put(own_ref[...])

    @pl.when(jnp.logical_not(first))
    def _():
        put(other_ref[...])


def halves(own, other):
    rows, width = own.shape
    tile = min(256, rows)
    steps = rows // tile
    out = jax.ShapeDtypeStruct((2 * rows, width), BF16)
    return pl.pallas_call(
        halves_kernel,
        grid=(2 * steps,),
        in_specs=[
            pl.BlockSpec((tile, width), lambda i: (jnp.minimum(i, steps - 1), 0)),
            pl.BlockSpec((tile, width), lambda i: (jnp.maximum(i - steps, 0), 0)),
        ],
        out_specs=[pl.BlockSpec((tile, width), lambda i: (i, 0))] * 4,
        out_shape=[out] * 4,
        compiler_params=params(16),
        cost_estimate=pl.CostEstimate(
            flops=20 * rows * width, bytes_accessed=24 * rows * width, transcendentals=0
        ),
        name="halves",
    )(own, other)


def load_packs(packs, weights, n):
    comps = n * len(packs)
    for q, pack in enumerate(packs):
        for c in range(weights.shape[1] // LANES):
            lanes = slice(c * LANES, (c + 1) * LANES)
            high, low = split(pack[c * n : (c + 1) * n, :])
            weights[q * n : (q + 1) * n, lanes] = high
            weights[comps + q * n : comps + (q + 1) * n, lanes] = low


def product(weights, high, low, dims):
    comps = weights.shape[0] // 2
    both = lax.dot_general(weights, high, dims, preferred_element_type=F32)
    rest = lax.dot_general(weights[:comps], low, dims, preferred_element_type=F32)
    return both[:comps] + (both[comps:] + rest)


def quad_kernel(n, *refs):
    *packs, high_ref, low_ref, out_ref, weights, offset = refs

    @pl.when(pl.program_id(0) == 0)
    def _():
        load_packs(packs, weights, n)
        tiles = weights.shape[1] // LANES * n
        for q, pack in enumerate(packs):
            column = to_column(pack[tiles : tiles + 1, :], n)
            offset[q * n : (q + 1) * n, :] = jnp.broadcast_to(column, (n, LANES))

    scores = product(weights[...], high_ref[...], low_ref[...], ACROSS)
    out_ref[...] = scores + offset[:, :1]


def linear_kernel(n, *refs):
    *packs, quad_ref, high_ref, low_ref, out_ref, stats_ref, weights = refs

    @pl.when(pl.program_id(0) == 0)
    def _():
        load_packs(packs, weights, n)

    scores = quad_ref[...] + product(weights[...], high_ref[...], low_ref[...], ACROSS)
    out_ref[...] = scores
    peak = jnp.max(scores, axis=0, keepdims=True)
    stats_ref[0, 0:1, :] = peak
    stats_ref[0, 1:2, :] = jnp.sum(jnp.exp(scores - peak), axis=0, keepdims=True)


def score_call(body, packs, n, extra, high, low, name):
    rows, width = high.shape
    comps = n * len(packs)
    tile = min(256, rows // 2)
    steps = rows // 2 // tile
    row_block = pl.BlockSpec((tile, width), lambda i: (i, 0))
    score_block = pl.BlockSpec((comps, tile), lambda i: (0, i))
    out_specs, out_shape = [score_block], [jax.ShapeDtypeStruct((comps, rows), F32)]
    scratch = [pltpu.VMEM((2 * comps, width), BF16)]
    if extra:
        out_specs.append(pl.BlockSpec((1, 2, tile), lambda i: (i // steps, 0, i % steps)))
        out_shape.append(jax.ShapeDtypeStruct((2, 2, rows // 2), F32))
    else:
        scratch.append(pltpu.VMEM((comps, LANES), F32))
    return pl.pallas_call(
        functools.partial(body, n),
        grid=(2 * steps,),
        in_specs=[whole(pack.shape) for pack in packs]
        + [score_block] * len(extra)
        + [row_block, row_block],
        out_specs=out_specs,
        out_shape=out_shape,
        scratch_shapes=scratch,
        compiler_params=params(24),
        cost_estimate=pl.CostEstimate(
            flops=6 * rows * width * comps,
            bytes_accessed=4 * rows * (width + comps),
            transcendentals=rows * comps * len(extra),
        ),
        name=name,
    )(*packs, *extra, high, low)


def store_packs(total, packs, n):
    for q, pack in enumerate(packs):
        for c in range(total.shape[1] // LANES):
            lanes = slice(c * LANES, (c + 1) * LANES)
            pack[c * n : (c + 1) * n, :] = total[q * n : (q + 1) * n, lanes]


def first_kernel(n, scores_ref, stats_ref, high_ref, low_ref, *refs):
    *packs, resp_ref, total, counts = refs
    comps, width = total.shape
    step = pl.program_id(0)

    @pl.when(step == 0)
    def _():
        total[...] = jnp.zeros_like(total)
        counts[...] = jnp.zeros_like(counts)

    peak, row_total = stats_ref[0, 0:1, :], stats_ref[0, 1:2, :]
    resp = jnp.exp(scores_ref[...] - peak) * (1.0 / row_total)
    resp_high, resp_low = split(resp)
    resp_ref[:comps, :] = resp_high
    resp_ref[comps:, :] = resp_low
    counts[...] += sum(resp[:, c : c + LANES] for c in range(0, resp.shape[1], LANES))
    total[...] += product(resp_ref[...], high_ref[...], low_ref[...], WITHIN)

    @pl.when(step == pl.num_programs(0) - 1)
    def _():
        store_packs(total, packs, n)
        column = jnp.sum(counts[...], axis=1, keepdims=True)
        for q, pack in enumerate(packs):
            row = to_row(column[q * n : (q + 1) * n], LANES)
            pack[width // LANES * n :, :] = jnp.broadcast_to(row, (8, LANES))


def first_moments(scores, stats, high, low, n):
    rows, width = high.shape
    comps = scores.shape[0]
    tile = min(256, rows // 2)
    steps = rows // 2 // tile
    planes = comps // n
    pack = (width // LANES * n + 8, LANES)
    row_block = pl.BlockSpec((tile, width), lambda i: (i, 0))
    return pl.pallas_call(
        functools.partial(first_kernel, n),
        grid=(2 * steps,),
        in_specs=[
            pl.BlockSpec((comps, tile), lambda i: (0, i)),
            pl.BlockSpec((1, 2, tile), lambda i: (i // steps, 0, i % steps)),
            row_block,
            row_block,
        ],
        out_specs=[whole(pack)] * planes + [pl.BlockSpec((2 * comps, tile), lambda i: (0, i))],
        out_shape=[jax.ShapeDtypeStruct(pack, F32)] * planes
        + [jax.ShapeDtypeStruct((2 * comps, rows), BF16)],
        scratch_shapes=[pltpu.VMEM((comps, width), F32), pltpu.VMEM((comps, LANES), F32)],
        compiler_params=params(24),
        cost_estimate=pl.CostEstimate(
            flops=6 * rows * width * comps,
            bytes_accessed=4 * rows * (width + 2 * comps),
            transcendentals=rows * comps,
        ),
        name="first_moments",
    )(scores, stats, high, low)


def second_kernel(n, resp_ref, high_ref, low_ref, *refs):
    *packs, total = refs
    step = pl.program_id(0)

    @pl.when(step == 0)
    def _():
        total[...] = jnp.zeros_like(total)

    total[...] += product(resp_ref[...], high_ref[...], low_ref[...], WITHIN)

    @pl.when(step == pl.num_programs(0) - 1)
    def _():
        store_packs(total, packs, n)


def second_moments(resp, high, low, n):
    rows, width = high.shape
    comps = resp.shape[0] // 2
    tile = min(256, rows // 2)
    planes = comps // n
    pack = (width // LANES * n, LANES)
    row_block = pl.BlockSpec((tile, width), lambda i: (i, 0))
    return pl.pallas_call(
        functools.partial(second_kernel, n),
        grid=(rows // tile,),
        in_specs=[pl.BlockSpec((2 * comps, tile), lambda i: (0, i)), row_block, row_block],
        out_specs=[whole(pack)] * planes,
        out_shape=[jax.ShapeDtypeStruct(pack, F32)] * planes,
        scratch_shapes=[pltpu.VMEM((comps, width), F32)],
        compiler_params=params(24),
        cost_estimate=pl.CostEstimate(
            flops=6 * rows * width * comps,
            bytes_accessed=4 * rows * (width + comps),
            transcendentals=0,
        ),
        name="second_moments",
    )(resp, high, low)


def update_kernel(scale, parts, means_ref, variances_ref, mass_ref, *refs):
    first, second = refs[:parts], refs[parts : 2 * parts]
    new_means_ref, new_variances_ref, new_mass_ref = refs[2 * parts :]
    n, width = means_ref.shape
    tiles = width // LANES * n
    row = sum(part[tiles : tiles + 1, :n] for part in first)
    new_row = 0.4 * mass_ref[...] + scale * row
    new_mass_ref[...] = new_row
    inverse = to_column(1.0 / new_row, n)
    kept = 0.4 * to_column(mass_ref[...], n)
    for c in range(width // LANES):
        lanes, tile = slice(c * LANES, (c + 1) * LANES), slice(c * n, (c + 1) * n)
        means, variances = means_ref[:, lanes], variances_ref[:, lanes]
        first_moment = kept * means + scale * sum(part[tile, :] for part in first)
        second_moment = kept * (variances + means * means) + scale * sum(
            part[tile, :] for part in second
        )
        new_means = first_moment * inverse
        new_means_ref[:, lanes] = new_means
        new_variances_ref[:, lanes] = second_moment * inverse - new_means * new_means


def update(scale, means, variances, mass, first, second):
    n, width = means.shape
    block = jax.ShapeDtypeStruct((n, width), F32)
    new_means, new_variances, new_mass = pl.pallas_call(
        functools.partial(update_kernel, scale, len(first)),
        out_shape=(block, block, jax.ShapeDtypeStruct((1, n), F32)),
        compiler_params=params(16),
        name="update",
    )(means, variances, mass.reshape(1, n), *first, *second)
    return new_means, new_variances, new_mass.reshape(n)


def swap(value, axis, bit):
    size = lax.axis_size(axis)
    return lax.ppermute(value, axis, [(i, i ^ bit) for i in range(size)])


def after(value, *others):
    return lax.optimization_barrier((value, *others))[0]


def gather_planes(piece):
    planes = lax.axis_size("dp") // 2
    held = {0: piece}
    bit = planes // 2
    while bit:
        held.update({q ^ bit: swap(value, "dp", 2 * bit) for q, value in held.items()})
        bit //= 2
    return [held[q] for q in range(planes)]


def scatter_planes(parts):
    planes = lax.axis_size("dp") // 2
    held = {q: [part] for q, part in enumerate(parts)}
    bit = 1
    while bit < planes:
        for q in sorted((q for q in held if q & bit), reverse=True):
            held[q ^ bit].append(swap(sum(held.pop(q)), "dp", 2 * bit))
        bit *= 2
    return held[0]


def merge(stats):
    peak = functools.reduce(jnp.maximum, [s[:, 0] for s in stats])
    total = sum(s[:, 1] * jnp.exp(s[:, 0] - peak) for s in stats)
    return jnp.stack([peak, total], axis=1)


def per_device(embeddings, comp_means, comp_variances, comp_mass):
    n = comp_means.shape[0]
    quad_pack, linear_pack = coefficients(comp_means, comp_variances, comp_mass)
    quad_packs = gather_planes(quad_pack)
    linear_packs = gather_planes(linear_pack)
    x_high, x_low, s_high, s_low = halves(embeddings, swap(embeddings, "dp", 1))
    (quad,) = score_call(quad_kernel, quad_packs, n, [], s_high, s_low, "quad_scores")
    scores, stats = score_call(
        linear_kernel, linear_packs, n, [quad], x_high, x_low, "linear_scores"
    )
    stats = merge([stats, swap(stats, "dp", 1)[::-1]])
    n_comp = lax.axis_size("comp")
    stats = merge([stats] + [swap(stats, "comp", q) for q in range(1, n_comp)])

    *first, resp = first_moments(scores, stats, x_high, x_low, n)
    second = second_moments(resp, s_high, s_low, n)
    first, second = scatter_planes(first), scatter_planes(second)

    total_comps = n * lax.axis_size("dp") * lax.axis_size("comp")
    total_rows = embeddings.shape[0] * lax.axis_size("dp")
    scale = 0.6 * (total_comps / total_rows)
    return update(scale, comp_means, comp_variances, comp_mass, first, second)


def solution(mesh):
    placed = (P("dp", None), P(("comp", "dp"), None), P(("comp", "dp"), None), P(("comp", "dp")))
    return jax.shard_map(
        per_device,
        mesh=mesh,
        in_specs=placed,
        out_specs=(P(("comp", "dp"), None), P(("comp", "dp"), None), P(("comp", "dp"))),
        check_vma=False,
    )
```

```python
import functools

import jax
import jax.numpy as jnp
from jax import lax
from jax.experimental import pallas as pl
from jax.experimental.pallas import tpu as pltpu
from jax.sharding import PartitionSpec as P

F32 = jnp.float32
BF16 = jnp.bfloat16
LANES = 128
ACROSS = (((1,), (1,)), ((), ()))
WITHIN = (((1,), (0,)), ((), ()))


def params(megabytes):
    return pltpu.CompilerParams(vmem_limit_bytes=megabytes * 1024 * 1024)


def split(value):
    high = value.astype(BF16)
    return high, (value - high.astype(F32)).astype(BF16)


def diagonal(rows, columns):
    shape = (rows, columns)
    return lax.broadcasted_iota(jnp.int32, shape, 0) == lax.broadcasted_iota(jnp.int32, shape, 1)


def to_row(column, lanes):
    return jnp.sum(jnp.where(diagonal(column.shape[0], lanes), column, 0.0), axis=0, keepdims=True)


def to_column(row, rows):
    return jnp.sum(jnp.where(diagonal(rows, row.shape[1]), row, 0.0), axis=1, keepdims=True)


def coefficient_kernel(
    means_hbm, variances_hbm, mass_hbm, quad_ref, linear_ref, means_ref, variances_ref, mass_ref, sems
):
    sources = (variances_hbm, means_hbm, mass_hbm)
    targets = (variances_ref, means_ref, mass_ref)
    copies = [pltpu.make_async_copy(s, t, sems.at[i]) for i, (s, t) in enumerate(zip(sources, targets))]
    for copy in copies:
        copy.start()
    for copy in copies:
        copy.wait()
    n, width = means_ref.shape
    means, variances = means_ref[...], variances_ref[...]
    precision = 1.0 / variances
    neg_half = -0.5 * precision
    mean_prec = means * precision
    sums = jnp.sum(jnp.log(variances) + means * mean_prec, axis=1, keepdims=True)
    offset = to_column(jnp.log(mass_ref[...]), n) - 0.5 * sums
    for c in range(width // LANES):
        lanes = slice(c * LANES, (c + 1) * LANES)
        quad_ref[c * n : (c + 1) * n, :] = neg_half[:, lanes]
        linear_ref[c * n : (c + 1) * n, :] = mean_prec[:, lanes]
    quad_ref[width // LANES * n :, :] = jnp.broadcast_to(to_row(offset, LANES), (8, LANES))


def coefficients(means, variances, mass):
    n, width = means.shape
    tiles = width // LANES * n
    return pl.pallas_call(
        coefficient_kernel,
        in_specs=[pl.BlockSpec(memory_space=pltpu.HBM)] * 3,
        out_shape=(
            jax.ShapeDtypeStruct((tiles + 8, LANES), F32),
            jax.ShapeDtypeStruct((tiles, LANES), F32),
        ),
        scratch_shapes=[
            pltpu.VMEM((n, width), F32),
            pltpu.VMEM((n, width), F32),
            pltpu.VMEM((1, n), F32),
            pltpu.SemaphoreType.DMA((3,)),
        ],
        compiler_params=params(48),
        name="coefficients",
    )(means, variances, mass.reshape(1, n))


def halves_kernel(own_ref, other_ref, xh_ref, xl_ref, sh_ref, sl_ref):
    def put(block):
        xh_ref[...], xl_ref[...] = split(block)
        sh_ref[...], sl_ref[...] = split(block * block)

    first = pl.program_id(0) < pl.num_programs(0) // 2

    @pl.when(first)
    def _():
        put(own_ref[...])

    @pl.when(jnp.logical_not(first))
    def _():
        put(other_ref[...])


def halves(own, other):
    rows, width = own.shape
    tile = min(256, rows)
    steps = rows // tile
    out = jax.ShapeDtypeStruct((2 * rows, width), BF16)
    return pl.pallas_call(
        halves_kernel,
        grid=(2 * steps,),
        in_specs=[
            pl.BlockSpec((tile, width), lambda i: (jnp.minimum(i, steps - 1), 0)),
            pl.BlockSpec((tile, width), lambda i: (jnp.maximum(i - steps, 0), 0)),
        ],
        out_specs=[pl.BlockSpec((tile, width), lambda i: (i, 0))] * 4,
        out_shape=[out] * 4,
        compiler_params=params(16),
        name="halves",
    )(own, other)


def load_packs(packs, weights, n):
    comps = n * len(packs)
    for q, pack in enumerate(packs):
        for c in range(weights.shape[1] // LANES):
            lanes = slice(c * LANES, (c + 1) * LANES)
            high, low = split(pack[c * n : (c + 1) * n, :])
            weights[q * n : (q + 1) * n, lanes] = high
            weights[comps + q * n : comps + (q + 1) * n, lanes] = low


def product(weights, high, low, dims):
    comps = weights.shape[0] // 2
    both = lax.dot_general(weights, high, dims, preferred_element_type=F32)
    rest = lax.dot_general(weights[:comps], low, dims, preferred_element_type=F32)
    return both[:comps] + (both[comps:] + rest)


def row_tiles(rows, tile=256):
    tile = min(tile, rows)
    return [slice(i, i + tile) for i in range(0, rows, tile)]


def load_offsets(packs, n, width):
    tiles = width // LANES * n
    return jnp.concatenate([to_column(pack[tiles : tiles + 1, :], n) for pack in packs])


def quad_kernel(n, *refs):
    *packs, high_ref, low_ref, out_ref, weights = refs
    load_packs(packs, weights, n)
    offset = load_offsets(packs, n, weights.shape[1])
    for tile in row_tiles(high_ref.shape[0]):
        scores = product(weights[...], high_ref[tile, :], low_ref[tile, :], ACROSS)
        out_ref[:, tile] = scores + offset


def stats_of(scores):
    peak = jnp.max(scores, axis=0, keepdims=True)
    return peak, jnp.sum(jnp.exp(scores - peak), axis=0, keepdims=True)


def joined(one, other):
    peak = jnp.maximum(one[0], other[0])
    return peak, one[1] * jnp.exp(one[0] - peak) + other[1] * jnp.exp(other[0] - peak)


def middle_kernel(n, early, *refs):
    linear, refs = refs[:early], refs[early:]
    *quad, xh_ref, xl_ref, sh_ref, sl_ref, quad_ref, out_ref, stats_ref, late_ref, weights, late = refs
    load_packs(linear, weights, n)
    load_packs(quad, late, n)
    offset = load_offsets(quad, n, late.shape[1])
    for tile in row_tiles(xh_ref.shape[0]):
        scores = quad_ref[:, tile] + product(weights[...], xh_ref[tile, :], xl_ref[tile, :], ACROSS)
        out_ref[:, tile] = scores
        stats_ref[0:1, tile], stats_ref[1:2, tile] = stats_of(scores)
        scores = product(late[...], sh_ref[tile, :], sl_ref[tile, :], ACROSS)
        late_ref[:, tile] = scores + offset


def last_kernel(n, *refs):
    *linear, xh_ref, xl_ref, quad_ref, early_ref, out_ref, stats_ref, weights = refs
    load_packs(linear, weights, n)
    half = stats_ref.shape[2]
    for tile in row_tiles(xh_ref.shape[0], min(256, half)):
        scores = quad_ref[:, tile] + product(weights[...], xh_ref[tile, :], xl_ref[tile, :], ACROSS)
        out_ref[:, tile] = scores
        early = early_ref[0:1, tile], early_ref[1:2, tile]
        block, part = tile.start // half, slice(tile.start % half, tile.start % half + tile.stop - tile.start)
        peak, total = joined(stats_of(scores), early)
        stats_ref[block, 0:1, part] = peak
        stats_ref[block, 1:2, part] = total


def score_call(body, out_shape, scratch, name, *operands):
    return pl.pallas_call(
        body,
        out_shape=[jax.ShapeDtypeStruct(shape, F32) for shape in out_shape],
        scratch_shapes=[pltpu.VMEM(shape, BF16) for shape in scratch],
        compiler_params=params(24),
        name=name,
    )(*operands)


def moment_tiles(resp_ref, high_ref, low_ref, packs, n):
    for c in range(0, high_ref.shape[1], 2 * LANES):
        columns = slice(c, c + 2 * LANES)
        total = product(resp_ref[...], high_ref[:, columns], low_ref[:, columns], WITHIN)
        for q, pack in enumerate(packs):
            for k in range(2):
                place = (c // LANES + k) * n
                pack[place : place + n, :] = total[q * n : (q + 1) * n, k * LANES : (k + 1) * LANES]


def first_kernel(n, planes, early_ref, late_ref, stats_ref, high_ref, low_ref, *refs):
    *packs, resp_ref = refs
    comps = resp_ref.shape[0] // 2
    half = stats_ref.shape[2]
    counts = jnp.zeros((comps, LANES), F32)
    for tile in row_tiles(high_ref.shape[0], min(256, half)):
        block, part = tile.start // half, slice(tile.start % half, tile.start % half + tile.stop - tile.start)
        peak, total = stats_ref[block, 0:1, part], stats_ref[block, 1:2, part]
        scores = jnp.concatenate([early_ref[:, tile], late_ref[:, tile]])
        resp = jnp.exp(scores - peak) * (1.0 / total)
        resp_ref[:comps, tile], resp_ref[comps:, tile] = split(resp)
        counts += sum(resp[:, c : c + LANES] for c in range(0, resp.shape[1], LANES))
    moment_tiles(resp_ref, high_ref, low_ref, packs, n)
    column = jnp.sum(counts, axis=1, keepdims=True)
    for q, pack in enumerate(packs):
        row = to_row(column[q * n : (q + 1) * n], LANES)
        pack[-8:, :] = jnp.broadcast_to(row, (8, LANES))


def first_moments(early, late, stats, high, low, n):
    rows, width = high.shape
    comps = early.shape[0] + late.shape[0]
    planes = comps // n
    pack = jax.ShapeDtypeStruct((width // LANES * n + 8, LANES), F32)
    return pl.pallas_call(
        functools.partial(first_kernel, n, planes),
        out_shape=[pack] * planes + [jax.ShapeDtypeStruct((2 * comps, rows), BF16)],
        compiler_params=params(24),
        name="first_moments",
    )(early, late, stats, high, low)


def second_kernel(n, resp_ref, high_ref, low_ref, *packs):
    moment_tiles(resp_ref, high_ref, low_ref, packs, n)


def second_moments(resp, high, low, n):
    width = high.shape[1]
    planes = resp.shape[0] // 2 // n
    pack = jax.ShapeDtypeStruct((width // LANES * n, LANES), F32)
    return pl.pallas_call(
        functools.partial(second_kernel, n),
        out_shape=[pack] * planes,
        compiler_params=params(24),
        name="second_moments",
    )(resp, high, low)


def update_kernel(scale, parts, means_ref, variances_ref, mass_ref, *refs):
    first, second = refs[:parts], refs[parts : 2 * parts]
    new_means_ref, new_variances_ref, new_mass_ref = refs[2 * parts :]
    n, width = means_ref.shape
    tiles = width // LANES * n
    row = sum(part[tiles : tiles + 1, :n] for part in first)
    new_row = 0.4 * mass_ref[...] + scale * row
    new_mass_ref[...] = new_row
    inverse = to_column(1.0 / new_row, n)
    kept = 0.4 * to_column(mass_ref[...], n)
    for c in range(width // LANES):
        lanes, tile = slice(c * LANES, (c + 1) * LANES), slice(c * n, (c + 1) * n)
        means, variances = means_ref[:, lanes], variances_ref[:, lanes]
        first_moment = kept * means + scale * sum(part[tile, :] for part in first)
        second_moment = kept * (variances + means * means) + scale * sum(
            part[tile, :] for part in second
        )
        new_means = first_moment * inverse
        new_means_ref[:, lanes] = new_means
        new_variances_ref[:, lanes] = second_moment * inverse - new_means * new_means


def update(scale, means, variances, mass, first, second):
    n, width = means.shape
    block = jax.ShapeDtypeStruct((n, width), F32)
    new_means, new_variances, new_mass = pl.pallas_call(
        functools.partial(update_kernel, scale, len(first)),
        out_shape=(block, block, jax.ShapeDtypeStruct((1, n), F32)),
        compiler_params=params(16),
        name="update",
    )(means, variances, mass.reshape(1, n), *first, *second)
    return new_means, new_variances, new_mass.reshape(n)


def swap(value, axis, bit):
    size = lax.axis_size(axis)
    return lax.ppermute(value, axis, [(i, i ^ bit) for i in range(size)])


def after(value, *others):
    return lax.optimization_barrier((value, *others))[0]


def gather_early(piece):
    bit = lax.axis_size("dp") // 4
    held = {0: piece}
    while bit > 1:
        held.update({q ^ bit: swap(value, "dp", 2 * bit) for q, value in held.items()})
        bit //= 2
    held[1] = swap(piece, "dp", 2)
    return held


def scatter_planes(first, second):
    planes = len(first)
    held = [{q: [part] for q, part in enumerate(parts)} for parts in (first, second)]
    bit = 1
    while bit < planes:
        arrived = []
        for parts in held:
            for q in sorted((q for q in parts if q & bit and q != bit), reverse=True):
                arrived.append(swap(after(sum(parts.pop(q)), *arrived[-1:]), "dp", 2 * bit))
                parts[q ^ bit].append(arrived[-1])
        for parts in held:
            direct = sum(parts.pop(bit))
            parts[0].append(swap(after(direct, *arrived[-1:]), "dp", 2 * bit))
        bit *= 2
    return held[0][0], held[1][0]


def merge(stats):
    peak = functools.reduce(jnp.maximum, [s[:, 0] for s in stats])
    total = sum(s[:, 1] * jnp.exp(s[:, 0] - peak) for s in stats)
    return jnp.stack([peak, total], axis=1)


def per_device(embeddings, comp_means, comp_variances, comp_mass):
    n = comp_means.shape[0]
    rows, width = embeddings.shape
    planes = lax.axis_size("dp") // 2
    comps = planes * n
    quad_pack, linear_pack = coefficients(comp_means, comp_variances, comp_mass)
    quad, linear = gather_early(quad_pack), gather_early(linear_pack)
    order = sorted(quad)
    late = [q for q in range(planes) if q not in quad]
    x_high, x_low, s_high, s_low = halves(embeddings, swap(embeddings, "dp", 1))
    for q in late:
        quad[q] = swap(after(quad[q ^ 1], x_high), "dp", 2)
    n_early, n_late = n * len(order), n * len(late)
    (early,) = score_call(
        functools.partial(quad_kernel, n),
        [(n_early, 2 * rows)],
        [(2 * n_early, width)],
        "quad_scores",
        *(quad[q] for q in order),
        s_high,
        s_low,
    )
    for q in late:
        linear[q] = swap(after(linear[q ^ 1], early), "dp", 2)
    early, early_stats, last = score_call(
        functools.partial(middle_kernel, n, len(order)),
        [(n_early, 2 * rows), (2, 2 * rows), (n_late, 2 * rows)],
        [(2 * n_early, width), (2 * n_late, width)],
        "middle_scores",
        *(linear[q] for q in order),
        *(quad[q] for q in late),
        x_high,
        x_low,
        s_high,
        s_low,
        early,
    )
    last, stats = score_call(
        functools.partial(last_kernel, n),
        [(n_late, 2 * rows), (2, 2, rows)],
        [(2 * n_late, width)],
        "last_scores",
        *(linear[q] for q in late),
        x_high,
        x_low,
        last,
        early_stats,
    )
    stats = merge([stats, swap(stats, "dp", 1)[::-1]])
    n_comp = lax.axis_size("comp")
    stats = merge([stats] + [swap(stats, "comp", q) for q in range(1, n_comp)])

    *first, resp = first_moments(early, last, stats, x_high, x_low, n)
    second = second_moments(resp, s_high, s_low, n)
    place = {q: i for i, q in enumerate(order + late)}
    first, second = ([parts[place[q]] for q in range(planes)] for parts in (first, second))
    first, second = scatter_planes(first, second)

    total_comps = n * lax.axis_size("dp") * lax.axis_size("comp")
    total_rows = embeddings.shape[0] * lax.axis_size("dp")
    scale = 0.6 * (total_comps / total_rows)
    return update(scale, comp_means, comp_variances, comp_mass, first, second)


def solution(mesh):
    placed = (P("dp", None), P(("comp", "dp"), None), P(("comp", "dp"), None), P(("comp", "dp")))
    return jax.shard_map(
        per_device,
        mesh=mesh,
        in_specs=placed,
        out_specs=(P(("comp", "dp"), None), P(("comp", "dp"), None), P(("comp", "dp"))),
        check_vma=False,
    )
```

```python
import functools

import jax
import jax.numpy as jnp
from jax import lax
from jax.experimental import pallas as pl
from jax.experimental.pallas import tpu as pltpu
from jax.sharding import PartitionSpec as P

F32 = jnp.float32
BF16 = jnp.bfloat16
LANES = 128
ACROSS = (((1,), (1,)), ((), ()))
WITHIN = (((1,), (0,)), ((), ()))


def params(megabytes):
    return pltpu.CompilerParams(vmem_limit_bytes=megabytes * 1024 * 1024)


def split(value):
    high = value.astype(BF16)
    return high, (value - high.astype(F32)).astype(BF16)


def diagonal(rows, columns):
    shape = (rows, columns)
    return lax.broadcasted_iota(jnp.int32, shape, 0) == lax.broadcasted_iota(jnp.int32, shape, 1)


def to_row(column, lanes):
    return jnp.sum(jnp.where(diagonal(column.shape[0], lanes), column, 0.0), axis=0, keepdims=True)


def to_column(row, rows):
    return jnp.sum(jnp.where(diagonal(rows, row.shape[1]), row, 0.0), axis=1, keepdims=True)


def coefficient_kernel(
    means_any, variances_any, mass_any, half_ref, pack_ref, means_ref, variances_ref, mass_ref, sems
):
    sources = (variances_any, means_any, mass_any)
    targets = (variances_ref, means_ref, mass_ref)
    copies = [pltpu.make_async_copy(s, t, sems.at[i]) for i, (s, t) in enumerate(zip(sources, targets))]
    for copy in copies:
        copy.start()
    for copy in copies:
        copy.wait()
    n, width = means_ref.shape
    means, variances = means_ref[...], variances_ref[...]
    precision = 1.0 / variances
    half_ref[...] = -0.5 * precision
    mean_prec = means * precision
    sums = jnp.sum(jnp.log(variances) + means * mean_prec, axis=1, keepdims=True)
    offset = to_column(jnp.log(mass_ref[...]), n) - 0.5 * sums
    for c in range(width // LANES):
        pack_ref[c * n : (c + 1) * n, :] = mean_prec[:, c * LANES : (c + 1) * LANES]
    pack_ref[width // LANES * n :, :] = jnp.broadcast_to(to_row(offset, LANES), (8, LANES))


def coefficients(means, variances, mass):
    n, width = means.shape
    return pl.pallas_call(
        coefficient_kernel,
        in_specs=[pl.BlockSpec(memory_space=pl.ANY)] * 3,
        out_shape=(
            jax.ShapeDtypeStruct((n, width), F32),
            jax.ShapeDtypeStruct((width // LANES * n + 8, LANES), F32),
        ),
        scratch_shapes=[
            pltpu.VMEM((n, width), F32),
            pltpu.VMEM((n, width), F32),
            pltpu.VMEM((1, n), F32),
            pltpu.SemaphoreType.DMA((3,)),
        ],
        compiler_params=params(60),
        name="coefficients",
    )(means, variances, mass.reshape(1, n))


def halves_kernel(own_ref, other_ref, xh_ref, xl_ref, sh_ref, sl_ref):
    def put(block):
        xh_ref[...], xl_ref[...] = split(block)
        sh_ref[...], sl_ref[...] = split(block * block)

    first = pl.program_id(0) < pl.num_programs(0) // 2

    @pl.when(first)
    def _():
        put(own_ref[...])

    @pl.when(jnp.logical_not(first))
    def _():
        put(other_ref[...])


def halves(own, other):
    rows, width = own.shape
    tile = min(256, rows)
    steps = rows // tile
    out = jax.ShapeDtypeStruct((2 * rows, width), BF16)
    return pl.pallas_call(
        halves_kernel,
        grid=(2 * steps,),
        in_specs=[
            pl.BlockSpec((tile, width), lambda i: (jnp.minimum(i, steps - 1), 0)),
            pl.BlockSpec((tile, width), lambda i: (jnp.maximum(i - steps, 0), 0)),
        ],
        out_specs=[pl.BlockSpec((tile, width), lambda i: (i, 0))] * 4,
        out_shape=[out] * 4,
        compiler_params=params(16),
        name="halves",
    )(own, other)


def load_packs(packs, weights, n):
    comps, tiles = n * len(packs), weights.shape[1] // LANES
    for q, pack in enumerate(packs):
        for c in range(tiles):
            lanes = slice(c * LANES, (c + 1) * LANES)
            high, low = split(pack[c * n : (c + 1) * n, :])
            weights[q * n : (q + 1) * n, lanes] = high
            weights[comps + q * n : comps + (q + 1) * n, lanes] = low
    return jnp.concatenate([to_column(pack[tiles * n : tiles * n + 1, :], n) for pack in packs])


def load_halves(halves, weights, n):
    comps = n * len(halves)
    for q, ref in enumerate(halves):
        high, low = split(ref[...])
        weights[q * n : (q + 1) * n, :] = high
        weights[comps + q * n : comps + (q + 1) * n, :] = low


def product(weights, high, low, dims):
    comps = weights.shape[0] // 2
    both = lax.dot_general(weights, high, dims, preferred_element_type=F32)
    rest = lax.dot_general(weights[:comps], low, dims, preferred_element_type=F32)
    return both[:comps] + (both[comps:] + rest)


def row_tiles(rows, tile=256):
    tile = min(tile, rows)
    return [slice(i, i + tile) for i in range(0, rows, tile)]


def quad_kernel(n, *refs):
    *neg_half, high_ref, low_ref, out_ref, weights = refs
    load_halves(neg_half, weights, n)
    for tile in row_tiles(high_ref.shape[0]):
        out_ref[:, tile] = product(weights[...], high_ref[tile, :], low_ref[tile, :], ACROSS)


def stats_of(scores):
    peak = jnp.max(scores, axis=0, keepdims=True)
    return peak, jnp.sum(jnp.exp(scores - peak), axis=0, keepdims=True)


def joined(one, other):
    peak = jnp.maximum(one[0], other[0])
    return peak, one[1] * jnp.exp(one[0] - peak) + other[1] * jnp.exp(other[0] - peak)


def early_kernel(n, *refs):
    *linear, high_ref, low_ref, quad_ref, out_ref, stats_ref, weights = refs
    offset = load_packs(linear, weights, n)
    comps = out_ref.shape[0]
    for tile in row_tiles(high_ref.shape[0]):
        scores = product(weights[...], high_ref[tile, :], low_ref[tile, :], ACROSS)
        scores = quad_ref[:comps, tile] + scores + offset
        out_ref[:, tile] = scores
        stats_ref[0:1, tile], stats_ref[1:2, tile] = stats_of(scores)


def half_tiles(half):
    for block in range(2):
        for part in row_tiles(half):
            yield slice(block * half + part.start, block * half + part.stop), block, part


def last_kernel(n, *refs):
    *linear, xh_ref, xl_ref, quad_ref, early_ref, out_ref, stats_ref, weights = refs
    offset = load_packs(linear, weights, n)
    skip = quad_ref.shape[0] - out_ref.shape[0]
    for tile, block, part in half_tiles(stats_ref.shape[2]):
        scores = product(weights[...], xh_ref[tile, :], xl_ref[tile, :], ACROSS)
        scores = quad_ref[skip:, tile] + scores + offset
        out_ref[:, tile] = scores
        early = early_ref[0:1, tile], early_ref[1:2, tile]
        peak, total = joined(stats_of(scores), early)
        stats_ref[block, 0:1, part] = peak
        stats_ref[block, 1:2, part] = total


def score_call(body, out_shape, scratch, name, *operands):
    return pl.pallas_call(
        body,
        out_shape=[jax.ShapeDtypeStruct(shape, F32) for shape in out_shape],
        scratch_shapes=[pltpu.VMEM(shape, BF16) for shape in scratch],
        compiler_params=params(24),
        name=name,
    )(*operands)


def moment_tiles(resp_ref, high_ref, low_ref, packs, n):
    for c in range(0, high_ref.shape[1], 2 * LANES):
        columns = slice(c, c + 2 * LANES)
        total = product(resp_ref[...], high_ref[:, columns], low_ref[:, columns], WITHIN)
        for q, pack in enumerate(packs):
            for k in range(2):
                place = (c // LANES + k) * n
                pack[place : place + n, :] = total[q * n : (q + 1) * n, k * LANES : (k + 1) * LANES]


def first_kernel(n, early_ref, late_ref, stats_ref, high_ref, low_ref, *refs):
    *packs, resp_ref = refs
    comps = resp_ref.shape[0] // 2
    counts = jnp.zeros((comps, LANES), F32)
    for tile, block, part in half_tiles(stats_ref.shape[2]):
        peak, total = stats_ref[block, 0:1, part], stats_ref[block, 1:2, part]
        scores = jnp.concatenate([early_ref[:, tile], late_ref[:, tile]])
        resp = jnp.exp(scores - peak) * (1.0 / total)
        resp_ref[:comps, tile], resp_ref[comps:, tile] = split(resp)
        counts += sum(resp[:, c : c + LANES] for c in range(0, resp.shape[1], LANES))
    moment_tiles(resp_ref, high_ref, low_ref, packs, n)
    column = jnp.sum(counts, axis=1, keepdims=True)
    for q, pack in enumerate(packs):
        row = to_row(column[q * n : (q + 1) * n], LANES)
        pack[-8:, :] = jnp.broadcast_to(row, (8, LANES))


def first_moments(early, late, stats, high, low, n):
    rows, width = high.shape
    comps = early.shape[0] + late.shape[0]
    planes = comps // n
    pack = jax.ShapeDtypeStruct((width // LANES * n + 8, LANES), F32)
    return pl.pallas_call(
        functools.partial(first_kernel, n),
        out_shape=[pack] * planes + [jax.ShapeDtypeStruct((2 * comps, rows), BF16)],
        compiler_params=params(24),
        name="first_moments",
    )(early, late, stats, high, low)


def second_kernel(n, resp_ref, high_ref, low_ref, *packs):
    moment_tiles(resp_ref, high_ref, low_ref, packs, n)


def second_moments(resp, high, low, n):
    width = high.shape[1]
    planes = resp.shape[0] // 2 // n
    pack = jax.ShapeDtypeStruct((width // LANES * n, LANES), F32)
    return pl.pallas_call(
        functools.partial(second_kernel, n),
        out_shape=[pack] * planes,
        compiler_params=params(24),
        name="second_moments",
    )(resp, high, low)


def tiles_of(n, width):
    return [(slice(c * LANES, (c + 1) * LANES), slice(c * n, (c + 1) * n)) for c in range(width // LANES)]


def means_kernel(scale, means_ref, variances_ref, mass_ref, *refs):
    *parts, new_means_ref, new_mass_ref, base_ref, factor_ref = refs
    n, width = means_ref.shape
    row = sum(part[-8:-7, :n] for part in parts)
    new_row = 0.4 * mass_ref[...] + scale * row
    new_mass_ref[...] = new_row
    new_mass = to_column(new_row, n)
    kept = 0.4 * to_column(mass_ref[...], n)
    factor_ref[...] = jnp.broadcast_to(scale / new_mass, factor_ref.shape)
    for lanes, tile in tiles_of(n, width):
        means = means_ref[:, lanes]
        moment = kept * means + scale * sum(part[tile, :] for part in parts)
        new_means = moment / new_mass
        new_means_ref[:, lanes] = new_means
        base_ref[:, lanes] = kept * (variances_ref[:, lanes] + means * means) / new_mass - new_means * new_means


def variances_kernel(base_ref, factor_ref, *refs):
    *parts, new_variances_ref = refs
    for lanes, tile in tiles_of(*base_ref.shape):
        new_variances_ref[:, lanes] = base_ref[:, lanes] + factor_ref[...] * sum(part[tile, :] for part in parts)


def update(scale, means, variances, mass, first, second):
    n = mass.shape[0]
    block = jax.ShapeDtypeStruct(means.shape, F32)
    new_means, new_mass, base, factor = pl.pallas_call(
        functools.partial(means_kernel, scale),
        out_shape=(
            block,
            jax.ShapeDtypeStruct((1, n), F32),
            block,
            jax.ShapeDtypeStruct((n, LANES), F32),
        ),
        compiler_params=params(16),
        name="update_means",
    )(means, variances, mass.reshape(1, n), *first)
    new_variances = pl.pallas_call(
        variances_kernel, out_shape=block, compiler_params=params(16), name="update_variances"
    )(base, factor, *second)
    return new_means, new_variances, new_mass.reshape(n)


def swap(value, axis, bit):
    size = lax.axis_size(axis)
    return lax.ppermute(value, axis, [(i, i ^ bit) for i in range(size)])


def after(value, *others):
    return lax.optimization_barrier((value, *others))[0]


def gather_early(piece):
    bit = lax.axis_size("dp") // 4
    held = {0: piece}
    while bit > 1:
        held.update({q ^ bit: swap(value, "dp", 2 * bit) for q, value in held.items()})
        bit //= 2
    held[1] = swap(piece, "dp", 2)
    return held


def scatter_planes(first, second):
    planes = len(first)
    held = [{q: [part] for q, part in enumerate(parts)} for parts in (first, second)]
    bit = 1
    while bit < planes:
        arrived = []
        for parts in held:
            for q in sorted((q for q in parts if q & bit and q != bit), reverse=True):
                arrived.append(swap(after(sum(parts.pop(q)), *arrived[-1:]), "dp", 2 * bit))
                parts[q ^ bit].append(arrived[-1])
        for parts, before in zip(held, (second[:1], arrived[-1:])):
            direct = sum(parts.pop(bit))
            parts[0].append(swap(after(direct, *before), "dp", 2 * bit))
        bit *= 2
    return held[0][0], held[1][0]


def merge(stats):
    peak = functools.reduce(jnp.maximum, [s[:, 0] for s in stats])
    total = sum(s[:, 1] * jnp.exp(s[:, 0] - peak) for s in stats)
    return jnp.stack([peak, total], axis=1)


def per_device(embeddings, comp_means, comp_variances, comp_mass):
    n = comp_means.shape[0]
    rows, width = embeddings.shape
    planes = lax.axis_size("dp") // 2
    neg_half, linear = coefficients(comp_means, comp_variances, comp_mass)
    neg_half, linear = gather_early(neg_half), gather_early(linear)
    other = swap(embeddings, "dp", 1)
    order = sorted(linear)
    late = [q for q in range(planes) if q not in linear]
    x_high, x_low, s_high, s_low = halves(embeddings, other)
    for q in late:
        neg_half[q] = swap(after(neg_half[q ^ 1], x_high), "dp", 2)
    n_early, n_late = n * len(order), n * len(late)
    (quad,) = score_call(
        functools.partial(quad_kernel, n),
        [(n * planes, 2 * rows)],
        [(2 * n * planes, width)],
        "quad_scores",
        *(neg_half[q] for q in order + late),
        after(s_high, linear[1]),
        s_low,
    )
    for q in late:
        linear[q] = swap(after(linear[q ^ 1], quad), "dp", 2)
    early, early_stats = score_call(
        functools.partial(early_kernel, n),
        [(n_early, 2 * rows), (2, 2 * rows)],
        [(2 * n_early, width)],
        "early_scores",
        *(linear[q] for q in order),
        x_high,
        x_low,
        quad,
    )
    last, stats = score_call(
        functools.partial(last_kernel, n),
        [(n_late, 2 * rows), (2, 2, rows)],
        [(2 * n_late, width)],
        "last_scores",
        *(linear[q] for q in late),
        x_high,
        x_low,
        quad,
        early_stats,
    )
    stats = merge([stats, swap(stats, "dp", 1)[::-1]])
    n_comp = lax.axis_size("comp")
    stats = merge([stats] + [swap(stats, "comp", q) for q in range(1, n_comp)])

    *first, resp = first_moments(early, last, stats, x_high, x_low, n)
    second = second_moments(resp, s_high, s_low, n)
    place = {q: i for i, q in enumerate(order + late)}
    first, second = ([parts[place[q]] for q in range(planes)] for parts in (first, second))
    first, second = scatter_planes(first, second)

    total_comps = n * lax.axis_size("dp") * lax.axis_size("comp")
    total_rows = embeddings.shape[0] * lax.axis_size("dp")
    scale = 0.6 * (total_comps / total_rows)
    return update(scale, comp_means, comp_variances, comp_mass, first, second)


def solution(mesh):
    placed = (P("dp", None), P(("comp", "dp"), None), P(("comp", "dp"), None), P(("comp", "dp")))
    return jax.shard_map(
        per_device,
        mesh=mesh,
        in_specs=placed,
        out_specs=(P(("comp", "dp"), None), P(("comp", "dp"), None), P(("comp", "dp"))),
        check_vma=False,
    )
```

```python
import functools

import jax
import jax.numpy as jnp
from jax import lax
from jax.experimental import pallas as pl
from jax.experimental.pallas import tpu as pltpu
from jax.sharding import PartitionSpec as P

F32 = jnp.float32
BF16 = jnp.bfloat16
LANES = 128
HEAVY = pl.CostEstimate(flops=10**11, bytes_accessed=1, transcendentals=0)
ACROSS = (((1,), (1,)), ((), ()))
WITHIN = (((1,), (0,)), ((), ()))


def params(megabytes):
    return pltpu.CompilerParams(vmem_limit_bytes=megabytes * 1024 * 1024)


def split(value):
    high = value.astype(BF16)
    return high, (value - high.astype(F32)).astype(BF16)


def diagonal(rows, columns):
    shape = (rows, columns)
    return lax.broadcasted_iota(jnp.int32, shape, 0) == lax.broadcasted_iota(jnp.int32, shape, 1)


def to_row(column, lanes):
    return jnp.sum(jnp.where(diagonal(column.shape[0], lanes), column, 0.0), axis=0, keepdims=True)


def to_column(row, rows):
    return jnp.sum(jnp.where(diagonal(rows, row.shape[1]), row, 0.0), axis=1, keepdims=True)


def coefficient_kernel(
    means_any, variances_any, mass_any, half_ref, pack_ref, means_ref, variances_ref, mass_ref, sems
):
    sources = (variances_any, means_any, mass_any)
    targets = (variances_ref, means_ref, mass_ref)
    copies = [pltpu.make_async_copy(s, t, sems.at[i]) for i, (s, t) in enumerate(zip(sources, targets))]
    for copy in copies:
        copy.start()
    for copy in copies:
        copy.wait()
    n, width = means_ref.shape
    means, variances = means_ref[...], variances_ref[...]
    precision = 1.0 / variances
    half_ref[...] = -0.5 * precision
    mean_prec = means * precision
    sums = jnp.sum(jnp.log(variances) + means * mean_prec, axis=1, keepdims=True)
    offset = to_column(jnp.log(mass_ref[...]), n) - 0.5 * sums
    for c in range(width // LANES):
        pack_ref[c * n : (c + 1) * n, :] = mean_prec[:, c * LANES : (c + 1) * LANES]
    pack_ref[width // LANES * n :, :] = jnp.broadcast_to(to_row(offset, LANES), (8, LANES))


def coefficients(means, variances, mass):
    n, width = means.shape
    return pl.pallas_call(
        coefficient_kernel,
        in_specs=[pl.BlockSpec(memory_space=pl.ANY)] * 3,
        out_shape=(
            jax.ShapeDtypeStruct((n, width), F32),
            jax.ShapeDtypeStruct((width // LANES * n + 8, LANES), F32),
        ),
        scratch_shapes=[
            pltpu.VMEM((n, width), F32),
            pltpu.VMEM((n, width), F32),
            pltpu.VMEM((1, n), F32),
            pltpu.SemaphoreType.DMA((3,)),
        ],
        cost_estimate=HEAVY,
        compiler_params=params(60),
        name="coefficients",
    )(means, variances, mass.reshape(1, n))


def halves_kernel(own_ref, other_ref, xh_ref, xl_ref, sh_ref, sl_ref):
    def put(block):
        xh_ref[...], xl_ref[...] = split(block)
        sh_ref[...], sl_ref[...] = split(block * block)

    first = pl.program_id(0) < pl.num_programs(0) // 2

    @pl.when(first)
    def _():
        put(own_ref[...])

    @pl.when(jnp.logical_not(first))
    def _():
        put(other_ref[...])


def halves(own, other):
    rows, width = own.shape
    tile = min(256, rows)
    steps = rows // tile
    out = jax.ShapeDtypeStruct((2 * rows, width), BF16)
    return pl.pallas_call(
        halves_kernel,
        grid=(2 * steps,),
        in_specs=[
            pl.BlockSpec((tile, width), lambda i: (jnp.minimum(i, steps - 1), 0)),
            pl.BlockSpec((tile, width), lambda i: (jnp.maximum(i - steps, 0), 0)),
        ],
        out_specs=[pl.BlockSpec((tile, width), lambda i: (i, 0))] * 4,
        out_shape=[out] * 4,
        cost_estimate=HEAVY,
        compiler_params=params(16),
        name="halves",
    )(own, other)


def load_packs(packs, weights, n):
    comps, tiles = n * len(packs), weights.shape[1] // LANES
    for q, pack in enumerate(packs):
        for c in range(tiles):
            lanes = slice(c * LANES, (c + 1) * LANES)
            high, low = split(pack[c * n : (c + 1) * n, :])
            weights[q * n : (q + 1) * n, lanes] = high
            weights[comps + q * n : comps + (q + 1) * n, lanes] = low
    return jnp.concatenate([to_column(pack[tiles * n : tiles * n + 1, :], n) for pack in packs])


def load_halves(halves, weights, n):
    comps = n * len(halves)
    for q, ref in enumerate(halves):
        high, low = split(ref[...])
        weights[q * n : (q + 1) * n, :] = high
        weights[comps + q * n : comps + (q + 1) * n, :] = low


def product(weights, high, low, dims):
    comps = weights.shape[0] // 2
    both = lax.dot_general(weights, high, dims, preferred_element_type=F32)
    rest = lax.dot_general(weights[:comps], low, dims, preferred_element_type=F32)
    return both[:comps] + (both[comps:] + rest)


def row_tiles(rows, tile=256):
    tile = min(tile, rows)
    return [slice(i, i + tile) for i in range(0, rows, tile)]


def quad_kernel(n, *refs):
    *neg_half, high_ref, low_ref, out_ref, weights = refs
    load_halves(neg_half, weights, n)
    for tile in row_tiles(high_ref.shape[0]):
        out_ref[:, tile] = product(weights[...], high_ref[tile, :], low_ref[tile, :], ACROSS)


def stats_of(scores):
    peak = jnp.max(scores, axis=0, keepdims=True)
    return peak, jnp.sum(jnp.exp(scores - peak), axis=0, keepdims=True)


def joined(one, other):
    peak = jnp.maximum(one[0], other[0])
    return peak, one[1] * jnp.exp(one[0] - peak) + other[1] * jnp.exp(other[0] - peak)


def middle_kernel(n, early, *refs):
    linear, refs = refs[:early], refs[early:]
    *neg_half, xh_ref, xl_ref, sh_ref, sl_ref, quad_ref, out_ref, stats_ref, late_ref, weights, late = refs
    offset = load_packs(linear, weights, n)
    load_halves(neg_half, late, n)
    for tile in row_tiles(xh_ref.shape[0]):
        scores = product(weights[...], xh_ref[tile, :], xl_ref[tile, :], ACROSS)
        scores = quad_ref[:, tile] + scores + offset
        out_ref[:, tile] = scores
        stats_ref[0:1, tile], stats_ref[1:2, tile] = stats_of(scores)
        late_ref[:, tile] = product(late[...], sh_ref[tile, :], sl_ref[tile, :], ACROSS)


def half_tiles(half):
    for block in range(2):
        for part in row_tiles(half):
            yield slice(block * half + part.start, block * half + part.stop), block, part


def last_kernel(n, *refs):
    *linear, xh_ref, xl_ref, quad_ref, early_ref, out_ref, stats_ref, weights = refs
    offset = load_packs(linear, weights, n)
    for tile, block, part in half_tiles(stats_ref.shape[2]):
        scores = product(weights[...], xh_ref[tile, :], xl_ref[tile, :], ACROSS)
        scores = quad_ref[:, tile] + scores + offset
        out_ref[:, tile] = scores
        early = early_ref[0:1, tile], early_ref[1:2, tile]
        peak, total = joined(stats_of(scores), early)
        stats_ref[block, 0:1, part] = peak
        stats_ref[block, 1:2, part] = total


def score_call(body, out_shape, scratch, name, *operands):
    return pl.pallas_call(
        body,
        out_shape=[jax.ShapeDtypeStruct(shape, F32) for shape in out_shape],
        scratch_shapes=[pltpu.VMEM(shape, BF16) for shape in scratch],
        cost_estimate=HEAVY,
        compiler_params=params(24),
        name=name,
    )(*operands)


def moment_tiles(resp_ref, high_ref, low_ref, packs, n):
    for c in range(0, high_ref.shape[1], 2 * LANES):
        columns = slice(c, c + 2 * LANES)
        total = product(resp_ref[...], high_ref[:, columns], low_ref[:, columns], WITHIN)
        for q, pack in enumerate(packs):
            for k in range(2):
                place = (c // LANES + k) * n
                pack[place : place + n, :] = total[q * n : (q + 1) * n, k * LANES : (k + 1) * LANES]


def first_kernel(n, early_ref, late_ref, stats_ref, high_ref, low_ref, *refs):
    *packs, resp_ref = refs
    comps = resp_ref.shape[0] // 2
    counts = jnp.zeros((comps, LANES), F32)
    for tile, block, part in half_tiles(stats_ref.shape[2]):
        peak, total = stats_ref[block, 0:1, part], stats_ref[block, 1:2, part]
        scores = jnp.concatenate([early_ref[:, tile], late_ref[:, tile]])
        resp = jnp.exp(scores - peak) * (1.0 / total)
        resp_ref[:comps, tile], resp_ref[comps:, tile] = split(resp)
        counts += sum(resp[:, c : c + LANES] for c in range(0, resp.shape[1], LANES))
    moment_tiles(resp_ref, high_ref, low_ref, packs, n)
    column = jnp.sum(counts, axis=1, keepdims=True)
    for q, pack in enumerate(packs):
        row = to_row(column[q * n : (q + 1) * n], LANES)
        pack[-8:, :] = jnp.broadcast_to(row, (8, LANES))


def first_moments(early, late, stats, high, low, n):
    rows, width = high.shape
    comps = early.shape[0] + late.shape[0]
    planes = comps // n
    pack = jax.ShapeDtypeStruct((width // LANES * n + 8, LANES), F32)
    return pl.pallas_call(
        functools.partial(first_kernel, n),
        out_shape=[pack] * planes + [jax.ShapeDtypeStruct((2 * comps, rows), BF16)],
        cost_estimate=HEAVY,
        compiler_params=params(24),
        name="first_moments",
    )(early, late, stats, high, low)


def second_kernel(n, resp_ref, high_ref, low_ref, *packs):
    moment_tiles(resp_ref, high_ref, low_ref, packs, n)


def second_moments(resp, high, low, n):
    width = high.shape[1]
    planes = resp.shape[0] // 2 // n
    pack = jax.ShapeDtypeStruct((width // LANES * n, LANES), F32)
    return pl.pallas_call(
        functools.partial(second_kernel, n),
        out_shape=[pack] * planes,
        cost_estimate=HEAVY,
        compiler_params=params(24),
        name="second_moments",
    )(resp, high, low)


def tiles_of(n, width):
    return [(slice(c * LANES, (c + 1) * LANES), slice(c * n, (c + 1) * n)) for c in range(width // LANES)]


def means_kernel(scale, means_ref, variances_ref, mass_ref, *refs):
    *parts, new_means_ref, new_mass_ref, base_ref, factor_ref = refs
    n, width = means_ref.shape
    row = sum(part[-8:-7, :n] for part in parts)
    new_row = 0.4 * mass_ref[...] + scale * row
    new_mass_ref[...] = new_row
    new_mass = to_column(new_row, n)
    kept = 0.4 * to_column(mass_ref[...], n)
    factor_ref[...] = jnp.broadcast_to(scale / new_mass, factor_ref.shape)
    for lanes, tile in tiles_of(n, width):
        means = means_ref[:, lanes]
        moment = kept * means + scale * sum(part[tile, :] for part in parts)
        new_means = moment / new_mass
        new_means_ref[:, lanes] = new_means
        base_ref[:, lanes] = kept * (variances_ref[:, lanes] + means * means) / new_mass - new_means * new_means


def variances_kernel(base_ref, factor_ref, *refs):
    *parts, new_variances_ref = refs
    for lanes, tile in tiles_of(*base_ref.shape):
        new_variances_ref[:, lanes] = base_ref[:, lanes] + factor_ref[...] * sum(part[tile, :] for part in parts)


def update(scale, means, variances, mass, first, second):
    n = mass.shape[0]
    block = jax.ShapeDtypeStruct(means.shape, F32)
    new_means, new_mass, base, factor = pl.pallas_call(
        functools.partial(means_kernel, scale),
        out_shape=(
            block,
            jax.ShapeDtypeStruct((1, n), F32),
            block,
            jax.ShapeDtypeStruct((n, LANES), F32),
        ),
        cost_estimate=HEAVY,
        compiler_params=params(16),
        name="update_means",
    )(means, variances, mass.reshape(1, n), *first)
    new_variances = pl.pallas_call(
        variances_kernel, out_shape=block, compiler_params=params(16), name="update_variances"
    )(base, factor, *second)
    return new_means, new_variances, new_mass.reshape(n)


def swap(value, axis, bit):
    size = lax.axis_size(axis)
    return lax.ppermute(value, axis, [(i, i ^ bit) for i in range(size)])


def after(value, *others):
    return lax.optimization_barrier((value, *others))[0]


def gather_early(piece):
    bit = lax.axis_size("dp") // 4
    held = {0: piece}
    while bit > 1:
        held.update({q ^ bit: swap(value, "dp", 2 * bit) for q, value in held.items()})
        bit //= 2
    held[1] = swap(piece, "dp", 2)
    return held


def scatter_planes(first, second):
    planes = len(first)
    held = [dict(enumerate(parts)) for parts in (first, second)]
    direct, last = [[], []], []
    bit = 1
    while bit < planes:
        arrived = []
        for parts in held:
            for q in sorted((q for q in parts if q & bit and q != bit), reverse=True):
                arrived.append(swap(after(parts.pop(q), *arrived[-1:]), "dp", 2 * bit))
                parts[q ^ bit] = parts[q ^ bit] + arrived[-1]
        for got, parts in zip(direct, held):
            got.append(swap(after(parts.pop(bit), *arrived[-1:]), "dp", 2 * bit))
        bit *= 2
    totals = [sum(got[1:], parts[0]) for got, parts in zip(direct, held)]
    totals = lax.optimization_barrier(tuple(totals))
    return [[total, *got[:1]] for total, got in zip(totals, direct)]


def merge(stats):
    peak = functools.reduce(jnp.maximum, [s[:, 0] for s in stats])
    total = sum(s[:, 1] * jnp.exp(s[:, 0] - peak) for s in stats)
    return jnp.stack([peak, total], axis=1)


def per_device(embeddings, comp_means, comp_variances, comp_mass):
    n = comp_means.shape[0]
    rows, width = embeddings.shape
    planes = lax.axis_size("dp") // 2
    neg_half, linear = coefficients(comp_means, comp_variances, comp_mass)
    neg_half, linear = gather_early(neg_half), gather_early(linear)
    other = swap(embeddings, "dp", 1)
    order = sorted(linear)
    late = [q for q in range(planes) if q not in linear]
    x_high, x_low, s_high, s_low = halves(embeddings, other)
    for q in late:
        neg_half[q] = swap(after(neg_half[q ^ 1], x_high), "dp", 2)
    n_early, n_late = n * len(order), n * len(late)
    (early,) = score_call(
        functools.partial(quad_kernel, n),
        [(n_early, 2 * rows)],
        [(2 * n_early, width)],
        "quad_scores",
        *(neg_half[q] for q in order),
        s_high,
        s_low,
    )
    for q in late:
        linear[q] = swap(after(linear[q ^ 1], early, linear[1]), "dp", 2)
    early, early_stats, last = score_call(
        functools.partial(middle_kernel, n, len(order)),
        [(n_early, 2 * rows), (2, 2 * rows), (n_late, 2 * rows)],
        [(2 * n_early, width), (2 * n_late, width)],
        "middle_scores",
        *(linear[q] for q in order),
        *(neg_half[q] for q in late),
        x_high,
        x_low,
        s_high,
        s_low,
        early,
    )
    last, stats = score_call(
        functools.partial(last_kernel, n),
        [(n_late, 2 * rows), (2, 2, rows)],
        [(2 * n_late, width)],
        "last_scores",
        *(linear[q] for q in late),
        x_high,
        x_low,
        last,
        early_stats,
    )
    stats = merge([stats, swap(stats, "dp", 1)[::-1]])
    n_comp = lax.axis_size("comp")
    stats = merge([stats] + [swap(stats, "comp", q) for q in range(1, n_comp)])

    *first, resp = first_moments(early, last, stats, x_high, x_low, n)
    second = second_moments(resp, s_high, s_low, n)
    place = {q: i for i, q in enumerate(order + late)}
    first, second = ([parts[place[q]] for q in range(planes)] for parts in (first, second))
    first, second = scatter_planes(first, second)

    total_comps = n * lax.axis_size("dp") * lax.axis_size("comp")
    total_rows = embeddings.shape[0] * lax.axis_size("dp")
    scale = 0.6 * (total_comps / total_rows)
    return update(scale, comp_means, comp_variances, comp_mass, first, second)


def solution(mesh):
    placed = (P("dp", None), P(("comp", "dp"), None), P(("comp", "dp"), None), P(("comp", "dp")))
    return jax.shard_map(
        per_device,
        mesh=mesh,
        in_specs=placed,
        out_specs=(P(("comp", "dp"), None), P(("comp", "dp"), None), P(("comp", "dp"))),
        check_vma=False,
    )
```

```python
import functools

import jax
import jax.numpy as jnp
from jax import lax
from jax.experimental import pallas as pl
from jax.experimental.pallas import tpu as pltpu
from jax.sharding import PartitionSpec as P

F32 = jnp.float32
BF16 = jnp.bfloat16
LANES = 128
HEAVY = pl.CostEstimate(flops=10**11, bytes_accessed=1, transcendentals=0)
ACROSS = (((1,), (1,)), ((), ()))
WITHIN = (((1,), (0,)), ((), ()))


def params(megabytes):
    return pltpu.CompilerParams(vmem_limit_bytes=megabytes * 1024 * 1024)


def split(value):
    high = value.astype(BF16)
    return high, (value - high.astype(F32)).astype(BF16)


def diagonal(rows, columns):
    shape = (rows, columns)
    return lax.broadcasted_iota(jnp.int32, shape, 0) == lax.broadcasted_iota(jnp.int32, shape, 1)


def to_row(column, lanes):
    return jnp.sum(jnp.where(diagonal(column.shape[0], lanes), column, 0.0), axis=0, keepdims=True)


def to_column(row, rows):
    return jnp.sum(jnp.where(diagonal(rows, row.shape[1]), row, 0.0), axis=1, keepdims=True)


def coefficient_kernel(means_ref, variances_ref, mass_ref, pack_ref):
    n, width = means_ref.shape
    means, variances = means_ref[...], variances_ref[...]
    mean_prec = means * (1.0 / variances)
    sums = jnp.sum(jnp.log(variances) + means * mean_prec, axis=1, keepdims=True)
    offset = to_column(jnp.log(mass_ref[...]), n) - 0.5 * sums
    for c in range(width // LANES):
        pack_ref[c * n : (c + 1) * n, :] = mean_prec[:, c * LANES : (c + 1) * LANES]
    pack_ref[width // LANES * n :, :] = jnp.broadcast_to(to_row(offset, LANES), (8, LANES))


def coefficients(means, variances, mass):
    n, width = means.shape
    return pl.pallas_call(
        coefficient_kernel,
        out_shape=jax.ShapeDtypeStruct((width // LANES * n + 8, LANES), F32),
        cost_estimate=HEAVY,
        compiler_params=params(16),
        name="coefficients",
    )(means, variances, mass.reshape(1, n))


def halves_kernel(own_ref, other_ref, xh_ref, xl_ref, sh_ref, sl_ref):
    def put(block):
        xh_ref[...], xl_ref[...] = split(block)
        sh_ref[...], sl_ref[...] = split(block * block)

    first = pl.program_id(0) < pl.num_programs(0) // 2

    @pl.when(first)
    def _():
        put(own_ref[...])

    @pl.when(jnp.logical_not(first))
    def _():
        put(other_ref[...])


def halves(own, other):
    rows, width = own.shape
    tile = min(256, rows)
    steps = rows // tile
    out = jax.ShapeDtypeStruct((2 * rows, width), BF16)
    return pl.pallas_call(
        halves_kernel,
        grid=(2 * steps,),
        in_specs=[
            pl.BlockSpec((tile, width), lambda i: (jnp.minimum(i, steps - 1), 0)),
            pl.BlockSpec((tile, width), lambda i: (jnp.maximum(i - steps, 0), 0)),
        ],
        out_specs=[pl.BlockSpec((tile, width), lambda i: (i, 0))] * 4,
        out_shape=[out] * 4,
        cost_estimate=HEAVY,
        compiler_params=params(16),
        name="halves",
    )(own, other)


def load_packs(packs, weights, n):
    comps, tiles = n * len(packs), weights.shape[1] // LANES
    for q, pack in enumerate(packs):
        for c in range(tiles):
            lanes = slice(c * LANES, (c + 1) * LANES)
            high, low = split(pack[c * n : (c + 1) * n, :])
            weights[q * n : (q + 1) * n, lanes] = high
            weights[comps + q * n : comps + (q + 1) * n, lanes] = low
    return jnp.concatenate([to_column(pack[tiles * n : tiles * n + 1, :], n) for pack in packs])


def load_variances(variances, weights, n):
    comps = n * len(variances)
    for q, ref in enumerate(variances):
        high, low = split(-0.5 * (1.0 / ref[...]))
        weights[q * n : (q + 1) * n, :] = high
        weights[comps + q * n : comps + (q + 1) * n, :] = low


def product(weights, high, low, dims):
    comps = weights.shape[0] // 2
    both = lax.dot_general(weights, high, dims, preferred_element_type=F32)
    rest = lax.dot_general(weights[:comps], low, dims, preferred_element_type=F32)
    return both[:comps] + (both[comps:] + rest)


def row_tiles(rows, tile=256):
    tile = min(tile, rows)
    return [slice(i, i + tile) for i in range(0, rows, tile)]


def quad_kernel(n, *refs):
    *variances, high_ref, low_ref, out_ref, weights = refs
    load_variances(variances, weights, n)
    for tile in row_tiles(high_ref.shape[0]):
        out_ref[:, tile] = product(weights[...], high_ref[tile, :], low_ref[tile, :], ACROSS)


def stats_of(scores):
    peak = jnp.max(scores, axis=0, keepdims=True)
    return peak, jnp.sum(jnp.exp(scores - peak), axis=0, keepdims=True)


def joined(one, other):
    peak = jnp.maximum(one[0], other[0])
    return peak, one[1] * jnp.exp(one[0] - peak) + other[1] * jnp.exp(other[0] - peak)


def early_kernel(n, *refs):
    *linear, high_ref, low_ref, quad_ref, out_ref, stats_ref, weights = refs
    offset = load_packs(linear, weights, n)
    for tile in row_tiles(high_ref.shape[0]):
        scores = product(weights[...], high_ref[tile, :], low_ref[tile, :], ACROSS)
        scores = quad_ref[:, tile] + scores + offset
        out_ref[:, tile] = scores
        stats_ref[0:1, tile], stats_ref[1:2, tile] = stats_of(scores)


def half_tiles(half):
    for block in range(2):
        for part in row_tiles(half):
            yield slice(block * half + part.start, block * half + part.stop), block, part


def last_kernel(n, *refs):
    *linear, xh_ref, xl_ref, quad_ref, early_ref, out_ref, stats_ref, weights = refs
    offset = load_packs(linear, weights, n)
    for tile, block, part in half_tiles(stats_ref.shape[2]):
        scores = product(weights[...], xh_ref[tile, :], xl_ref[tile, :], ACROSS)
        scores = quad_ref[:, tile] + scores + offset
        out_ref[:, tile] = scores
        early = early_ref[0:1, tile], early_ref[1:2, tile]
        peak, total = joined(stats_of(scores), early)
        stats_ref[block, 0:1, part] = peak
        stats_ref[block, 1:2, part] = total


def score_call(body, out_shape, scratch, name, *operands):
    return pl.pallas_call(
        body,
        out_shape=[jax.ShapeDtypeStruct(shape, F32) for shape in out_shape],
        scratch_shapes=[pltpu.VMEM(shape, BF16) for shape in scratch],
        cost_estimate=HEAVY,
        compiler_params=params(24),
        name=name,
    )(*operands)


def moment_tiles(resp_ref, high_ref, low_ref, packs, n):
    for c in range(0, high_ref.shape[1], 2 * LANES):
        columns = slice(c, c + 2 * LANES)
        total = product(resp_ref[...], high_ref[:, columns], low_ref[:, columns], WITHIN)
        for q, pack in enumerate(packs):
            for k in range(2):
                place = (c // LANES + k) * n
                pack[place : place + n, :] = total[q * n : (q + 1) * n, k * LANES : (k + 1) * LANES]


def first_kernel(n, early_ref, late_ref, stats_ref, high_ref, low_ref, *refs):
    *packs, resp_ref = refs
    comps = resp_ref.shape[0] // 2
    counts = jnp.zeros((comps, LANES), F32)
    for tile, block, part in half_tiles(stats_ref.shape[2]):
        peak, total = stats_ref[block, 0:1, part], stats_ref[block, 1:2, part]
        scores = jnp.concatenate([early_ref[:, tile], late_ref[:, tile]])
        resp = jnp.exp(scores - peak) * (1.0 / total)
        resp_ref[:comps, tile], resp_ref[comps:, tile] = split(resp)
        counts += sum(resp[:, c : c + LANES] for c in range(0, resp.shape[1], LANES))
    moment_tiles(resp_ref, high_ref, low_ref, packs, n)
    column = jnp.sum(counts, axis=1, keepdims=True)
    for q, pack in enumerate(packs):
        row = to_row(column[q * n : (q + 1) * n], LANES)
        pack[-8:, :] = jnp.broadcast_to(row, (8, LANES))


def first_moments(early, late, stats, high, low, n):
    rows, width = high.shape
    comps = early.shape[0] + late.shape[0]
    pack = jax.ShapeDtypeStruct((width // LANES * n + 8, LANES), F32)
    return pl.pallas_call(
        functools.partial(first_kernel, n),
        out_shape=[pack] * (comps // n) + [jax.ShapeDtypeStruct((2 * comps, rows), BF16)],
        cost_estimate=HEAVY,
        compiler_params=params(24),
        name="first_moments",
    )(early, late, stats, high, low)


def second_kernel(n, resp_ref, high_ref, low_ref, *packs):
    moment_tiles(resp_ref, high_ref, low_ref, packs, n)


def second_moments(resp, high, low, n):
    pack = jax.ShapeDtypeStruct((high.shape[1] // LANES * n, LANES), F32)
    return pl.pallas_call(
        functools.partial(second_kernel, n),
        out_shape=[pack] * (resp.shape[0] // 2 // n),
        cost_estimate=HEAVY,
        compiler_params=params(24),
        name="second_moments",
    )(resp, high, low)


def update_kernel(
    scale,
    means_ref,
    variances_ref,
    mass_ref,
    first_ref,
    second_ref,
    near_first_ref,
    near_second_ref,
    new_means_ref,
    new_variances_ref,
    new_mass_ref,
):
    n, width = means_ref.shape
    tiles = width // LANES * n
    row = first_ref[tiles : tiles + 1, :n] + near_first_ref[tiles : tiles + 1, :n]
    new_row = 0.4 * mass_ref[...] + scale * row
    new_mass_ref[...] = new_row
    inverse = 1.0 / to_column(new_row, n)
    kept = 0.4 * to_column(mass_ref[...], n)
    for c in range(width // LANES):
        lanes, tile = slice(c * LANES, (c + 1) * LANES), slice(c * n, (c + 1) * n)
        means, variances = means_ref[:, lanes], variances_ref[:, lanes]
        first = first_ref[tile, :] + near_first_ref[tile, :]
        second = second_ref[tile, :] + near_second_ref[tile, :]
        new_means = (kept * means + scale * first) * inverse
        new_means_ref[:, lanes] = new_means
        second_moment = kept * (variances + means * means) + scale * second
        new_variances_ref[:, lanes] = second_moment * inverse - new_means * new_means


def update(scale, means, variances, mass, *sums):
    n = mass.shape[0]
    block = jax.ShapeDtypeStruct(means.shape, F32)
    new_means, new_variances, new_mass = pl.pallas_call(
        functools.partial(update_kernel, scale),
        out_shape=(block, block, jax.ShapeDtypeStruct((1, n), F32)),
        cost_estimate=HEAVY,
        compiler_params=params(16),
        name="update",
    )(means, variances, mass.reshape(1, n), *sums)
    return new_means, new_variances, new_mass.reshape(n)


def swap(value, axis, bit):
    size = lax.axis_size(axis)
    return lax.ppermute(value, axis, [(i, i ^ bit) for i in range(size)])


def after(value, *others):
    return lax.optimization_barrier((value, *others))[0]


def gather_early(piece):
    bit = lax.axis_size("dp") // 4
    held = {0: piece}
    while bit > 1:
        held.update({q ^ bit: swap(value, "dp", 2 * bit) for q, value in held.items()})
        bit //= 2
    held[1] = swap(piece, "dp", 2)
    return held


def scatter_planes(first, second):
    held = [dict(enumerate(parts)) for parts in (first, second)]
    totals, near = [[parts.pop(0)] for parts in held], []
    planes, bit = len(first), 1
    while bit < planes:
        ready = []
        for parts in held:
            for q in sorted((q for q in parts if q & bit and q != bit), reverse=True):
                parts[q ^ bit] = parts[q ^ bit] + swap(after(parts.pop(q), *ready), "dp", 2 * bit)
                ready = [parts[q ^ bit]]
        for total, parts in zip(totals, held):
            part = swap(after(parts.pop(bit), *ready), "dp", 2 * bit)
            (near if bit == 1 else total).append(part)
        bit *= 2
    return *lax.optimization_barrier(tuple(sum(t[1:], t[0]) for t in totals)), *near


def merge(one, other):
    peak, total = joined((one[:, 0], one[:, 1]), (other[:, 0], other[:, 1]))
    return jnp.stack([peak, total], axis=1)


def per_device(embeddings, comp_means, comp_variances, comp_mass):
    n = comp_means.shape[0]
    rows, width = embeddings.shape
    planes = lax.axis_size("dp") // 2
    variances = gather_early(comp_variances)
    linear = gather_early(coefficients(comp_means, comp_variances, comp_mass))
    other = swap(embeddings, "dp", 1)
    order = sorted(linear)
    late = [q for q in range(planes) if q not in linear]
    x_high, x_low, s_high, s_low = halves(embeddings, other)
    for q in late:
        variances[q] = swap(after(variances[q ^ 1], x_high), "dp", 2)
    n_early, n_late = n * len(order), n * len(late)

    def quad_scores(group, name):
        comps = n * len(group)
        operands = (*(variances[q] for q in group), s_high, s_low)
        body = functools.partial(quad_kernel, n)
        return score_call(body, [(comps, 2 * rows)], [(2 * comps, width)], name, *operands)[0]

    quad = quad_scores(order, "early_quad")
    for q in late:
        linear[q] = swap(after(linear[q ^ 1], quad, linear[1]), "dp", 2)
    early, early_stats = score_call(
        functools.partial(early_kernel, n),
        [(n_early, 2 * rows), (2, 2 * rows)],
        [(2 * n_early, width)],
        "early_scores",
        *(linear[q] for q in order),
        x_high,
        x_low,
        quad,
    )
    last, stats = score_call(
        functools.partial(last_kernel, n),
        [(n_late, 2 * rows), (2, 2, rows)],
        [(2 * n_late, width)],
        "last_scores",
        *(linear[q] for q in late),
        x_high,
        x_low,
        quad_scores(late, "late_quad"),
        early_stats,
    )
    stats = merge(stats, swap(stats, "dp", 1)[::-1])
    bit = 1
    while bit < lax.axis_size("comp"):
        stats = merge(stats, swap(stats, "comp", bit))
        bit *= 2

    *first, resp = first_moments(early, last, stats, x_high, x_low, n)
    second = second_moments(resp, s_high, s_low, n)
    place = {q: i for i, q in enumerate(order + late)}
    first, second = ([parts[place[q]] for q in range(planes)] for parts in (first, second))
    sums = scatter_planes(first, second)

    total_comps = n * lax.axis_size("dp") * lax.axis_size("comp")
    total_rows = embeddings.shape[0] * lax.axis_size("dp")
    scale = 0.6 * (total_comps / total_rows)
    return update(scale, comp_means, comp_variances, comp_mass, *sums)


def solution(mesh):
    placed = (P("dp", None), P(("comp", "dp"), None), P(("comp", "dp"), None), P(("comp", "dp")))
    return jax.shard_map(
        per_device,
        mesh=mesh,
        in_specs=placed,
        out_specs=(P(("comp", "dp"), None), P(("comp", "dp"), None), P(("comp", "dp"))),
        check_vma=False,
    )
```

```python
import functools

import jax
import jax.numpy as jnp
from jax import lax
from jax.experimental import pallas as pl
from jax.experimental.pallas import tpu as pltpu
from jax.sharding import PartitionSpec as P

F32 = jnp.float32
BF16 = jnp.bfloat16
LANES = 128
HEAVY = pl.CostEstimate(flops=10**11, bytes_accessed=1, transcendentals=0)
ACROSS = (((1,), (1,)), ((), ()))
WITHIN = (((1,), (0,)), ((), ()))


def params(megabytes):
    return pltpu.CompilerParams(vmem_limit_bytes=megabytes * 1024 * 1024)


def split(value):
    high = value.astype(BF16)
    return high, (value - high.astype(F32)).astype(BF16)


def diagonal(rows, columns):
    shape = (rows, columns)
    return lax.broadcasted_iota(jnp.int32, shape, 0) == lax.broadcasted_iota(jnp.int32, shape, 1)


def to_row(column, lanes):
    return jnp.sum(jnp.where(diagonal(column.shape[0], lanes), column, 0.0), axis=0, keepdims=True)


def to_column(row, rows):
    return jnp.sum(jnp.where(diagonal(rows, row.shape[1]), row, 0.0), axis=1, keepdims=True)


def coefficient_kernel(means_ref, variances_ref, mass_ref, pack_ref):
    n, width = means_ref.shape
    means, variances = means_ref[...], variances_ref[...]
    mean_prec = means * (1.0 / variances)
    sums = jnp.sum(jnp.log(variances) + means * mean_prec, axis=1, keepdims=True)
    offset = to_column(jnp.log(mass_ref[...]), n) - 0.5 * sums
    for c in range(width // LANES):
        pack_ref[c * n : (c + 1) * n, :] = mean_prec[:, c * LANES : (c + 1) * LANES]
    pack_ref[width // LANES * n :, :] = jnp.broadcast_to(to_row(offset, LANES), (8, LANES))


def coefficients(means, variances, mass):
    n, width = means.shape
    return pl.pallas_call(
        coefficient_kernel,
        out_shape=jax.ShapeDtypeStruct((width // LANES * n + 8, LANES), F32),
        cost_estimate=HEAVY,
        compiler_params=params(16),
        name="coefficients",
    )(means, variances, mass.reshape(1, n))


def halves_kernel(own_ref, other_ref, xh_ref, xl_ref, sh_ref, sl_ref):
    def put(block):
        xh_ref[...], xl_ref[...] = split(block)
        sh_ref[...], sl_ref[...] = split(block * block)

    first = pl.program_id(0) < pl.num_programs(0) // 2

    @pl.when(first)
    def _():
        put(own_ref[...])

    @pl.when(jnp.logical_not(first))
    def _():
        put(other_ref[...])


def halves(own, other):
    rows, width = own.shape
    tile = min(256, rows)
    steps = rows // tile
    out = jax.ShapeDtypeStruct((2 * rows, width), BF16)
    return pl.pallas_call(
        halves_kernel,
        grid=(2 * steps,),
        in_specs=[
            pl.BlockSpec((tile, width), lambda i: (jnp.minimum(i, steps - 1), 0)),
            pl.BlockSpec((tile, width), lambda i: (jnp.maximum(i - steps, 0), 0)),
        ],
        out_specs=[pl.BlockSpec((tile, width), lambda i: (i, 0))] * 4,
        out_shape=[out] * 4,
        cost_estimate=HEAVY,
        compiler_params=params(16),
        name="halves",
    )(own, other)


def load_packs(packs, weights, n):
    comps, tiles = n * len(packs), weights.shape[1] // LANES
    for q, pack in enumerate(packs):
        for c in range(tiles):
            lanes = slice(c * LANES, (c + 1) * LANES)
            high, low = split(pack[c * n : (c + 1) * n, :])
            weights[q * n : (q + 1) * n, lanes] = high
            weights[comps + q * n : comps + (q + 1) * n, lanes] = low
    return jnp.concatenate([to_column(pack[tiles * n : tiles * n + 1, :], n) for pack in packs])


def load_variances(variances, weights, n):
    comps = n * len(variances)
    for q, ref in enumerate(variances):
        high, low = split(-0.5 * (1.0 / ref[...]))
        weights[q * n : (q + 1) * n, :] = high
        weights[comps + q * n : comps + (q + 1) * n, :] = low


def product(weights, high, low, dims):
    comps = weights.shape[0] // 2
    both = lax.dot_general(weights, high, dims, preferred_element_type=F32)
    rest = lax.dot_general(weights[:comps], low, dims, preferred_element_type=F32)
    return both[:comps] + (both[comps:] + rest)


def over_rows(rows, body, tile=256, together=2):
    tile = min(tile, rows)
    together = min(together, rows // tile)
    step = tile * together

    def several(i, carry):
        for k in range(together):
            body(pl.ds(pl.multiple_of(i * step + k * tile, tile), tile))
        return carry

    lax.fori_loop(0, rows // step, several, 0)


def quad_kernel(n, *refs):
    *variances, high_ref, low_ref, out_ref, weights = refs
    load_variances(variances, weights, n)

    def rows(tile):
        out_ref[:, tile] = product(weights[...], high_ref[tile, :], low_ref[tile, :], ACROSS)

    over_rows(high_ref.shape[0], rows)


def stats_of(scores):
    peak = jnp.max(scores, axis=0, keepdims=True)
    return peak, jnp.sum(jnp.exp(scores - peak), axis=0, keepdims=True)


def joined(one, other):
    peak = jnp.maximum(one[0], other[0])
    return peak, one[1] * jnp.exp(one[0] - peak) + other[1] * jnp.exp(other[0] - peak)


def early_kernel(n, *refs):
    *linear, high_ref, low_ref, quad_ref, out_ref, stats_ref, weights = refs
    offset = load_packs(linear, weights, n)

    def rows(tile):
        scores = product(weights[...], high_ref[tile, :], low_ref[tile, :], ACROSS)
        scores = quad_ref[:, tile] + scores + offset
        out_ref[:, tile] = scores
        stats_ref[0:1, tile], stats_ref[1:2, tile] = stats_of(scores)

    over_rows(high_ref.shape[0], rows)


def last_kernel(n, *refs):
    *linear, high_ref, low_ref, quad_ref, early_ref, out_ref, stats_ref, weights = refs
    offset = load_packs(linear, weights, n)

    def rows(tile):
        scores = product(weights[...], high_ref[tile, :], low_ref[tile, :], ACROSS)
        scores = quad_ref[:, tile] + scores + offset
        out_ref[:, tile] = scores
        early = early_ref[0:1, tile], early_ref[1:2, tile]
        stats_ref[0:1, tile], stats_ref[1:2, tile] = joined(stats_of(scores), early)

    over_rows(high_ref.shape[0], rows)


def score_call(body, out_shape, scratch, name, *operands):
    return pl.pallas_call(
        body,
        out_shape=[jax.ShapeDtypeStruct(shape, F32) for shape in out_shape],
        scratch_shapes=[pltpu.VMEM(shape, BF16) for shape in scratch],
        cost_estimate=HEAVY,
        compiler_params=params(24),
        name=name,
    )(*operands)


def moment_tiles(resp_ref, high_ref, low_ref, packs, n):
    for c in range(0, high_ref.shape[1], 2 * LANES):
        columns = slice(c, c + 2 * LANES)
        total = product(resp_ref[...], high_ref[:, columns], low_ref[:, columns], WITHIN)
        for q, pack in enumerate(packs):
            for k in range(2):
                place = (c // LANES + k) * n
                pack[place : place + n, :] = total[q * n : (q + 1) * n, k * LANES : (k + 1) * LANES]


def first_kernel(n, early_ref, late_ref, stats_ref, high_ref, low_ref, *refs):
    *packs, resp_ref = refs
    comps = resp_ref.shape[0] // 2
    counts = jnp.zeros((comps, LANES), F32)
    for start in range(0, high_ref.shape[0], 256):
        tile = slice(start, start + 256)
        peak, total = stats_ref[0:1, tile], stats_ref[1:2, tile]
        scores = jnp.concatenate([early_ref[:, tile], late_ref[:, tile]])
        resp = jnp.exp(scores - peak) * (1.0 / total)
        resp_ref[:comps, tile], resp_ref[comps:, tile] = split(resp)
        counts += sum(resp[:, c : c + LANES] for c in range(0, resp.shape[1], LANES))
    moment_tiles(resp_ref, high_ref, low_ref, packs, n)
    column = jnp.sum(counts, axis=1, keepdims=True)
    for q, pack in enumerate(packs):
        row = to_row(column[q * n : (q + 1) * n], LANES)
        pack[-8:, :] = jnp.broadcast_to(row, (8, LANES))


def first_moments(early, late, stats, high, low, n):
    rows, width = high.shape
    comps = early.shape[0] + late.shape[0]
    pack = jax.ShapeDtypeStruct((width // LANES * n + 8, LANES), F32)
    return pl.pallas_call(
        functools.partial(first_kernel, n),
        out_shape=[pack] * (comps // n) + [jax.ShapeDtypeStruct((2 * comps, rows), BF16)],
        cost_estimate=HEAVY,
        compiler_params=params(24),
        name="first_moments",
    )(early, late, stats, high, low)


def second_kernel(n, resp_ref, high_ref, low_ref, *packs):
    moment_tiles(resp_ref, high_ref, low_ref, packs, n)


def second_moments(resp, high, low, n):
    pack = jax.ShapeDtypeStruct((high.shape[1] // LANES * n, LANES), F32)
    return pl.pallas_call(
        functools.partial(second_kernel, n),
        out_shape=[pack] * (resp.shape[0] // 2 // n),
        cost_estimate=HEAVY,
        compiler_params=params(24),
        name="second_moments",
    )(resp, high, low)


def update_kernel(
    scale,
    means_ref,
    variances_ref,
    mass_ref,
    first_ref,
    second_ref,
    near_first_ref,
    near_second_ref,
    new_means_ref,
    new_variances_ref,
    new_mass_ref,
):
    n, width = means_ref.shape
    tiles = width // LANES * n
    row = first_ref[tiles : tiles + 1, :n] + near_first_ref[tiles : tiles + 1, :n]
    new_row = 0.4 * mass_ref[...] + scale * row
    new_mass_ref[...] = new_row
    inverse = 1.0 / to_column(new_row, n)
    kept = 0.4 * to_column(mass_ref[...], n)
    for c in range(width // LANES):
        lanes, tile = slice(c * LANES, (c + 1) * LANES), slice(c * n, (c + 1) * n)
        means, variances = means_ref[:, lanes], variances_ref[:, lanes]
        first = first_ref[tile, :] + near_first_ref[tile, :]
        second = second_ref[tile, :] + near_second_ref[tile, :]
        new_means = (kept * means + scale * first) * inverse
        new_means_ref[:, lanes] = new_means
        second_moment = kept * (variances + means * means) + scale * second
        new_variances_ref[:, lanes] = second_moment * inverse - new_means * new_means


def update(scale, means, variances, mass, *sums):
    n = mass.shape[0]
    block = jax.ShapeDtypeStruct(means.shape, F32)
    new_means, new_variances, new_mass = pl.pallas_call(
        functools.partial(update_kernel, scale),
        out_shape=(block, block, jax.ShapeDtypeStruct((1, n), F32)),
        cost_estimate=HEAVY,
        compiler_params=params(16),
        name="update",
    )(means, variances, mass.reshape(1, n), *sums)
    return new_means, new_variances, new_mass.reshape(n)


def swap(value, axis, bit):
    size = lax.axis_size(axis)
    return lax.ppermute(value, axis, [(i, i ^ bit) for i in range(size)])


def after(value, *others):
    return lax.optimization_barrier((value, *others))[0]


def gather_early(piece):
    bit = lax.axis_size("dp") // 4
    held = {0: piece}
    while bit > 1:
        held.update({q ^ bit: swap(value, "dp", 2 * bit) for q, value in held.items()})
        bit //= 2
    held[1] = swap(piece, "dp", 2)
    return held


def scatter_planes(first, second):
    held = [dict(enumerate(parts)) for parts in (first, second)]
    totals, near = [[parts.pop(0)] for parts in held], []
    planes, bit = len(first), 1
    while bit < planes:
        ready = []
        for parts in held:
            for q in sorted((q for q in parts if q & bit and q != bit), reverse=True):
                parts[q ^ bit] = parts[q ^ bit] + swap(after(parts.pop(q), *ready), "dp", 2 * bit)
                ready = [parts[q ^ bit]]
        for total, parts in zip(totals, held):
            part = swap(after(parts.pop(bit), *ready), "dp", 2 * bit)
            (near if bit == 1 else total).append(part)
        bit *= 2
    return *lax.optimization_barrier(tuple(sum(t[1:], t[0]) for t in totals)), *near


def merge(stats):
    peak = functools.reduce(jnp.maximum, [s[0] for s in stats])
    return jnp.stack([peak, sum(s[1] * jnp.exp(s[0] - peak) for s in stats)])


def per_device(embeddings, comp_means, comp_variances, comp_mass):
    n = comp_means.shape[0]
    rows, width = embeddings.shape
    planes = lax.axis_size("dp") // 2
    variances = gather_early(comp_variances)
    linear = gather_early(coefficients(comp_means, comp_variances, comp_mass))
    other = swap(embeddings, "dp", 1)
    order = sorted(linear)
    late = [q for q in range(planes) if q not in linear]
    x_high, x_low, s_high, s_low = halves(embeddings, other)
    for q in late:
        variances[q] = swap(after(variances[q ^ 1], x_high), "dp", 2)
    n_early, n_late = n * len(order), n * len(late)

    def quad_scores(group, name):
        comps = n * len(group)
        operands = (*(variances[q] for q in group), s_high, s_low)
        body = functools.partial(quad_kernel, n)
        return score_call(body, [(comps, 2 * rows)], [(2 * comps, width)], name, *operands)[0]

    quad = quad_scores(order, "early_quad")
    for q in late:
        linear[q] = swap(after(linear[q ^ 1], quad, linear[1]), "dp", 2)
    early, early_stats = score_call(
        functools.partial(early_kernel, n),
        [(n_early, 2 * rows), (2, 2 * rows)],
        [(2 * n_early, width)],
        "early_scores",
        *(linear[q] for q in order),
        x_high,
        x_low,
        quad,
    )
    last, stats = score_call(
        functools.partial(last_kernel, n),
        [(n_late, 2 * rows), (2, 2 * rows)],
        [(2 * n_late, width)],
        "last_scores",
        *(linear[q] for q in late),
        x_high,
        x_low,
        quad_scores(late, "late_quad"),
        early_stats,
    )
    other = swap(stats, "dp", 1)
    stats = merge([stats, jnp.concatenate([other[:, rows:], other[:, :rows]], axis=1)])
    n_comp = lax.axis_size("comp")
    copies = jnp.broadcast_to(stats, (n_comp, *stats.shape))
    stats = merge(list(lax.all_to_all(copies, "comp", 0, 0)))

    *first, resp = first_moments(early, last, stats, x_high, x_low, n)
    second = second_moments(resp, s_high, s_low, n)
    place = {q: i for i, q in enumerate(order + late)}
    first, second = ([parts[place[q]] for q in range(planes)] for parts in (first, second))
    sums = scatter_planes(first, second)

    total_comps = n * lax.axis_size("dp") * lax.axis_size("comp")
    total_rows = embeddings.shape[0] * lax.axis_size("dp")
    scale = 0.6 * (total_comps / total_rows)
    return update(scale, comp_means, comp_variances, comp_mass, *sums)


def solution(mesh):
    placed = (P("dp", None), P(("comp", "dp"), None), P(("comp", "dp"), None), P(("comp", "dp")))
    return jax.shard_map(
        per_device,
        mesh=mesh,
        in_specs=placed,
        out_specs=(P(("comp", "dp"), None), P(("comp", "dp"), None), P(("comp", "dp"))),
        check_vma=False,
    )
```

```python
import functools

import jax
import jax.numpy as jnp
from jax import lax
from jax.experimental import pallas as pl
from jax.experimental.pallas import tpu as pltpu
from jax.sharding import PartitionSpec as P

F32 = jnp.float32
BF16 = jnp.bfloat16
LANES = 128
HEAVY = pl.CostEstimate(flops=10**10, bytes_accessed=10**8, transcendentals=0)
ACROSS = (((1,), (1,)), ((), ()))
WITHIN = (((1,), (0,)), ((), ()))


def params(megabytes):
    return pltpu.CompilerParams(vmem_limit_bytes=megabytes * 1024 * 1024)


def split(value):
    high = value.astype(BF16)
    return high, (value - high.astype(F32)).astype(BF16)


def diagonal(rows, columns):
    shape = (rows, columns)
    return lax.broadcasted_iota(jnp.int32, shape, 0) == lax.broadcasted_iota(jnp.int32, shape, 1)


def to_row(column, lanes):
    return jnp.sum(jnp.where(diagonal(column.shape[0], lanes), column, 0.0), axis=0, keepdims=True)


def to_column(row, rows):
    return jnp.sum(jnp.where(diagonal(rows, row.shape[1]), row, 0.0), axis=1, keepdims=True)


def coefficient_kernel(means_ref, variances_ref, mass_ref, pack_ref):
    n, width = means_ref.shape
    means, variances = means_ref[...], variances_ref[...]
    mean_prec = means * (1.0 / variances)
    sums = jnp.sum(jnp.log(variances) + means * mean_prec, axis=1, keepdims=True)
    offset = to_column(jnp.log(mass_ref[...]), n) - 0.5 * sums
    for c in range(width // LANES):
        pack_ref[c * n : (c + 1) * n, :] = mean_prec[:, c * LANES : (c + 1) * LANES]
    pack_ref[width // LANES * n :, :] = jnp.broadcast_to(to_row(offset, LANES), (8, LANES))


def coefficients(means, variances, mass):
    n, width = means.shape
    return pl.pallas_call(
        coefficient_kernel,
        out_shape=jax.ShapeDtypeStruct((width // LANES * n + 8, LANES), F32),
        cost_estimate=HEAVY,
        compiler_params=params(16),
        name="coefficients",
    )(means, variances, mass.reshape(1, n))


def halves_kernel(own_ref, other_ref, xh_ref, xl_ref, sh_ref, sl_ref):
    def put(block):
        xh_ref[...], xl_ref[...] = split(block)
        sh_ref[...], sl_ref[...] = split(block * block)

    first = pl.program_id(0) < pl.num_programs(0) // 2

    @pl.when(first)
    def _():
        put(own_ref[...])

    @pl.when(jnp.logical_not(first))
    def _():
        put(other_ref[...])


def halves(own, other):
    rows, width = own.shape
    tile = min(256, rows)
    steps = rows // tile
    out = jax.ShapeDtypeStruct((2 * rows, width), BF16)
    return pl.pallas_call(
        halves_kernel,
        grid=(2 * steps,),
        in_specs=[
            pl.BlockSpec((tile, width), lambda i: (jnp.minimum(i, steps - 1), 0)),
            pl.BlockSpec((tile, width), lambda i: (jnp.maximum(i - steps, 0), 0)),
        ],
        out_specs=[pl.BlockSpec((tile, width), lambda i: (i, 0))] * 4,
        out_shape=[out] * 4,
        cost_estimate=HEAVY,
        compiler_params=params(16),
        name="halves",
    )(own, other)


def load_packs(packs, weights, n):
    comps, tiles = n * len(packs), weights.shape[1] // LANES
    for q, pack in enumerate(packs):
        for c in range(tiles):
            lanes = slice(c * LANES, (c + 1) * LANES)
            high, low = split(pack[c * n : (c + 1) * n, :])
            weights[q * n : (q + 1) * n, lanes] = high
            weights[comps + q * n : comps + (q + 1) * n, lanes] = low
    return jnp.concatenate([to_column(pack[tiles * n : tiles * n + 1, :], n) for pack in packs])


def load_variances(variances, weights, n):
    comps = n * len(variances)
    for q, ref in enumerate(variances):
        high, low = split(-0.5 * (1.0 / ref[...]))
        weights[q * n : (q + 1) * n, :] = high
        weights[comps + q * n : comps + (q + 1) * n, :] = low


def product(weights, high, low, dims):
    comps = weights.shape[0] // 2
    both = lax.dot_general(weights, high, dims, preferred_element_type=F32)
    rest = lax.dot_general(weights[:comps], low, dims, preferred_element_type=F32)
    return both[:comps] + (both[comps:] + rest)


def row_tiles(rows, tile=256):
    tile = min(tile, rows)
    return [slice(i, i + tile) for i in range(0, rows, tile)]


def quad_kernel(n, *refs):
    *variances, high_ref, low_ref, out_ref, weights = refs
    load_variances(variances, weights, n)
    for tile in row_tiles(high_ref.shape[0]):
        out_ref[:, tile] = product(weights[...], high_ref[tile, :], low_ref[tile, :], ACROSS)


def stats_of(scores):
    peak = jnp.max(scores, axis=0, keepdims=True)
    return peak, jnp.sum(jnp.exp(scores - peak), axis=0, keepdims=True)


def joined(one, other):
    peak = jnp.maximum(one[0], other[0])
    return peak, one[1] * jnp.exp(one[0] - peak) + other[1] * jnp.exp(other[0] - peak)


def early_kernel(n, *refs):
    *linear, high_ref, low_ref, quad_ref, out_ref, stats_ref, weights = refs
    offset = load_packs(linear, weights, n)
    for tile in row_tiles(high_ref.shape[0]):
        scores = product(weights[...], high_ref[tile, :], low_ref[tile, :], ACROSS)
        scores = quad_ref[:, tile] + scores + offset
        out_ref[:, tile] = scores
        stats_ref[0:1, tile], stats_ref[1:2, tile] = stats_of(scores)


def half_tiles(half):
    for block in range(2):
        for part in row_tiles(half):
            yield slice(block * half + part.start, block * half + part.stop), block, part


def last_kernel(n, *refs):
    *linear, xh_ref, xl_ref, quad_ref, early_ref, out_ref, stats_ref, weights = refs
    offset = load_packs(linear, weights, n)
    for tile, block, part in half_tiles(stats_ref.shape[2]):
        scores = product(weights[...], xh_ref[tile, :], xl_ref[tile, :], ACROSS)
        scores = quad_ref[:, tile] + scores + offset
        out_ref[:, tile] = scores
        early = early_ref[0:1, tile], early_ref[1:2, tile]
        peak, total = joined(stats_of(scores), early)
        stats_ref[block, 0:1, part] = peak
        stats_ref[block, 1:2, part] = total


def score_call(body, out_shape, scratch, name, *operands):
    return pl.pallas_call(
        body,
        out_shape=[jax.ShapeDtypeStruct(shape, F32) for shape in out_shape],
        scratch_shapes=[pltpu.VMEM(shape, BF16) for shape in scratch],
        cost_estimate=HEAVY,
        compiler_params=params(24),
        name=name,
    )(*operands)


def moment_tiles(resp_ref, high_ref, low_ref, packs, n):
    for c in range(0, high_ref.shape[1], 2 * LANES):
        columns = slice(c, c + 2 * LANES)
        total = product(resp_ref[...], high_ref[:, columns], low_ref[:, columns], WITHIN)
        for q, pack in enumerate(packs):
            for k in range(2):
                place = (c // LANES + k) * n
                pack[place : place + n, :] = total[q * n : (q + 1) * n, k * LANES : (k + 1) * LANES]


def first_kernel(n, early_ref, late_ref, stats_ref, high_ref, low_ref, *refs):
    *packs, resp_ref = refs
    comps = resp_ref.shape[0] // 2
    counts = jnp.zeros((comps, LANES), F32)
    for tile, block, part in half_tiles(stats_ref.shape[2]):
        peak, total = stats_ref[block, 0:1, part], stats_ref[block, 1:2, part]
        scores = jnp.concatenate([early_ref[:, tile], late_ref[:, tile]])
        resp = jnp.exp(scores - peak) * (1.0 / total)
        resp_ref[:comps, tile], resp_ref[comps:, tile] = split(resp)
        counts += sum(resp[:, c : c + LANES] for c in range(0, resp.shape[1], LANES))
    moment_tiles(resp_ref, high_ref, low_ref, packs, n)
    column = jnp.sum(counts, axis=1, keepdims=True)
    for q, pack in enumerate(packs):
        row = to_row(column[q * n : (q + 1) * n], LANES)
        pack[-8:, :] = jnp.broadcast_to(row, (8, LANES))


def first_moments(early, late, stats, high, low, n):
    rows, width = high.shape
    comps = early.shape[0] + late.shape[0]
    pack = jax.ShapeDtypeStruct((width // LANES * n + 8, LANES), F32)
    return pl.pallas_call(
        functools.partial(first_kernel, n),
        out_shape=[pack] * (comps // n) + [jax.ShapeDtypeStruct((2 * comps, rows), BF16)],
        cost_estimate=HEAVY,
        compiler_params=params(24),
        name="first_moments",
    )(early, late, stats, high, low)


def second_kernel(n, resp_ref, high_ref, low_ref, *packs):
    moment_tiles(resp_ref, high_ref, low_ref, packs, n)


def second_moments(resp, high, low, n):
    pack = jax.ShapeDtypeStruct((high.shape[1] // LANES * n, LANES), F32)
    return pl.pallas_call(
        functools.partial(second_kernel, n),
        out_shape=[pack] * (resp.shape[0] // 2 // n),
        cost_estimate=HEAVY,
        compiler_params=params(24),
        name="second_moments",
    )(resp, high, low)


def update_kernel(
    scale,
    means_ref,
    variances_ref,
    mass_ref,
    first_ref,
    second_ref,
    near_first_ref,
    near_second_ref,
    new_means_ref,
    new_variances_ref,
    new_mass_ref,
):
    n, width = means_ref.shape
    tiles = width // LANES * n
    row = first_ref[tiles : tiles + 1, :n] + near_first_ref[tiles : tiles + 1, :n]
    new_row = 0.4 * mass_ref[...] + scale * row
    new_mass_ref[...] = new_row
    inverse = 1.0 / to_column(new_row, n)
    kept = 0.4 * to_column(mass_ref[...], n)
    for c in range(width // LANES):
        lanes, tile = slice(c * LANES, (c + 1) * LANES), slice(c * n, (c + 1) * n)
        means, variances = means_ref[:, lanes], variances_ref[:, lanes]
        first = first_ref[tile, :] + near_first_ref[tile, :]
        second = second_ref[tile, :] + near_second_ref[tile, :]
        new_means = (kept * means + scale * first) * inverse
        new_means_ref[:, lanes] = new_means
        second_moment = kept * (variances + means * means) + scale * second
        new_variances_ref[:, lanes] = second_moment * inverse - new_means * new_means


def update(scale, means, variances, mass, *sums):
    n = mass.shape[0]
    block = jax.ShapeDtypeStruct(means.shape, F32)
    new_means, new_variances, new_mass = pl.pallas_call(
        functools.partial(update_kernel, scale),
        out_shape=(block, block, jax.ShapeDtypeStruct((1, n), F32)),
        cost_estimate=HEAVY,
        compiler_params=params(16),
        name="update",
    )(means, variances, mass.reshape(1, n), *sums)
    return new_means, new_variances, new_mass.reshape(n)


def swap(value, axis, bit):
    size = lax.axis_size(axis)
    return lax.ppermute(value, axis, [(i, i ^ bit) for i in range(size)])


def vmem(value):
    return pltpu.with_memory_space_constraint(value, pltpu.VMEM)


def after(value, *others):
    return lax.optimization_barrier((value, *others))[0]


def gather_early(piece):
    bit = lax.axis_size("dp") // 4
    held = {0: piece}
    while bit > 1:
        held.update({q ^ bit: swap(value, "dp", 2 * bit) for q, value in held.items()})
        bit //= 2
    held[1] = swap(piece, "dp", 2)
    return held


def scatter_planes(first, second):
    held = [dict(enumerate(parts)) for parts in (first, second)]
    totals, near = [[parts.pop(0)] for parts in held], []
    planes, bit = len(first), 1
    while bit < planes:
        ready = []
        for parts in held:
            for q in sorted((q for q in parts if q & bit and q != bit), reverse=True):
                parts[q ^ bit] = parts[q ^ bit] + swap(after(parts.pop(q), *ready), "dp", 2 * bit)
                ready = [parts[q ^ bit]]
        for total, parts in zip(totals, held):
            part = swap(after(parts.pop(bit), *ready), "dp", 2 * bit)
            (near if bit == 1 else total).append(part)
        bit *= 2
    return *lax.optimization_barrier(tuple(sum(t[1:], t[0]) for t in totals)), *near


def merge(stats):
    peak = functools.reduce(jnp.maximum, [s[:, 0] for s in stats])
    total = sum(s[:, 1] * jnp.exp(s[:, 0] - peak) for s in stats)
    return jnp.stack([peak, total], axis=1)


def per_device(embeddings, comp_means, comp_variances, comp_mass):
    n = comp_means.shape[0]
    rows, width = embeddings.shape
    planes = lax.axis_size("dp") // 2
    variances = gather_early(comp_variances)
    linear = gather_early(coefficients(comp_means, comp_variances, comp_mass))
    other = swap(embeddings, "dp", 1)
    order = sorted(linear)
    late = [q for q in range(planes) if q not in linear]
    x_high, x_low, s_high, s_low = halves(embeddings, other)
    for q in late:
        variances[q] = swap(after(variances[q ^ 1], x_high), "dp", 2)
    n_early, n_late = n * len(order), n * len(late)

    def quad_scores(group, name):
        comps = n * len(group)
        operands = (*(vmem(variances[q]) for q in group), s_high, s_low)
        body = functools.partial(quad_kernel, n)
        return score_call(body, [(comps, 2 * rows)], [(2 * comps, width)], name, *operands)[0]

    quad = quad_scores(order, "early_quad")
    for q in late:
        linear[q] = swap(after(linear[q ^ 1], quad, linear[1]), "dp", 2)
    early, early_stats = score_call(
        functools.partial(early_kernel, n),
        [(n_early, 2 * rows), (2, 2 * rows)],
        [(2 * n_early, width)],
        "early_scores",
        *(vmem(linear[q]) for q in order),
        x_high,
        x_low,
        quad,
    )
    last, stats = score_call(
        functools.partial(last_kernel, n),
        [(n_late, 2 * rows), (2, 2, rows)],
        [(2 * n_late, width)],
        "last_scores",
        *(vmem(linear[q]) for q in late),
        x_high,
        x_low,
        quad_scores(late, "late_quad"),
        early_stats,
    )
    stats = merge([stats, swap(stats, "dp", 1)[::-1]])
    stats = merge([stats] + [swap(stats, "comp", q) for q in range(1, lax.axis_size("comp"))])

    *first, resp = first_moments(early, last, stats, x_high, x_low, n)
    second = second_moments(resp, s_high, s_low, n)
    place = {q: i for i, q in enumerate(order + late)}
    first, second = ([parts[place[q]] for q in range(planes)] for parts in (first, second))
    sums = scatter_planes(first, second)

    total_comps = n * lax.axis_size("dp") * lax.axis_size("comp")
    total_rows = embeddings.shape[0] * lax.axis_size("dp")
    scale = 0.6 * (total_comps / total_rows)
    return update(scale, comp_means, comp_variances, comp_mass, *sums)


def solution(mesh):
    placed = (P("dp", None), P(("comp", "dp"), None), P(("comp", "dp"), None), P(("comp", "dp")))
    return jax.shard_map(
        per_device,
        mesh=mesh,
        in_specs=placed,
        out_specs=(P(("comp", "dp"), None), P(("comp", "dp"), None), P(("comp", "dp"))),
        check_vma=False,
    )
```

```python
import functools

import jax
import jax.numpy as jnp
from jax import lax
from jax.experimental import pallas as pl
from jax.experimental.pallas import tpu as pltpu
from jax.sharding import PartitionSpec as P

F32 = jnp.float32
BF16 = jnp.bfloat16
LANES = 128
HEAVY = pl.CostEstimate(flops=10**10, bytes_accessed=10**8, transcendentals=0)
ACROSS = (((1,), (1,)), ((), ()))
WITHIN = (((1,), (0,)), ((), ()))


def params(megabytes):
    return pltpu.CompilerParams(vmem_limit_bytes=megabytes * 1024 * 1024)


def split(value):
    high = value.astype(BF16)
    return high, (value - high.astype(F32)).astype(BF16)


def diagonal(rows, columns):
    shape = (rows, columns)
    return lax.broadcasted_iota(jnp.int32, shape, 0) == lax.broadcasted_iota(jnp.int32, shape, 1)


def to_row(column, lanes):
    return jnp.sum(jnp.where(diagonal(column.shape[0], lanes), column, 0.0), axis=0, keepdims=True)


def to_column(row, rows):
    return jnp.sum(jnp.where(diagonal(rows, row.shape[1]), row, 0.0), axis=1, keepdims=True)


def coefficient_kernel(means_ref, variances_ref, mass_ref, pack_ref):
    n, width = means_ref.shape
    means, variances = means_ref[...], variances_ref[...]
    mean_prec = means * (1.0 / variances)
    sums = jnp.sum(jnp.log(variances) + means * mean_prec, axis=1, keepdims=True)
    offset = to_column(jnp.log(mass_ref[...]), n) - 0.5 * sums
    for c in range(width // LANES):
        pack_ref[c * n : (c + 1) * n, :] = mean_prec[:, c * LANES : (c + 1) * LANES]
    pack_ref[width // LANES * n :, :] = jnp.broadcast_to(to_row(offset, LANES), (8, LANES))


def coefficients(means, variances, mass):
    n, width = means.shape
    return pl.pallas_call(
        coefficient_kernel,
        out_shape=jax.ShapeDtypeStruct((width // LANES * n + 8, LANES), F32),
        cost_estimate=HEAVY,
        compiler_params=params(16),
        name="coefficients",
    )(means, variances, mass.reshape(1, n))


def halves_kernel(own_ref, other_ref, xh_ref, xl_ref, sh_ref, sl_ref):
    def put(block):
        xh_ref[...], xl_ref[...] = split(block)
        sh_ref[...], sl_ref[...] = split(block * block)

    first = pl.program_id(0) < pl.num_programs(0) // 2

    @pl.when(first)
    def _():
        put(own_ref[...])

    @pl.when(jnp.logical_not(first))
    def _():
        put(other_ref[...])


def halves(own, other):
    rows, width = own.shape
    tile = min(256, rows)
    steps = rows // tile
    out = jax.ShapeDtypeStruct((2 * rows, width), BF16)
    return pl.pallas_call(
        halves_kernel,
        grid=(2 * steps,),
        in_specs=[
            pl.BlockSpec((tile, width), lambda i: (jnp.minimum(i, steps - 1), 0)),
            pl.BlockSpec((tile, width), lambda i: (jnp.maximum(i - steps, 0), 0)),
        ],
        out_specs=[pl.BlockSpec((tile, width), lambda i: (i, 0))] * 4,
        out_shape=[out] * 4,
        cost_estimate=HEAVY,
        compiler_params=params(16),
        name="halves",
    )(own, other)


def load_packs(packs, weights, n):
    comps, tiles = n * len(packs), weights.shape[1] // LANES
    for q, pack in enumerate(packs):
        for c in range(tiles):
            lanes = slice(c * LANES, (c + 1) * LANES)
            high, low = split(pack[c * n : (c + 1) * n, :])
            weights[q * n : (q + 1) * n, lanes] = high
            weights[comps + q * n : comps + (q + 1) * n, lanes] = low
    return jnp.concatenate([to_column(pack[tiles * n : tiles * n + 1, :], n) for pack in packs])


def load_variances(variances, weights, n):
    comps = n * len(variances)
    for q, ref in enumerate(variances):
        high, low = split(-0.5 * (1.0 / ref[...]))
        weights[q * n : (q + 1) * n, :] = high
        weights[comps + q * n : comps + (q + 1) * n, :] = low


def product(weights, high, low, dims):
    comps = weights.shape[0] // 2
    both = lax.dot_general(weights, high, dims, preferred_element_type=F32)
    rest = lax.dot_general(weights[:comps], low, dims, preferred_element_type=F32)
    return both[:comps] + (both[comps:] + rest)


def row_tiles(rows, tile=256):
    tile = min(tile, rows)
    return [slice(i, i + tile) for i in range(0, rows, tile)]


def quad_kernel(n, *refs):
    *variances, high_ref, low_ref, out_ref, weights = refs
    load_variances(variances, weights, n)
    for tile in row_tiles(high_ref.shape[0]):
        out_ref[:, tile] = product(weights[...], high_ref[tile, :], low_ref[tile, :], ACROSS)


def stats_of(scores):
    peak = jnp.max(scores, axis=0, keepdims=True)
    return peak, jnp.sum(jnp.exp(scores - peak), axis=0, keepdims=True)


def joined(one, other):
    peak = jnp.maximum(one[0], other[0])
    return peak, one[1] * jnp.exp(one[0] - peak) + other[1] * jnp.exp(other[0] - peak)


def early_kernel(n, *refs):
    *linear, high_ref, low_ref, quad_ref, out_ref, stats_ref, weights = refs
    offset = load_packs(linear, weights, n)
    for tile in row_tiles(high_ref.shape[0]):
        scores = product(weights[...], high_ref[tile, :], low_ref[tile, :], ACROSS)
        scores = quad_ref[:, tile] + scores + offset
        out_ref[:, tile] = scores
        stats_ref[0:1, tile], stats_ref[1:2, tile] = stats_of(scores)


def half_tiles(half):
    for block in range(2):
        for part in row_tiles(half):
            yield slice(block * half + part.start, block * half + part.stop), block, part


def last_kernel(n, *refs):
    *linear, xh_ref, xl_ref, quad_ref, early_ref, out_ref, stats_ref, weights = refs
    offset = load_packs(linear, weights, n)
    for tile, block, part in half_tiles(stats_ref.shape[2]):
        scores = product(weights[...], xh_ref[tile, :], xl_ref[tile, :], ACROSS)
        scores = quad_ref[:, tile] + scores + offset
        out_ref[:, tile] = scores
        early = early_ref[0:1, tile], early_ref[1:2, tile]
        peak, total = joined(stats_of(scores), early)
        stats_ref[block, 0:1, part] = peak
        stats_ref[block, 1:2, part] = total


def score_call(body, out_shape, scratch, name, *operands):
    return pl.pallas_call(
        body,
        out_shape=[jax.ShapeDtypeStruct(shape, F32) for shape in out_shape],
        scratch_shapes=[pltpu.VMEM(shape, BF16) for shape in scratch],
        cost_estimate=HEAVY,
        compiler_params=params(24),
        name=name,
    )(*operands)


def moment_tiles(resp_ref, high_ref, low_ref, packs, n):
    for c in range(0, high_ref.shape[1], 2 * LANES):
        columns = slice(c, c + 2 * LANES)
        total = product(resp_ref[...], high_ref[:, columns], low_ref[:, columns], WITHIN)
        for q, pack in enumerate(packs):
            for k in range(2):
                place = (c // LANES + k) * n
                pack[place : place + n, :] = total[q * n : (q + 1) * n, k * LANES : (k + 1) * LANES]


def first_kernel(n, early_ref, late_ref, stats_ref, high_ref, low_ref, *refs):
    *packs, resp_ref = refs
    comps = resp_ref.shape[0] // 2
    counts = jnp.zeros((comps, LANES), F32)
    for tile, block, part in half_tiles(stats_ref.shape[2]):
        peak, total = stats_ref[block, 0:1, part], stats_ref[block, 1:2, part]
        scores = jnp.concatenate([early_ref[:, tile], late_ref[:, tile]])
        resp = jnp.exp(scores - peak) * (1.0 / total)
        resp_ref[:comps, tile], resp_ref[comps:, tile] = split(resp)
        counts += sum(resp[:, c : c + LANES] for c in range(0, resp.shape[1], LANES))
    moment_tiles(resp_ref, high_ref, low_ref, packs, n)
    column = jnp.sum(counts, axis=1, keepdims=True)
    for q, pack in enumerate(packs):
        row = to_row(column[q * n : (q + 1) * n], LANES)
        pack[-8:, :] = jnp.broadcast_to(row, (8, LANES))


def first_moments(early, late, stats, high, low, n):
    rows, width = high.shape
    comps = early.shape[0] + late.shape[0]
    pack = jax.ShapeDtypeStruct((width // LANES * n + 8, LANES), F32)
    return pl.pallas_call(
        functools.partial(first_kernel, n),
        out_shape=[pack] * (comps // n) + [jax.ShapeDtypeStruct((2 * comps, rows), BF16)],
        cost_estimate=HEAVY,
        compiler_params=params(24),
        name="first_moments",
    )(early, late, stats, high, low)


def second_kernel(n, resp_ref, high_ref, low_ref, *packs):
    moment_tiles(resp_ref, high_ref, low_ref, packs, n)


def second_moments(resp, high, low, n):
    pack = jax.ShapeDtypeStruct((high.shape[1] // LANES * n, LANES), F32)
    return pl.pallas_call(
        functools.partial(second_kernel, n),
        out_shape=[pack] * (resp.shape[0] // 2 // n),
        cost_estimate=HEAVY,
        compiler_params=params(24),
        name="second_moments",
    )(resp, high, low)


def update_kernel(
    scale,
    means_ref,
    variances_ref,
    mass_ref,
    first_ref,
    second_ref,
    near_first_ref,
    near_second_ref,
    new_means_ref,
    new_variances_ref,
    new_mass_ref,
):
    n, width = means_ref.shape
    tiles = width // LANES * n
    row = first_ref[tiles : tiles + 1, :n] + near_first_ref[tiles : tiles + 1, :n]
    new_row = 0.4 * mass_ref[...] + scale * row
    new_mass_ref[...] = new_row
    inverse = 1.0 / to_column(new_row, n)
    kept = 0.4 * to_column(mass_ref[...], n)
    for c in range(width // LANES):
        lanes, tile = slice(c * LANES, (c + 1) * LANES), slice(c * n, (c + 1) * n)
        means, variances = means_ref[:, lanes], variances_ref[:, lanes]
        first = first_ref[tile, :] + near_first_ref[tile, :]
        second = second_ref[tile, :] + near_second_ref[tile, :]
        new_means = (kept * means + scale * first) * inverse
        new_means_ref[:, lanes] = new_means
        second_moment = kept * (variances + means * means) + scale * second
        new_variances_ref[:, lanes] = second_moment * inverse - new_means * new_means


def update(scale, means, variances, mass, *sums):
    n = mass.shape[0]
    block = jax.ShapeDtypeStruct(means.shape, F32)
    new_means, new_variances, new_mass = pl.pallas_call(
        functools.partial(update_kernel, scale),
        out_shape=(block, block, jax.ShapeDtypeStruct((1, n), F32)),
        cost_estimate=HEAVY,
        compiler_params=params(16),
        name="update",
    )(means, variances, mass.reshape(1, n), *sums)
    return new_means, new_variances, new_mass.reshape(n)


def swap(value, axis, bit):
    size = lax.axis_size(axis)
    return lax.ppermute(value, axis, [(i, i ^ bit) for i in range(size)])


def vmem(value):
    return pltpu.with_memory_space_constraint(value, pltpu.VMEM)


def after(value, *others):
    return lax.optimization_barrier((value, *others))[0]


def gather_early(piece):
    bit = lax.axis_size("dp") // 4
    held = {0: piece}
    while bit > 1:
        held.update({q ^ bit: swap(value, "dp", 2 * bit) for q, value in held.items()})
        bit //= 2
    held[1] = swap(piece, "dp", 2)
    return held


def scatter_planes(first, second):
    held = [dict(enumerate(parts)) for parts in (first, second)]
    totals, near = [[parts.pop(0)] for parts in held], []
    planes, bit = len(first), 1
    while bit < planes:
        ready = []
        for parts in held:
            for q in sorted((q for q in parts if q & bit and q != bit), reverse=True):
                parts[q ^ bit] = parts[q ^ bit] + swap(parts.pop(q), "dp", 2 * bit)
                ready = [parts[q ^ bit]]
        for total, parts in zip(totals, held):
            part = swap(after(parts.pop(bit), *ready), "dp", 2 * bit)
            (near if bit == 1 else total).append(part)
        bit *= 2
    return *lax.optimization_barrier(tuple(sum(t[1:], t[0]) for t in totals)), *near


def merge(stats):
    peak = functools.reduce(jnp.maximum, [s[:, 0] for s in stats])
    total = sum(s[:, 1] * jnp.exp(s[:, 0] - peak) for s in stats)
    return jnp.stack([peak, total], axis=1)


def per_device(embeddings, comp_means, comp_variances, comp_mass):
    n = comp_means.shape[0]
    rows, width = embeddings.shape
    planes = lax.axis_size("dp") // 2
    variances = gather_early(comp_variances)
    linear = gather_early(coefficients(comp_means, comp_variances, comp_mass))
    other = swap(embeddings, "dp", 1)
    order = sorted(linear)
    late = [q for q in range(planes) if q not in linear]
    x_high, x_low, s_high, s_low = halves(embeddings, other)
    for q in late:
        variances[q] = swap(after(variances[q ^ 1], x_high), "dp", 2)
    n_early, n_late = n * len(order), n * len(late)

    def quad_scores(group, name):
        comps = n * len(group)
        operands = (*(vmem(variances[q]) for q in group), s_high, s_low)
        body = functools.partial(quad_kernel, n)
        return score_call(body, [(comps, 2 * rows)], [(2 * comps, width)], name, *operands)[0]

    quad = quad_scores(order, "early_quad")
    for q in late:
        linear[q] = swap(after(linear[q ^ 1], quad), "dp", 2)
    early, early_stats = score_call(
        functools.partial(early_kernel, n),
        [(n_early, 2 * rows), (2, 2 * rows)],
        [(2 * n_early, width)],
        "early_scores",
        *(vmem(linear[q]) for q in order),
        x_high,
        x_low,
        quad,
    )
    last, stats = score_call(
        functools.partial(last_kernel, n),
        [(n_late, 2 * rows), (2, 2, rows)],
        [(2 * n_late, width)],
        "last_scores",
        *(vmem(linear[q]) for q in late),
        x_high,
        x_low,
        quad_scores(late, "late_quad"),
        early_stats,
    )
    stats = merge([stats, swap(stats, "dp", 1)[::-1]])
    stats = merge([stats] + [swap(stats, "comp", q) for q in range(1, lax.axis_size("comp"))])

    *first, resp = first_moments(early, last, stats, x_high, x_low, n)
    second = second_moments(resp, s_high, s_low, n)
    place = {q: i for i, q in enumerate(order + late)}
    first, second = ([parts[place[q]] for q in range(planes)] for parts in (first, second))
    sums = scatter_planes(first, second)

    total_comps = n * lax.axis_size("dp") * lax.axis_size("comp")
    total_rows = embeddings.shape[0] * lax.axis_size("dp")
    scale = 0.6 * (total_comps / total_rows)
    return update(scale, comp_means, comp_variances, comp_mass, *sums)


def solution(mesh):
    placed = (P("dp", None), P(("comp", "dp"), None), P(("comp", "dp"), None), P(("comp", "dp")))
    return jax.shard_map(
        per_device,
        mesh=mesh,
        in_specs=placed,
        out_specs=(P(("comp", "dp"), None), P(("comp", "dp"), None), P(("comp", "dp"))),
        check_vma=False,
    )
```

```python
import functools

import jax
import jax.numpy as jnp
from jax import lax
from jax.experimental import pallas as pl
from jax.experimental.pallas import tpu as pltpu
from jax.sharding import PartitionSpec as P

F32 = jnp.float32
BF16 = jnp.bfloat16
LANES = 128
HEAVY = pl.CostEstimate(flops=10**10, bytes_accessed=10**8, transcendentals=0)
ACROSS = (((1,), (1,)), ((), ()))
WITHIN = (((1,), (0,)), ((), ()))


def params(megabytes):
    return pltpu.CompilerParams(vmem_limit_bytes=megabytes * 1024 * 1024)


def split(value):
    high = value.astype(BF16)
    return high, (value - high.astype(F32)).astype(BF16)


def diagonal(rows, columns):
    shape = (rows, columns)
    return lax.broadcasted_iota(jnp.int32, shape, 0) == lax.broadcasted_iota(jnp.int32, shape, 1)


def to_row(column, lanes):
    return jnp.sum(jnp.where(diagonal(column.shape[0], lanes), column, 0.0), axis=0, keepdims=True)


def to_column(row, rows):
    return jnp.sum(jnp.where(diagonal(rows, row.shape[1]), row, 0.0), axis=1, keepdims=True)


def coefficient_kernel(
    means_hbm, variances_hbm, mass_hbm, pack_ref, means_ref, variances_ref, mass_ref, sems
):
    sources = (variances_hbm, means_hbm, mass_hbm)
    targets = (variances_ref, means_ref, mass_ref)
    copies = [pltpu.make_async_copy(s, t, sems.at[i]) for i, (s, t) in enumerate(zip(sources, targets))]
    for copy in copies:
        copy.start()
    for copy in copies:
        copy.wait()
    n, width = means_ref.shape
    means, variances = means_ref[...], variances_ref[...]
    mean_prec = means * (1.0 / variances)
    sums = jnp.sum(jnp.log(variances) + means * mean_prec, axis=1, keepdims=True)
    offset = to_column(jnp.log(mass_ref[...]), n) - 0.5 * sums
    for c in range(width // LANES):
        pack_ref[c * n : (c + 1) * n, :] = mean_prec[:, c * LANES : (c + 1) * LANES]
    pack_ref[width // LANES * n :, :] = jnp.broadcast_to(to_row(offset, LANES), (8, LANES))


def coefficients(means, variances, mass):
    n, width = means.shape
    operands = (means, variances, mass.reshape(1, n))
    return pl.pallas_call(
        coefficient_kernel,
        in_specs=[pl.BlockSpec(memory_space=pl.ANY)] * 3,
        out_shape=jax.ShapeDtypeStruct((width // LANES * n + 8, LANES), F32),
        scratch_shapes=[
            pltpu.VMEM((n, width), F32),
            pltpu.VMEM((n, width), F32),
            pltpu.VMEM((1, n), F32),
            pltpu.SemaphoreType.DMA((3,)),
        ],
        cost_estimate=HEAVY,
        compiler_params=params(16),
        name="coefficients",
    )(*(pltpu.with_memory_space_constraint(x, pltpu.HBM) for x in operands))


def halves_kernel(own_ref, other_ref, xh_ref, xl_ref, sh_ref, sl_ref):
    def put(block):
        xh_ref[...], xl_ref[...] = split(block)
        sh_ref[...], sl_ref[...] = split(block * block)

    first = pl.program_id(0) < pl.num_programs(0) // 2

    @pl.when(first)
    def _():
        put(own_ref[...])

    @pl.when(jnp.logical_not(first))
    def _():
        put(other_ref[...])


def halves(own, other):
    rows, width = own.shape
    tile = min(256, rows)
    steps = rows // tile
    out = jax.ShapeDtypeStruct((2 * rows, width), BF16)
    return pl.pallas_call(
        halves_kernel,
        grid=(2 * steps,),
        in_specs=[
            pl.BlockSpec((tile, width), lambda i: (jnp.minimum(i, steps - 1), 0)),
            pl.BlockSpec((tile, width), lambda i: (jnp.maximum(i - steps, 0), 0)),
        ],
        out_specs=[pl.BlockSpec((tile, width), lambda i: (i, 0))] * 4,
        out_shape=[out] * 4,
        cost_estimate=HEAVY,
        compiler_params=params(16),
        name="halves",
    )(own, other)


def load_packs(packs, weights, n):
    comps, tiles = n * len(packs), weights.shape[1] // LANES
    for q, pack in enumerate(packs):
        for c in range(tiles):
            lanes = slice(c * LANES, (c + 1) * LANES)
            high, low = split(pack[c * n : (c + 1) * n, :])
            weights[q * n : (q + 1) * n, lanes] = high
            weights[comps + q * n : comps + (q + 1) * n, lanes] = low
    return jnp.concatenate([to_column(pack[tiles * n : tiles * n + 1, :], n) for pack in packs])


def load_variances(variances, weights, n):
    comps = n * len(variances)
    for q, ref in enumerate(variances):
        high, low = split(-0.5 * (1.0 / ref[...]))
        weights[q * n : (q + 1) * n, :] = high
        weights[comps + q * n : comps + (q + 1) * n, :] = low


def product(weights, high, low, dims):
    comps = weights.shape[0] // 2
    both = lax.dot_general(weights, high, dims, preferred_element_type=F32)
    rest = lax.dot_general(weights[:comps], low, dims, preferred_element_type=F32)
    return both[:comps] + (both[comps:] + rest)


def row_tiles(rows, tile=256):
    tile = min(tile, rows)
    return [slice(i, i + tile) for i in range(0, rows, tile)]


def quad_kernel(n, *refs):
    *variances, high_ref, low_ref, out_ref, weights = refs
    load_variances(variances, weights, n)
    for tile in row_tiles(high_ref.shape[0]):
        out_ref[:, tile] = product(weights[...], high_ref[tile, :], low_ref[tile, :], ACROSS)


def stats_of(scores):
    peak = jnp.max(scores, axis=0, keepdims=True)
    return peak, jnp.sum(jnp.exp(scores - peak), axis=0, keepdims=True)


def joined(one, other):
    peak = jnp.maximum(one[0], other[0])
    return peak, one[1] * jnp.exp(one[0] - peak) + other[1] * jnp.exp(other[0] - peak)


def early_kernel(n, *refs):
    *linear, high_ref, low_ref, quad_ref, out_ref, stats_ref, weights = refs
    offset = load_packs(linear, weights, n)
    for tile in row_tiles(high_ref.shape[0]):
        scores = product(weights[...], high_ref[tile, :], low_ref[tile, :], ACROSS)
        scores = quad_ref[:, tile] + scores + offset
        out_ref[:, tile] = scores
        stats_ref[0:1, tile], stats_ref[1:2, tile] = stats_of(scores)


def half_tiles(half):
    for block in range(2):
        for part in row_tiles(half):
            yield slice(block * half + part.start, block * half + part.stop), block, part


def last_kernel(n, *refs):
    *linear, xh_ref, xl_ref, quad_ref, early_ref, out_ref, stats_ref, weights = refs
    offset = load_packs(linear, weights, n)
    for tile, block, part in half_tiles(stats_ref.shape[2]):
        scores = product(weights[...], xh_ref[tile, :], xl_ref[tile, :], ACROSS)
        scores = quad_ref[:, tile] + scores + offset
        out_ref[:, tile] = scores
        early = early_ref[0:1, tile], early_ref[1:2, tile]
        peak, total = joined(stats_of(scores), early)
        stats_ref[block, 0:1, part] = peak
        stats_ref[block, 1:2, part] = total


def score_call(body, out_shape, scratch, name, *operands):
    return pl.pallas_call(
        body,
        out_shape=[jax.ShapeDtypeStruct(shape, F32) for shape in out_shape],
        scratch_shapes=[pltpu.VMEM(shape, BF16) for shape in scratch],
        cost_estimate=HEAVY,
        compiler_params=params(24),
        name=name,
    )(*operands)


def moment_tiles(resp_ref, high_ref, low_ref, packs, n):
    for c in range(0, high_ref.shape[1], 2 * LANES):
        columns = slice(c, c + 2 * LANES)
        total = product(resp_ref[...], high_ref[:, columns], low_ref[:, columns], WITHIN)
        for q, pack in enumerate(packs):
            for k in range(2):
                place = (c // LANES + k) * n
                pack[place : place + n, :] = total[q * n : (q + 1) * n, k * LANES : (k + 1) * LANES]


def first_kernel(n, early_ref, late_ref, stats_ref, high_ref, low_ref, *refs):
    *packs, resp_ref = refs
    comps = resp_ref.shape[0] // 2
    counts = jnp.zeros((comps, LANES), F32)
    for tile, block, part in half_tiles(stats_ref.shape[2]):
        peak, total = stats_ref[block, 0:1, part], stats_ref[block, 1:2, part]
        scores = jnp.concatenate([early_ref[:, tile], late_ref[:, tile]])
        resp = jnp.exp(scores - peak) * (1.0 / total)
        resp_ref[:comps, tile], resp_ref[comps:, tile] = split(resp)
        counts += sum(resp[:, c : c + LANES] for c in range(0, resp.shape[1], LANES))
    moment_tiles(resp_ref, high_ref, low_ref, packs, n)
    column = jnp.sum(counts, axis=1, keepdims=True)
    for q, pack in enumerate(packs):
        row = to_row(column[q * n : (q + 1) * n], LANES)
        pack[-8:, :] = jnp.broadcast_to(row, (8, LANES))


def first_moments(early, late, stats, high, low, n):
    rows, width = high.shape
    comps = early.shape[0] + late.shape[0]
    pack = jax.ShapeDtypeStruct((width // LANES * n + 8, LANES), F32)
    return pl.pallas_call(
        functools.partial(first_kernel, n),
        out_shape=[pack] * (comps // n) + [jax.ShapeDtypeStruct((2 * comps, rows), BF16)],
        cost_estimate=HEAVY,
        compiler_params=params(24),
        name="first_moments",
    )(early, late, stats, high, low)


def second_kernel(n, resp_ref, high_ref, low_ref, *packs):
    moment_tiles(resp_ref, high_ref, low_ref, packs, n)


def second_moments(resp, high, low, n):
    pack = jax.ShapeDtypeStruct((high.shape[1] // LANES * n, LANES), F32)
    return pl.pallas_call(
        functools.partial(second_kernel, n),
        out_shape=[pack] * (resp.shape[0] // 2 // n),
        cost_estimate=HEAVY,
        compiler_params=params(24),
        name="second_moments",
    )(resp, high, low)


def update_kernel(
    scale,
    means_ref,
    variances_ref,
    mass_ref,
    first_ref,
    second_ref,
    near_first_ref,
    near_second_ref,
    new_means_ref,
    new_variances_ref,
    new_mass_ref,
):
    n, width = means_ref.shape
    tiles = width // LANES * n
    row = first_ref[tiles : tiles + 1, :n] + near_first_ref[tiles : tiles + 1, :n]
    new_row = 0.4 * mass_ref[...] + scale * row
    new_mass_ref[...] = new_row
    inverse = 1.0 / to_column(new_row, n)
    kept = 0.4 * to_column(mass_ref[...], n)
    for c in range(width // LANES):
        lanes, tile = slice(c * LANES, (c + 1) * LANES), slice(c * n, (c + 1) * n)
        means, variances = means_ref[:, lanes], variances_ref[:, lanes]
        first = first_ref[tile, :] + near_first_ref[tile, :]
        second = second_ref[tile, :] + near_second_ref[tile, :]
        new_means = (kept * means + scale * first) * inverse
        new_means_ref[:, lanes] = new_means
        second_moment = kept * (variances + means * means) + scale * second
        new_variances_ref[:, lanes] = second_moment * inverse - new_means * new_means


def update(scale, means, variances, mass, *sums):
    n = mass.shape[0]
    block = jax.ShapeDtypeStruct(means.shape, F32)
    new_means, new_variances, new_mass = pl.pallas_call(
        functools.partial(update_kernel, scale),
        out_shape=(block, block, jax.ShapeDtypeStruct((1, n), F32)),
        cost_estimate=HEAVY,
        compiler_params=params(16),
        name="update",
    )(means, variances, mass.reshape(1, n), *sums)
    return new_means, new_variances, new_mass.reshape(n)


def swap(value, axis, bit):
    size = lax.axis_size(axis)
    return lax.ppermute(value, axis, [(i, i ^ bit) for i in range(size)])


def vmem(value):
    return pltpu.with_memory_space_constraint(value, pltpu.VMEM)


def after(value, *others):
    return lax.optimization_barrier((value, *others))[0]


def gather_early(piece):
    bit = lax.axis_size("dp") // 4
    held = {0: piece}
    while bit > 1:
        held.update({q ^ bit: swap(value, "dp", 2 * bit) for q, value in held.items()})
        bit //= 2
    held[1] = swap(piece, "dp", 2)
    return held


def scatter_planes(first, second):
    held = [dict(enumerate(parts)) for parts in (first, second)]
    totals, near = [[parts.pop(0)] for parts in held], []
    planes, bit = len(first), 1
    while bit < planes:
        ready = []
        for parts in held:
            for q in sorted((q for q in parts if q & bit and q != bit), reverse=True):
                parts[q ^ bit] = parts[q ^ bit] + swap(parts.pop(q), "dp", 2 * bit)
                ready = [parts[q ^ bit]]
        for total, parts in zip(totals, held):
            part = swap(after(parts.pop(bit), *ready), "dp", 2 * bit)
            (near if bit == 1 else total).append(part)
        bit *= 2
    return *lax.optimization_barrier(tuple(sum(t[1:], t[0]) for t in totals)), *near


def merge(stats):
    peak = functools.reduce(jnp.maximum, [s[:, 0] for s in stats])
    total = sum(s[:, 1] * jnp.exp(s[:, 0] - peak) for s in stats)
    return jnp.stack([peak, total], axis=1)


def per_device(embeddings, comp_means, comp_variances, comp_mass):
    n = comp_means.shape[0]
    rows, width = embeddings.shape
    planes = lax.axis_size("dp") // 2
    variances = gather_early(comp_variances)
    linear = gather_early(coefficients(comp_means, comp_variances, comp_mass))
    other = swap(embeddings, "dp", 1)
    order = sorted(linear)
    late = [q for q in range(planes) if q not in linear]
    x_high, x_low, s_high, s_low = halves(embeddings, other)
    for q in late:
        variances[q] = swap(after(variances[q ^ 1], x_high), "dp", 2)
    n_early, n_late = n * len(order), n * len(late)

    def quad_scores(group, name):
        comps = n * len(group)
        operands = (*(vmem(variances[q]) for q in group), s_high, s_low)
        body = functools.partial(quad_kernel, n)
        return score_call(body, [(comps, 2 * rows)], [(2 * comps, width)], name, *operands)[0]

    quad = quad_scores(order, "early_quad")
    for q in late:
        linear[q] = swap(after(linear[q ^ 1], quad), "dp", 2)
    early, early_stats = score_call(
        functools.partial(early_kernel, n),
        [(n_early, 2 * rows), (2, 2 * rows)],
        [(2 * n_early, width)],
        "early_scores",
        *(vmem(linear[q]) for q in order),
        x_high,
        x_low,
        quad,
    )
    last, stats = score_call(
        functools.partial(last_kernel, n),
        [(n_late, 2 * rows), (2, 2, rows)],
        [(2 * n_late, width)],
        "last_scores",
        *(vmem(linear[q]) for q in late),
        x_high,
        x_low,
        quad_scores(late, "late_quad"),
        early_stats,
    )
    stats = merge([stats, swap(stats, "dp", 1)[::-1]])
    stats = merge([stats] + [swap(stats, "comp", q) for q in range(1, lax.axis_size("comp"))])

    *first, resp = first_moments(early, last, stats, x_high, x_low, n)
    second = second_moments(resp, s_high, s_low, n)
    place = {q: i for i, q in enumerate(order + late)}
    first, second = ([parts[place[q]] for q in range(planes)] for parts in (first, second))
    sums = scatter_planes(first, second)

    total_comps = n * lax.axis_size("dp") * lax.axis_size("comp")
    total_rows = embeddings.shape[0] * lax.axis_size("dp")
    scale = 0.6 * (total_comps / total_rows)
    return update(scale, comp_means, comp_variances, comp_mass, *sums)


def solution(mesh):
    placed = (P("dp", None), P(("comp", "dp"), None), P(("comp", "dp"), None), P(("comp", "dp")))
    return jax.shard_map(
        per_device,
        mesh=mesh,
        in_specs=placed,
        out_specs=(P(("comp", "dp"), None), P(("comp", "dp"), None), P(("comp", "dp"))),
        check_vma=False,
    )
```

```python
import functools

import jax
import jax.numpy as jnp
from jax import lax
from jax.experimental import pallas as pl
from jax.experimental.pallas import tpu as pltpu
from jax.sharding import PartitionSpec as P

F32 = jnp.float32
BF16 = jnp.bfloat16
LANES = 128
HEAVY = pl.CostEstimate(flops=10**10, bytes_accessed=10**8, transcendentals=0)
LIGHT = pl.CostEstimate(flops=10**8, bytes_accessed=10**6, transcendentals=0)
ACROSS = (((1,), (1,)), ((), ()))
WITHIN = (((1,), (0,)), ((), ()))


def params(megabytes):
    return pltpu.CompilerParams(vmem_limit_bytes=megabytes * 1024 * 1024)


def split(value):
    high = value.astype(BF16)
    return high, (value - high.astype(F32)).astype(BF16)


def diagonal(rows, columns):
    shape = (rows, columns)
    return lax.broadcasted_iota(jnp.int32, shape, 0) == lax.broadcasted_iota(jnp.int32, shape, 1)


def to_row(column, lanes):
    return jnp.sum(jnp.where(diagonal(column.shape[0], lanes), column, 0.0), axis=0, keepdims=True)


def to_column(row, rows):
    return jnp.sum(jnp.where(diagonal(rows, row.shape[1]), row, 0.0), axis=1, keepdims=True)


def coefficient_kernel(
    means_hbm, variances_hbm, mass_hbm, pack_ref, means_ref, variances_ref, mass_ref, sems
):
    sources = (variances_hbm, means_hbm, mass_hbm)
    targets = (variances_ref, means_ref, mass_ref)
    copies = [pltpu.make_async_copy(s, t, sems.at[i]) for i, (s, t) in enumerate(zip(sources, targets))]
    for copy in copies:
        copy.start()
    for copy in copies:
        copy.wait()
    n, width = means_ref.shape
    means, variances = means_ref[...], variances_ref[...]
    mean_prec = means * (1.0 / variances)
    sums = jnp.sum(jnp.log(variances) + means * mean_prec, axis=1, keepdims=True)
    offset = to_column(jnp.log(mass_ref[...]), n) - 0.5 * sums
    for c in range(width // LANES):
        pack_ref[c * n : (c + 1) * n, :] = mean_prec[:, c * LANES : (c + 1) * LANES]
    pack_ref[width // LANES * n :, :] = jnp.broadcast_to(to_row(offset, LANES), (8, LANES))


def coefficients(means, variances, mass):
    n, width = means.shape
    operands = (means, variances, mass.reshape(1, n))
    return pl.pallas_call(
        coefficient_kernel,
        in_specs=[pl.BlockSpec(memory_space=pl.ANY)] * 3,
        out_shape=jax.ShapeDtypeStruct((width // LANES * n + 8, LANES), F32),
        scratch_shapes=[
            pltpu.VMEM((n, width), F32),
            pltpu.VMEM((n, width), F32),
            pltpu.VMEM((1, n), F32),
            pltpu.SemaphoreType.DMA((3,)),
        ],
        cost_estimate=HEAVY,
        compiler_params=params(16),
        name="coefficients",
    )(*(pltpu.with_memory_space_constraint(x, pltpu.HBM) for x in operands))


def halves_kernel(own_ref, other_ref, xh_ref, xl_ref, sh_ref, sl_ref):
    def put(block):
        xh_ref[...], xl_ref[...] = split(block)
        sh_ref[...], sl_ref[...] = split(block * block)

    first = pl.program_id(0) < pl.num_programs(0) // 2

    @pl.when(first)
    def _():
        put(own_ref[...])

    @pl.when(jnp.logical_not(first))
    def _():
        put(other_ref[...])


def halves(own, other):
    rows, width = own.shape
    tile = min(256, rows)
    steps = rows // tile
    out = jax.ShapeDtypeStruct((2 * rows, width), BF16)
    return pl.pallas_call(
        halves_kernel,
        grid=(2 * steps,),
        in_specs=[
            pl.BlockSpec((tile, width), lambda i: (jnp.minimum(i, steps - 1), 0)),
            pl.BlockSpec((tile, width), lambda i: (jnp.maximum(i - steps, 0), 0)),
        ],
        out_specs=[pl.BlockSpec((tile, width), lambda i: (i, 0))] * 4,
        out_shape=[out] * 4,
        cost_estimate=HEAVY,
        compiler_params=params(16),
        name="halves",
    )(own, other)


def load_packs(packs, weights, n):
    comps, tiles = n * len(packs), weights.shape[1] // LANES
    for q, pack in enumerate(packs):
        for c in range(tiles):
            lanes = slice(c * LANES, (c + 1) * LANES)
            high, low = split(pack[c * n : (c + 1) * n, :])
            weights[q * n : (q + 1) * n, lanes] = high
            weights[comps + q * n : comps + (q + 1) * n, lanes] = low
    if packs[0].shape[0] == tiles * n:
        return None
    return jnp.concatenate([to_column(pack[tiles * n : tiles * n + 1, :], n) for pack in packs])


def load_variances(variances, weights, n):
    comps = n * len(variances)
    for q, ref in enumerate(variances):
        high, low = split(-0.5 * (1.0 / ref[...]))
        weights[q * n : (q + 1) * n, :] = high
        weights[comps + q * n : comps + (q + 1) * n, :] = low


def product(weights, high, low, dims):
    comps = weights.shape[0] // 2
    both = lax.dot_general(weights, high, dims, preferred_element_type=F32)
    rest = lax.dot_general(weights[:comps], low, dims, preferred_element_type=F32)
    return both[:comps] + (both[comps:] + rest)


def row_tiles(rows, tile=256):
    tile = min(tile, rows)
    return [slice(i, i + tile) for i in range(0, rows, tile)]


def quad_kernel(n, *refs):
    *variances, high_ref, low_ref, out_ref, weights = refs
    load_variances(variances, weights, n)
    for tile in row_tiles(high_ref.shape[0]):
        out_ref[:, tile] = product(weights[...], high_ref[tile, :], low_ref[tile, :], ACROSS)


def stats_of(scores):
    peak = jnp.max(scores, axis=0, keepdims=True)
    return peak, jnp.sum(jnp.exp(scores - peak), axis=0, keepdims=True)


def joined(one, other):
    peak = jnp.maximum(one[0], other[0])
    return peak, one[1] * jnp.exp(one[0] - peak) + other[1] * jnp.exp(other[0] - peak)


def early_kernel(n, *refs):
    *linear, high_ref, low_ref, quad_ref, out_ref, stats_ref, weights = refs
    offset = load_packs(linear, weights, n)
    for tile in row_tiles(high_ref.shape[0]):
        scores = product(weights[...], high_ref[tile, :], low_ref[tile, :], ACROSS)
        scores = quad_ref[:, tile] + scores + offset
        out_ref[:, tile] = scores
        stats_ref[0:1, tile], stats_ref[1:2, tile] = stats_of(scores)


def half_tiles(half):
    for block in range(2):
        for part in row_tiles(half):
            yield slice(block * half + part.start, block * half + part.stop), block, part


def head_kernel(n, *refs):
    *linear, high_ref, low_ref, quad_ref, out_ref, weights = refs
    load_packs(linear, weights, n)
    columns = slice(0, weights.shape[1])
    for tile in row_tiles(high_ref.shape[0]):
        scores = product(weights[...], high_ref[tile, columns], low_ref[tile, columns], ACROSS)
        out_ref[:, tile] = quad_ref[:, tile] + scores


def last_kernel(n, *refs):
    *linear, high_ref, low_ref, quad_ref, early_ref, out_ref, stats_ref, weights = refs
    offset = load_packs(linear, weights, n)
    columns = slice(high_ref.shape[1] - weights.shape[1], high_ref.shape[1])
    for tile, block, part in half_tiles(stats_ref.shape[2]):
        scores = product(weights[...], high_ref[tile, columns], low_ref[tile, columns], ACROSS)
        scores = quad_ref[:, tile] + scores + offset
        out_ref[:, tile] = scores
        early = early_ref[0:1, tile], early_ref[1:2, tile]
        peak, total = joined(stats_of(scores), early)
        stats_ref[block, 0:1, part] = peak
        stats_ref[block, 1:2, part] = total


def score_call(body, out_shape, scratch, name, *operands, cost=None):
    return pl.pallas_call(
        body,
        out_shape=[jax.ShapeDtypeStruct(shape, F32) for shape in out_shape],
        scratch_shapes=[pltpu.VMEM(shape, BF16) for shape in scratch],
        cost_estimate=cost or HEAVY,
        compiler_params=params(24),
        name=name,
    )(*operands)


def moment_tiles(resp_ref, high_ref, low_ref, packs, n):
    for c in range(0, high_ref.shape[1], 2 * LANES):
        columns = slice(c, c + 2 * LANES)
        total = product(resp_ref[...], high_ref[:, columns], low_ref[:, columns], WITHIN)
        for q, pack in enumerate(packs):
            for k in range(2):
                place = (c // LANES + k) * n
                pack[place : place + n, :] = total[q * n : (q + 1) * n, k * LANES : (k + 1) * LANES]


def first_kernel(n, early_ref, late_ref, stats_ref, high_ref, low_ref, *refs):
    *packs, resp_ref = refs
    comps = resp_ref.shape[0] // 2
    counts = jnp.zeros((comps, LANES), F32)
    for tile, block, part in half_tiles(stats_ref.shape[2]):
        peak, total = stats_ref[block, 0:1, part], stats_ref[block, 1:2, part]
        scores = jnp.concatenate([early_ref[:, tile], late_ref[:, tile]])
        resp = jnp.exp(scores - peak) * (1.0 / total)
        resp_ref[:comps, tile], resp_ref[comps:, tile] = split(resp)
        counts += sum(resp[:, c : c + LANES] for c in range(0, resp.shape[1], LANES))
    moment_tiles(resp_ref, high_ref, low_ref, packs, n)
    column = jnp.sum(counts, axis=1, keepdims=True)
    for q, pack in enumerate(packs):
        row = to_row(column[q * n : (q + 1) * n], LANES)
        pack[-8:, :] = jnp.broadcast_to(row, (8, LANES))


def first_moments(early, late, stats, high, low, n):
    rows, width = high.shape
    comps = early.shape[0] + late.shape[0]
    pack = jax.ShapeDtypeStruct((width // LANES * n + 8, LANES), F32)
    return pl.pallas_call(
        functools.partial(first_kernel, n),
        out_shape=[pack] * (comps // n) + [jax.ShapeDtypeStruct((2 * comps, rows), BF16)],
        cost_estimate=HEAVY,
        compiler_params=params(24),
        name="first_moments",
    )(early, late, stats, high, low)


def second_kernel(n, resp_ref, high_ref, low_ref, *packs):
    moment_tiles(resp_ref, high_ref, low_ref, packs, n)


def second_moments(resp, high, low, n):
    pack = jax.ShapeDtypeStruct((high.shape[1] // LANES * n, LANES), F32)
    return pl.pallas_call(
        functools.partial(second_kernel, n),
        out_shape=[pack] * (resp.shape[0] // 2 // n),
        cost_estimate=HEAVY,
        compiler_params=params(24),
        name="second_moments",
    )(resp, high, low)


def update_kernel(
    scale,
    means_ref,
    variances_ref,
    mass_ref,
    first_ref,
    second_ref,
    near_first_ref,
    near_second_ref,
    new_means_ref,
    new_variances_ref,
    new_mass_ref,
):
    n, width = means_ref.shape
    tiles = width // LANES * n
    row = first_ref[tiles : tiles + 1, :n] + near_first_ref[tiles : tiles + 1, :n]
    new_row = 0.4 * mass_ref[...] + scale * row
    new_mass_ref[...] = new_row
    inverse = 1.0 / to_column(new_row, n)
    kept = 0.4 * to_column(mass_ref[...], n)
    for c in range(width // LANES):
        lanes, tile = slice(c * LANES, (c + 1) * LANES), slice(c * n, (c + 1) * n)
        means, variances = means_ref[:, lanes], variances_ref[:, lanes]
        first = first_ref[tile, :] + near_first_ref[tile, :]
        second = second_ref[tile, :] + near_second_ref[tile, :]
        new_means = (kept * means + scale * first) * inverse
        new_means_ref[:, lanes] = new_means
        second_moment = kept * (variances + means * means) + scale * second
        new_variances_ref[:, lanes] = second_moment * inverse - new_means * new_means


def update(scale, means, variances, mass, *sums):
    n = mass.shape[0]
    block = jax.ShapeDtypeStruct(means.shape, F32)
    new_means, new_variances, new_mass = pl.pallas_call(
        functools.partial(update_kernel, scale),
        out_shape=(block, block, jax.ShapeDtypeStruct((1, n), F32)),
        cost_estimate=HEAVY,
        compiler_params=params(16),
        name="update",
    )(means, variances, mass.reshape(1, n), *sums)
    return new_means, new_variances, new_mass.reshape(n)


def swap(value, axis, bit):
    size = lax.axis_size(axis)
    return lax.ppermute(value, axis, [(i, i ^ bit) for i in range(size)])


def vmem(value):
    return pltpu.with_memory_space_constraint(value, pltpu.VMEM)


def after(value, *others):
    return lax.optimization_barrier((value, *others))[0]


def gather_early(piece):
    bit = lax.axis_size("dp") // 4
    held = {0: piece}
    while bit > 1:
        held.update({q ^ bit: swap(value, "dp", 2 * bit) for q, value in held.items()})
        bit //= 2
    held[1] = swap(piece, "dp", 2)
    return held


def scatter_planes(first, second):
    held = [dict(enumerate(parts)) for parts in (first, second)]
    totals, near = [[parts.pop(0)] for parts in held], []
    planes, bit = len(first), 1
    while bit < planes:
        ready = []
        for parts in held:
            for q in sorted((q for q in parts if q & bit and q != bit), reverse=True):
                parts[q ^ bit] = parts[q ^ bit] + swap(parts.pop(q), "dp", 2 * bit)
                ready = [parts[q ^ bit]]
        for total, parts in zip(totals, held):
            part = swap(after(parts.pop(bit), *ready), "dp", 2 * bit)
            (near if bit == 1 else total).append(part)
        bit *= 2
    return *lax.optimization_barrier(tuple(sum(t[1:], t[0]) for t in totals)), *near


def merge(stats):
    peak = functools.reduce(jnp.maximum, [s[:, 0] for s in stats])
    total = sum(s[:, 1] * jnp.exp(s[:, 0] - peak) for s in stats)
    return jnp.stack([peak, total], axis=1)


def per_device(embeddings, comp_means, comp_variances, comp_mass):
    n = comp_means.shape[0]
    rows, width = embeddings.shape
    planes = lax.axis_size("dp") // 2
    variances = gather_early(comp_variances)
    linear = gather_early(coefficients(comp_means, comp_variances, comp_mass))
    other = swap(embeddings, "dp", 1)
    order = sorted(linear)
    late = [q for q in range(planes) if q not in linear]
    x_high, x_low, s_high, s_low = halves(embeddings, other)
    for q in late:
        variances[q] = swap(after(variances[q ^ 1], x_high), "dp", 2)
    n_early, n_late = n * len(order), n * len(late)

    def quad_scores(group, name, cost=None):
        comps = n * len(group)
        operands = (*(vmem(variances[q]) for q in group), s_high, s_low)
        body = functools.partial(quad_kernel, n)
        return score_call(body, [(comps, 2 * rows)], [(2 * comps, width)], name, *operands, cost=cost)[0]

    quad = quad_scores(order, "early_quad")
    head = width // LANES * 2 // 3
    heads, tails = [], []
    for q in late:
        source = after(linear[q ^ 1], quad)
        heads.append(vmem(swap(source[: head * n], "dp", 2)))
        tails.append(source[head * n :])
    early, early_stats = score_call(
        functools.partial(early_kernel, n),
        [(n_early, 2 * rows), (2, 2 * rows)],
        [(2 * n_early, width)],
        "early_scores",
        *(vmem(linear[q]) for q in order),
        x_high,
        x_low,
        quad,
        cost=LIGHT,
    )
    tails = [vmem(swap(after(tail, early), "dp", 2)) for tail in tails]
    (part,) = score_call(
        functools.partial(head_kernel, n),
        [(n_late, 2 * rows)],
        [(2 * n_late, head * LANES)],
        "late_head",
        *heads,
        x_high,
        x_low,
        quad_scores(late, "late_quad", LIGHT),
        cost=LIGHT,
    )
    last, stats = score_call(
        functools.partial(last_kernel, n),
        [(n_late, 2 * rows), (2, 2, rows)],
        [(2 * n_late, width - head * LANES)],
        "last_scores",
        *tails,
        x_high,
        x_low,
        part,
        early_stats,
    )
    stats = merge([stats, swap(stats, "dp", 1)[::-1]])
    stats = merge([stats] + [swap(stats, "comp", q) for q in range(1, lax.axis_size("comp"))])

    *first, resp = first_moments(early, last, stats, x_high, x_low, n)
    second = second_moments(resp, s_high, s_low, n)
    place = {q: i for i, q in enumerate(order + late)}
    first, second = ([parts[place[q]] for q in range(planes)] for parts in (first, second))
    sums = scatter_planes(first, second)

    total_comps = n * lax.axis_size("dp") * lax.axis_size("comp")
    total_rows = embeddings.shape[0] * lax.axis_size("dp")
    scale = 0.6 * (total_comps / total_rows)
    return update(scale, comp_means, comp_variances, comp_mass, *sums)


def solution(mesh):
    placed = (P("dp", None), P(("comp", "dp"), None), P(("comp", "dp"), None), P(("comp", "dp")))
    return jax.shard_map(
        per_device,
        mesh=mesh,
        in_specs=placed,
        out_specs=(P(("comp", "dp"), None), P(("comp", "dp"), None), P(("comp", "dp"))),
        check_vma=False,
    )
```

```python
import functools

import jax
import jax.numpy as jnp
from jax import lax
from jax.experimental import pallas as pl
from jax.experimental.pallas import tpu as pltpu
from jax.sharding import PartitionSpec as P

F32 = jnp.float32
BF16 = jnp.bfloat16
LANES = 128
HEAVY = pl.CostEstimate(flops=10**10, bytes_accessed=10**8, transcendentals=0)
LIGHT = pl.CostEstimate(flops=10**8, bytes_accessed=10**6, transcendentals=0)
ACROSS = (((1,), (1,)), ((), ()))
WITHIN = (((1,), (0,)), ((), ()))


def params(megabytes):
    return pltpu.CompilerParams(vmem_limit_bytes=megabytes * 1024 * 1024)


def split(value):
    high = value.astype(BF16)
    return high, (value - high.astype(F32)).astype(BF16)


def diagonal(rows, columns):
    shape = (rows, columns)
    return lax.broadcasted_iota(jnp.int32, shape, 0) == lax.broadcasted_iota(jnp.int32, shape, 1)


def to_row(column, lanes):
    return jnp.sum(jnp.where(diagonal(column.shape[0], lanes), column, 0.0), axis=0, keepdims=True)


def to_column(row, rows):
    return jnp.sum(jnp.where(diagonal(rows, row.shape[1]), row, 0.0), axis=1, keepdims=True)


def coefficient_kernel(
    means_hbm, variances_hbm, mass_hbm, pack_ref, means_ref, variances_ref, mass_ref, sems
):
    sources = (variances_hbm, means_hbm, mass_hbm)
    targets = (variances_ref, means_ref, mass_ref)
    copies = [pltpu.make_async_copy(s, t, sems.at[i]) for i, (s, t) in enumerate(zip(sources, targets))]
    for copy in copies:
        copy.start()
    for copy in copies:
        copy.wait()
    n, width = means_ref.shape
    means, variances = means_ref[...], variances_ref[...]
    mean_prec = means * (1.0 / variances)
    sums = jnp.sum(jnp.log(variances) + means * mean_prec, axis=1, keepdims=True)
    offset = to_column(jnp.log(mass_ref[...]), n) - 0.5 * sums
    for c in range(width // LANES):
        pack_ref[c * n : (c + 1) * n, :] = mean_prec[:, c * LANES : (c + 1) * LANES]
    pack_ref[width // LANES * n :, :] = jnp.broadcast_to(to_row(offset, LANES), (8, LANES))


def coefficients(means, variances, mass):
    n, width = means.shape
    operands = (means, variances, mass.reshape(1, n))
    return pl.pallas_call(
        coefficient_kernel,
        in_specs=[pl.BlockSpec(memory_space=pl.ANY)] * 3,
        out_shape=jax.ShapeDtypeStruct((width // LANES * n + 8, LANES), F32),
        scratch_shapes=[
            pltpu.VMEM((n, width), F32),
            pltpu.VMEM((n, width), F32),
            pltpu.VMEM((1, n), F32),
            pltpu.SemaphoreType.DMA((3,)),
        ],
        cost_estimate=HEAVY,
        compiler_params=params(16),
        name="coefficients",
    )(*(pltpu.with_memory_space_constraint(x, pltpu.HBM) for x in operands))


def halves_kernel(own_ref, other_ref, xh_ref, xl_ref, sh_ref, sl_ref):
    def put(block):
        xh_ref[...], xl_ref[...] = split(block)
        sh_ref[...], sl_ref[...] = split(block * block)

    first = pl.program_id(0) < pl.num_programs(0) // 2

    @pl.when(first)
    def _():
        put(own_ref[...])

    @pl.when(jnp.logical_not(first))
    def _():
        put(other_ref[...])


def halves(own, other):
    rows, width = own.shape
    tile = min(256, rows)
    steps = rows // tile
    out = jax.ShapeDtypeStruct((2 * rows, width), BF16)
    return pl.pallas_call(
        halves_kernel,
        grid=(2 * steps,),
        in_specs=[
            pl.BlockSpec((tile, width), lambda i: (jnp.minimum(i, steps - 1), 0)),
            pl.BlockSpec((tile, width), lambda i: (jnp.maximum(i - steps, 0), 0)),
        ],
        out_specs=[pl.BlockSpec((tile, width), lambda i: (i, 0))] * 4,
        out_shape=[out] * 4,
        cost_estimate=HEAVY,
        compiler_params=params(16),
        name="halves",
    )(own, other)


def load_packs(packs, weights, n):
    comps, tiles = n * len(packs), weights.shape[1] // LANES
    for q, pack in enumerate(packs):
        for c in range(tiles):
            lanes = slice(c * LANES, (c + 1) * LANES)
            high, low = split(pack[c * n : (c + 1) * n, :])
            weights[q * n : (q + 1) * n, lanes] = high
            weights[comps + q * n : comps + (q + 1) * n, lanes] = low
    if packs[0].shape[0] == tiles * n:
        return None
    return jnp.concatenate([to_column(pack[tiles * n : tiles * n + 1, :], n) for pack in packs])


def load_variances(variances, weights, n):
    comps = n * len(variances)
    for q, ref in enumerate(variances):
        high, low = split(-0.5 * (1.0 / ref[...]))
        weights[q * n : (q + 1) * n, :] = high
        weights[comps + q * n : comps + (q + 1) * n, :] = low


def product(weights, high, low, dims):
    comps = weights.shape[0] // 2
    both = lax.dot_general(weights, high, dims, preferred_element_type=F32)
    rest = lax.dot_general(weights[:comps], low, dims, preferred_element_type=F32)
    return both[:comps] + (both[comps:] + rest)


def row_tiles(rows, tile=256):
    tile = min(tile, rows)
    return [slice(i, i + tile) for i in range(0, rows, tile)]


def quad_kernel(n, *refs):
    *variances, high_ref, low_ref, out_ref, weights = refs
    load_variances(variances, weights, n)
    for tile in row_tiles(high_ref.shape[0]):
        out_ref[:, tile] = product(weights[...], high_ref[tile, :], low_ref[tile, :], ACROSS)


def stats_of(scores):
    peak = jnp.max(scores, axis=0, keepdims=True)
    return peak, jnp.sum(jnp.exp(scores - peak), axis=0, keepdims=True)


def joined(one, other):
    peak = jnp.maximum(one[0], other[0])
    return peak, one[1] * jnp.exp(one[0] - peak) + other[1] * jnp.exp(other[0] - peak)


def early_kernel(n, *refs):
    *linear, high_ref, low_ref, quad_ref, out_ref, stats_ref, weights = refs
    offset = load_packs(linear, weights, n)
    for tile in row_tiles(high_ref.shape[0]):
        scores = product(weights[...], high_ref[tile, :], low_ref[tile, :], ACROSS)
        scores = quad_ref[:, tile] + scores + offset
        out_ref[:, tile] = scores
        stats_ref[0:1, tile], stats_ref[1:2, tile] = stats_of(scores)


def half_tiles(half):
    for block in range(2):
        for part in row_tiles(half):
            yield slice(block * half + part.start, block * half + part.stop), block, part


def head_kernel(n, *refs):
    *linear, high_ref, low_ref, quad_ref, out_ref, weights = refs
    load_packs(linear, weights, n)
    columns = slice(0, weights.shape[1])
    for tile in row_tiles(high_ref.shape[0]):
        scores = product(weights[...], high_ref[tile, columns], low_ref[tile, columns], ACROSS)
        out_ref[:, tile] = quad_ref[:, tile] + scores


def last_kernel(n, *refs):
    *linear, high_ref, low_ref, quad_ref, early_ref, out_ref, stats_ref, weights = refs
    offset = load_packs(linear, weights, n)
    columns = slice(high_ref.shape[1] - weights.shape[1], high_ref.shape[1])
    for tile, block, part in half_tiles(stats_ref.shape[2]):
        scores = product(weights[...], high_ref[tile, columns], low_ref[tile, columns], ACROSS)
        scores = quad_ref[:, tile] + scores + offset
        out_ref[:, tile] = scores
        early = early_ref[0:1, tile], early_ref[1:2, tile]
        peak, total = joined(stats_of(scores), early)
        stats_ref[block, 0:1, part] = peak
        stats_ref[block, 1:2, part] = total


def score_call(body, out_shape, scratch, name, *operands, cost=None):
    return pl.pallas_call(
        body,
        out_shape=[jax.ShapeDtypeStruct(shape, F32) for shape in out_shape],
        scratch_shapes=[pltpu.VMEM(shape, BF16) for shape in scratch],
        cost_estimate=cost or HEAVY,
        compiler_params=params(24),
        name=name,
    )(*operands)


def moment_tiles(resp_ref, high_ref, low_ref, packs, n):
    for c in range(0, high_ref.shape[1], 2 * LANES):
        columns = slice(c, c + 2 * LANES)
        total = product(resp_ref[...], high_ref[:, columns], low_ref[:, columns], WITHIN)
        for q, pack in enumerate(packs):
            for k in range(2):
                place = (c // LANES + k) * n
                pack[place : place + n, :] = total[q * n : (q + 1) * n, k * LANES : (k + 1) * LANES]


def first_kernel(n, early_ref, late_ref, stats_ref, high_ref, low_ref, *refs):
    *packs, resp_ref = refs
    comps = resp_ref.shape[0] // 2
    counts = jnp.zeros((comps, LANES), F32)
    for tile, block, part in half_tiles(stats_ref.shape[2]):
        peak, total = stats_ref[block, 0:1, part], stats_ref[block, 1:2, part]
        scores = jnp.concatenate([early_ref[:, tile], late_ref[:, tile]])
        resp = jnp.exp(scores - peak) * (1.0 / total)
        resp_ref[:comps, tile], resp_ref[comps:, tile] = split(resp)
        counts += sum(resp[:, c : c + LANES] for c in range(0, resp.shape[1], LANES))
    moment_tiles(resp_ref, high_ref, low_ref, packs, n)
    column = jnp.sum(counts, axis=1, keepdims=True)
    for q, pack in enumerate(packs):
        row = to_row(column[q * n : (q + 1) * n], LANES)
        pack[-8:, :] = jnp.broadcast_to(row, (8, LANES))


def first_moments(early, late, stats, high, low, n):
    rows, width = high.shape
    comps = early.shape[0] + late.shape[0]
    pack = jax.ShapeDtypeStruct((width // LANES * n + 8, LANES), F32)
    return pl.pallas_call(
        functools.partial(first_kernel, n),
        out_shape=[pack] * (comps // n) + [jax.ShapeDtypeStruct((2 * comps, rows), BF16)],
        cost_estimate=HEAVY,
        compiler_params=params(24),
        name="first_moments",
    )(early, late, stats, high, low)


def second_kernel(n, resp_ref, high_ref, low_ref, *packs):
    moment_tiles(resp_ref, high_ref, low_ref, packs, n)


def second_moments(resp, high, low, n):
    pack = jax.ShapeDtypeStruct((high.shape[1] // LANES * n, LANES), F32)
    return pl.pallas_call(
        functools.partial(second_kernel, n),
        out_shape=[pack] * (resp.shape[0] // 2 // n),
        cost_estimate=HEAVY,
        compiler_params=params(24),
        name="second_moments",
    )(resp, high, low)


def update_kernel(
    scale,
    means_ref,
    variances_ref,
    mass_ref,
    first_ref,
    second_ref,
    near_first_ref,
    near_second_ref,
    new_means_ref,
    new_variances_ref,
    new_mass_ref,
):
    n, width = means_ref.shape
    tiles = width // LANES * n
    row = first_ref[tiles : tiles + 1, :n] + near_first_ref[tiles : tiles + 1, :n]
    new_row = 0.4 * mass_ref[...] + scale * row
    new_mass_ref[...] = new_row
    inverse = 1.0 / to_column(new_row, n)
    kept = 0.4 * to_column(mass_ref[...], n)
    for c in range(width // LANES):
        lanes, tile = slice(c * LANES, (c + 1) * LANES), slice(c * n, (c + 1) * n)
        means, variances = means_ref[:, lanes], variances_ref[:, lanes]
        first = first_ref[tile, :] + near_first_ref[tile, :]
        second = second_ref[tile, :] + near_second_ref[tile, :]
        new_means = (kept * means + scale * first) * inverse
        new_means_ref[:, lanes] = new_means
        second_moment = kept * (variances + means * means) + scale * second
        new_variances_ref[:, lanes] = second_moment * inverse - new_means * new_means


def update(scale, means, variances, mass, *sums):
    n = mass.shape[0]
    block = jax.ShapeDtypeStruct(means.shape, F32)
    new_means, new_variances, new_mass = pl.pallas_call(
        functools.partial(update_kernel, scale),
        out_shape=(block, block, jax.ShapeDtypeStruct((1, n), F32)),
        cost_estimate=HEAVY,
        compiler_params=params(16),
        name="update",
    )(means, variances, mass.reshape(1, n), *sums)
    return new_means, new_variances, new_mass.reshape(n)


def swap(value, axis, bit):
    size = lax.axis_size(axis)
    return lax.ppermute(value, axis, [(i, i ^ bit) for i in range(size)])


def vmem(value):
    return pltpu.with_memory_space_constraint(value, pltpu.VMEM)


def after(value, *others):
    return lax.optimization_barrier((value, *others))[0]


def dp_planes():
    planes = lax.axis_size("dp") // 2
    return planes, planes.bit_length() - 1


def swap_planes(value, step):
    planes, _ = dp_planes()
    bits = (planes >> (step + 1), 1 << step)
    pairs = [(2 * p + core, 2 * (p ^ bit) + core) for p in range(planes) for core, bit in enumerate(bits)]
    return lax.ppermute(value, "dp", pairs)


def gather_early(piece):
    _, steps = dp_planes()
    held = {0: piece}
    for step in range(steps - 1):
        held.update({m | 1 << step: swap_planes(value, step) for m, value in held.items()})
    held[1 << (steps - 1)] = swap_planes(piece, steps - 1)
    return held


def scatter_planes(first, second):
    held = [dict(enumerate(parts)) for parts in (first, second)]
    totals, near = [[parts.pop(0)] for parts in held], []
    _, steps = dp_planes()
    for step in reversed(range(steps)):
        bit, ready = 1 << step, []
        for parts in held:
            for m in sorted((m for m in parts if m & bit and m != bit), reverse=True):
                parts[m ^ bit] = parts[m ^ bit] + swap_planes(after(parts.pop(m), *ready), step)
                ready = [parts[m ^ bit]]
        for total, parts in zip(totals, held):
            part = swap_planes(after(parts.pop(bit), *ready), step)
            (near if step == steps - 1 else total).append(part)
    return *lax.optimization_barrier(tuple(sum(t[1:], t[0]) for t in totals)), *near


def merge(stats):
    peak = functools.reduce(jnp.maximum, [s[:, 0] for s in stats])
    total = sum(s[:, 1] * jnp.exp(s[:, 0] - peak) for s in stats)
    return jnp.stack([peak, total], axis=1)


def per_device(embeddings, comp_means, comp_variances, comp_mass):
    n = comp_means.shape[0]
    rows, width = embeddings.shape
    planes, steps = dp_planes()
    last_bit = 1 << (steps - 1)
    variances = gather_early(comp_variances)
    linear = gather_early(coefficients(comp_means, comp_variances, comp_mass))
    other = swap(embeddings, "dp", 1)
    order = sorted(linear)
    late = [q for q in range(planes) if q not in linear]
    x_high, x_low, s_high, s_low = halves(embeddings, other)
    for q in late:
        variances[q] = swap_planes(after(variances[q ^ last_bit], x_high), steps - 1)
    n_early, n_late = n * len(order), n * len(late)

    def quad_scores(group, name, cost=None):
        comps = n * len(group)
        operands = (*(vmem(variances[q]) for q in group), s_high, s_low)
        body = functools.partial(quad_kernel, n)
        return score_call(body, [(comps, 2 * rows)], [(2 * comps, width)], name, *operands, cost=cost)[0]

    quad = quad_scores(order, "early_quad")
    head = width // LANES * 2 // 3
    heads, tails = [], []
    for q in late:
        source = after(linear[q ^ last_bit], quad)
        heads.append(vmem(swap_planes(source[: head * n], steps - 1)))
        tails.append(source[head * n :])
    early, early_stats = score_call(
        functools.partial(early_kernel, n),
        [(n_early, 2 * rows), (2, 2 * rows)],
        [(2 * n_early, width)],
        "early_scores",
        *(vmem(linear[q]) for q in order),
        x_high,
        x_low,
        quad,
        cost=LIGHT,
    )
    tails = [vmem(swap_planes(after(tail, early), steps - 1)) for tail in tails]
    (part,) = score_call(
        functools.partial(head_kernel, n),
        [(n_late, 2 * rows)],
        [(2 * n_late, head * LANES)],
        "late_head",
        *heads,
        x_high,
        x_low,
        quad_scores(late, "late_quad", LIGHT),
        cost=LIGHT,
    )
    last, stats = score_call(
        functools.partial(last_kernel, n),
        [(n_late, 2 * rows), (2, 2, rows)],
        [(2 * n_late, width - head * LANES)],
        "last_scores",
        *tails,
        x_high,
        x_low,
        part,
        early_stats,
    )
    stats = merge([stats, swap(stats, "dp", 1)[::-1]])
    stats = merge([stats] + [swap(stats, "comp", q) for q in range(1, lax.axis_size("comp"))])

    *first, resp = first_moments(early, last, stats, x_high, x_low, n)
    second = second_moments(resp, s_high, s_low, n)
    place = {q: i for i, q in enumerate(order + late)}
    first, second = ([parts[place[q]] for q in range(planes)] for parts in (first, second))
    sums = scatter_planes(first, second)

    total_comps = n * lax.axis_size("dp") * lax.axis_size("comp")
    total_rows = embeddings.shape[0] * lax.axis_size("dp")
    scale = 0.6 * (total_comps / total_rows)
    return update(scale, comp_means, comp_variances, comp_mass, *sums)


def solution(mesh):
    placed = (P("dp", None), P(("comp", "dp"), None), P(("comp", "dp"), None), P(("comp", "dp")))
    return jax.shard_map(
        per_device,
        mesh=mesh,
        in_specs=placed,
        out_specs=(P(("comp", "dp"), None), P(("comp", "dp"), None), P(("comp", "dp"))),
        check_vma=False,
    )
```

```python
import functools

import jax
import jax.numpy as jnp
from jax import lax
from jax.experimental import pallas as pl
from jax.experimental.pallas import tpu as pltpu
from jax.sharding import PartitionSpec as P

F32 = jnp.float32
BF16 = jnp.bfloat16
LANES = 128
HEAVY = pl.CostEstimate(flops=10**10, bytes_accessed=10**8, transcendentals=0)
ACROSS = (((1,), (1,)), ((), ()))
WITHIN = (((1,), (0,)), ((), ()))


def params(megabytes):
    return pltpu.CompilerParams(vmem_limit_bytes=megabytes * 1024 * 1024)


def split(value):
    high = value.astype(BF16)
    return high, (value - high.astype(F32)).astype(BF16)


def diagonal(rows, columns):
    shape = (rows, columns)
    return lax.broadcasted_iota(jnp.int32, shape, 0) == lax.broadcasted_iota(jnp.int32, shape, 1)


def to_row(column, lanes):
    return jnp.sum(jnp.where(diagonal(column.shape[0], lanes), column, 0.0), axis=0, keepdims=True)


def to_column(row, rows):
    return jnp.sum(jnp.where(diagonal(rows, row.shape[1]), row, 0.0), axis=1, keepdims=True)


def coefficient_kernel(
    means_hbm, variances_hbm, mass_hbm, pack_ref, means_ref, variances_ref, mass_ref, sems
):
    sources = (variances_hbm, means_hbm, mass_hbm)
    targets = (variances_ref, means_ref, mass_ref)
    copies = [pltpu.make_async_copy(s, t, sems.at[i]) for i, (s, t) in enumerate(zip(sources, targets))]
    for copy in copies:
        copy.start()
    for copy in copies:
        copy.wait()
    n, width = means_ref.shape
    means, variances = means_ref[...], variances_ref[...]
    mean_prec = means * (1.0 / variances)
    sums = jnp.sum(jnp.log(variances) + means * mean_prec, axis=1, keepdims=True)
    offset = to_column(jnp.log(mass_ref[...]), n) - 0.5 * sums
    for c in range(width // LANES):
        pack_ref[c * n : (c + 1) * n, :] = mean_prec[:, c * LANES : (c + 1) * LANES]
    pack_ref[width // LANES * n :, :] = jnp.broadcast_to(to_row(offset, LANES), (8, LANES))


def coefficients(means, variances, mass):
    n, width = means.shape
    operands = (means, variances, mass.reshape(1, n))
    return pl.pallas_call(
        coefficient_kernel,
        in_specs=[pl.BlockSpec(memory_space=pl.ANY)] * 3,
        out_shape=jax.ShapeDtypeStruct((width // LANES * n + 8, LANES), F32),
        scratch_shapes=[
            pltpu.VMEM((n, width), F32),
            pltpu.VMEM((n, width), F32),
            pltpu.VMEM((1, n), F32),
            pltpu.SemaphoreType.DMA((3,)),
        ],
        cost_estimate=HEAVY,
        compiler_params=params(16),
        name="coefficients",
    )(*(pltpu.with_memory_space_constraint(x, pltpu.HBM) for x in operands))


def halves_kernel(own_ref, other_ref, xh_ref, xl_ref, sh_ref, sl_ref):
    def put(block):
        xh_ref[...], xl_ref[...] = split(block)
        sh_ref[...], sl_ref[...] = split(block * block)

    first = pl.program_id(0) < pl.num_programs(0) // 2

    @pl.when(first)
    def _():
        put(own_ref[...])

    @pl.when(jnp.logical_not(first))
    def _():
        put(other_ref[...])


def halves(own, other):
    rows, width = own.shape
    tile = min(256, rows)
    steps = rows // tile
    out = jax.ShapeDtypeStruct((2 * rows, width), BF16)
    return pl.pallas_call(
        halves_kernel,
        grid=(2 * steps,),
        in_specs=[
            pl.BlockSpec((tile, width), lambda i: (jnp.minimum(i, steps - 1), 0)),
            pl.BlockSpec((tile, width), lambda i: (jnp.maximum(i - steps, 0), 0)),
        ],
        out_specs=[pl.BlockSpec((tile, width), lambda i: (i, 0))] * 4,
        out_shape=[out] * 4,
        cost_estimate=HEAVY,
        compiler_params=params(16),
        name="halves",
    )(own, other)


def load_packs(packs, weights, n):
    comps, tiles = n * len(packs), weights.shape[1] // LANES
    for q, pack in enumerate(packs):
        for c in range(tiles):
            lanes = slice(c * LANES, (c + 1) * LANES)
            high, low = split(pack[c * n : (c + 1) * n, :])
            weights[q * n : (q + 1) * n, lanes] = high
            weights[comps + q * n : comps + (q + 1) * n, lanes] = low
    return jnp.concatenate([to_column(pack[tiles * n : tiles * n + 1, :], n) for pack in packs])


def load_variances(variances, weights, n):
    comps = n * len(variances)
    for q, ref in enumerate(variances):
        high, low = split(-0.5 * (1.0 / ref[...]))
        weights[q * n : (q + 1) * n, :] = high
        weights[comps + q * n : comps + (q + 1) * n, :] = low


def product(weights, high, low, dims):
    comps = weights.shape[0] // 2
    both = lax.dot_general(weights, high, dims, preferred_element_type=F32)
    rest = lax.dot_general(weights[:comps], low, dims, preferred_element_type=F32)
    return both[:comps] + (both[comps:] + rest)


def row_tiles(rows, tile=256):
    tile = min(tile, rows)
    return [slice(i, i + tile) for i in range(0, rows, tile)]


def quad_kernel(n, *refs):
    *variances, high_ref, low_ref, out_ref, weights = refs
    load_variances(variances, weights, n)
    for tile in row_tiles(high_ref.shape[0]):
        out_ref[:, tile] = product(weights[...], high_ref[tile, :], low_ref[tile, :], ACROSS)


def stats_of(scores):
    peak = jnp.max(scores, axis=0, keepdims=True)
    return peak, jnp.sum(jnp.exp(scores - peak), axis=0, keepdims=True)


def joined(one, other):
    peak = jnp.maximum(one[0], other[0])
    return peak, one[1] * jnp.exp(one[0] - peak) + other[1] * jnp.exp(other[0] - peak)


def early_kernel(n, *refs):
    *linear, high_ref, low_ref, quad_ref, out_ref, stats_ref, weights = refs
    offset = load_packs(linear, weights, n)
    for tile in row_tiles(high_ref.shape[0]):
        scores = product(weights[...], high_ref[tile, :], low_ref[tile, :], ACROSS)
        scores = quad_ref[:, tile] + scores + offset
        out_ref[:, tile] = scores
        stats_ref[0:1, tile], stats_ref[1:2, tile] = stats_of(scores)


def half_tiles(half):
    for block in range(2):
        for part in row_tiles(half):
            yield slice(block * half + part.start, block * half + part.stop), block, part


def last_kernel(n, *refs):
    *linear, xh_ref, xl_ref, quad_ref, early_ref, out_ref, stats_ref, weights = refs
    offset = load_packs(linear, weights, n)
    for tile, block, part in half_tiles(stats_ref.shape[2]):
        scores = product(weights[...], xh_ref[tile, :], xl_ref[tile, :], ACROSS)
        scores = quad_ref[:, tile] + scores + offset
        out_ref[:, tile] = scores
        early = early_ref[0:1, tile], early_ref[1:2, tile]
        peak, total = joined(stats_of(scores), early)
        stats_ref[block, 0:1, part] = peak
        stats_ref[block, 1:2, part] = total


def score_call(body, out_shape, scratch, name, *operands):
    return pl.pallas_call(
        body,
        out_shape=[jax.ShapeDtypeStruct(shape, F32) for shape in out_shape],
        scratch_shapes=[pltpu.VMEM(shape, BF16) for shape in scratch],
        cost_estimate=HEAVY,
        compiler_params=params(24),
        name=name,
    )(*operands)


def moment_tiles(resp_ref, high_ref, low_ref, packs, n):
    for c in range(0, high_ref.shape[1], 2 * LANES):
        columns = slice(c, c + 2 * LANES)
        total = product(resp_ref[...], high_ref[:, columns], low_ref[:, columns], WITHIN)
        for q, pack in enumerate(packs):
            for k in range(2):
                place = (c // LANES + k) * n
                pack[place : place + n, :] = total[q * n : (q + 1) * n, k * LANES : (k + 1) * LANES]


def first_kernel(n, early_ref, late_ref, stats_ref, high_ref, low_ref, *refs):
    *packs, resp_ref = refs
    comps = resp_ref.shape[0] // 2
    counts = jnp.zeros((comps, LANES), F32)
    for tile, block, part in half_tiles(stats_ref.shape[2]):
        peak, total = stats_ref[block, 0:1, part], stats_ref[block, 1:2, part]
        scores = jnp.concatenate([early_ref[:, tile], late_ref[:, tile]])
        resp = jnp.exp(scores - peak) * (1.0 / total)
        resp_ref[:comps, tile], resp_ref[comps:, tile] = split(resp)
        counts += sum(resp[:, c : c + LANES] for c in range(0, resp.shape[1], LANES))
    moment_tiles(resp_ref, high_ref, low_ref, packs, n)
    column = jnp.sum(counts, axis=1, keepdims=True)
    for q, pack in enumerate(packs):
        row = to_row(column[q * n : (q + 1) * n], LANES)
        pack[-8:, :] = jnp.broadcast_to(row, (8, LANES))


def first_moments(early, late, stats, high, low, n):
    rows, width = high.shape
    comps = early.shape[0] + late.shape[0]
    pack = jax.ShapeDtypeStruct((width // LANES * n + 8, LANES), F32)
    return pl.pallas_call(
        functools.partial(first_kernel, n),
        out_shape=[pack] * (comps // n) + [jax.ShapeDtypeStruct((2 * comps, rows), BF16)],
        cost_estimate=HEAVY,
        compiler_params=params(24),
        name="first_moments",
    )(early, late, stats, high, low)


def second_kernel(n, resp_ref, high_ref, low_ref, *packs):
    moment_tiles(resp_ref, high_ref, low_ref, packs, n)


def second_moments(resp, high, low, n):
    pack = jax.ShapeDtypeStruct((high.shape[1] // LANES * n, LANES), F32)
    return pl.pallas_call(
        functools.partial(second_kernel, n),
        out_shape=[pack] * (resp.shape[0] // 2 // n),
        cost_estimate=HEAVY,
        compiler_params=params(24),
        name="second_moments",
    )(resp, high, low)


def update_kernel(
    scale,
    means_ref,
    variances_ref,
    mass_ref,
    first_ref,
    second_ref,
    near_first_ref,
    near_second_ref,
    new_means_ref,
    new_variances_ref,
    new_mass_ref,
):
    n, width = means_ref.shape
    tiles = width // LANES * n
    row = first_ref[tiles : tiles + 1, :n] + near_first_ref[tiles : tiles + 1, :n]
    new_row = 0.4 * mass_ref[...] + scale * row
    new_mass_ref[...] = new_row
    inverse = 1.0 / to_column(new_row, n)
    kept = 0.4 * to_column(mass_ref[...], n)
    for c in range(width // LANES):
        lanes, tile = slice(c * LANES, (c + 1) * LANES), slice(c * n, (c + 1) * n)
        means, variances = means_ref[:, lanes], variances_ref[:, lanes]
        first = first_ref[tile, :] + near_first_ref[tile, :]
        second = second_ref[tile, :] + near_second_ref[tile, :]
        new_means = (kept * means + scale * first) * inverse
        new_means_ref[:, lanes] = new_means
        second_moment = kept * (variances + means * means) + scale * second
        new_variances_ref[:, lanes] = second_moment * inverse - new_means * new_means


def update(scale, means, variances, mass, *sums):
    n = mass.shape[0]
    block = jax.ShapeDtypeStruct(means.shape, F32)
    new_means, new_variances, new_mass = pl.pallas_call(
        functools.partial(update_kernel, scale),
        out_shape=(block, block, jax.ShapeDtypeStruct((1, n), F32)),
        cost_estimate=HEAVY,
        compiler_params=params(16),
        name="update",
    )(means, variances, mass.reshape(1, n), *sums)
    return new_means, new_variances, new_mass.reshape(n)


def swap(value, axis, bit):
    size = lax.axis_size(axis)
    return lax.ppermute(value, axis, [(i, i ^ bit) for i in range(size)])


def after(value, *others):
    return lax.optimization_barrier((value, *others))[0]


NEAR = ((0, 1), (1, 0), (2, 3), (3, 2))
MIDDLE = ((1, 2), (2, 1))
OUTWARD = ((1, 0), (2, 3))
INWARD = ((0, 1), (3, 2))


def hop(value, moves):
    return lax.ppermute(value, "dp", [(2 * a + c, 2 * b + c) for a, b in moves for c in range(2)])


def gather_line(piece, soon, ready):
    near, across = hop(piece, NEAR), hop(piece, MIDDLE)
    second = across + hop(after(across, *soon), OUTWARD)
    far = hop(after(near, *soon), MIDDLE)
    return [piece, near, second], [far + hop(after(far, *ready()), OUTWARD)]


def scatter_line(first, second):
    arrived, own, near = [], [], []
    for parts in (first, second):
        arrived.append(hop(parts[3], INWARD))
        far = hop(parts[3] + arrived[-1], MIDDLE)
        across = parts[2] + hop(after(parts[2], arrived[0]), INWARD)
        own.append(parts[0] + hop(across, MIDDLE))
        near.append(hop(parts[1] + far, NEAR))
    return *own, *near


def gather_cube(piece, soon, ready):
    planes = lax.axis_size("dp") // 2
    bit = planes // 2
    held = {0: piece}
    while bit > 1:
        held.update({q ^ bit: swap(value, "dp", 2 * bit) for q, value in held.items()})
        bit //= 2
    late = [swap(after(held[q], *ready()), "dp", 2) for q in sorted(held) if q]
    return [held[q] for q in sorted(held)] + [swap(piece, "dp", 2)], late


def scatter_cube(first, second):
    planes = len(first)
    order = [*range(0, planes, 2), *range(1, planes, 2)]
    held = [{q: part for q, part in zip(order, parts)} for parts in (first, second)]
    totals, near = [[parts.pop(0)] for parts in held], []
    bit = 1
    while bit < planes:
        for parts in held:
            for q in sorted((q for q in parts if q & bit and q != bit), reverse=True):
                parts[q ^ bit] = parts[q ^ bit] + swap(parts.pop(q), "dp", 2 * bit)
        for total, parts in zip(totals, held):
            (near if bit == 1 else total).append(swap(parts.pop(bit), "dp", 2 * bit))
        bit *= 2
    return *(sum(t[1:], t[0]) for t in totals), *near


def merge(stats):
    peak = functools.reduce(jnp.maximum, [s[:, 0] for s in stats])
    total = sum(s[:, 1] * jnp.exp(s[:, 0] - peak) for s in stats)
    return jnp.stack([peak, total], axis=1)


def per_device(embeddings, comp_means, comp_variances, comp_mass):
    n = comp_means.shape[0]
    rows, width = embeddings.shape
    planes = lax.axis_size("dp") // 2
    gather, scatter = (gather_line, scatter_line) if planes == 4 else (gather_cube, scatter_cube)
    other = swap(embeddings, "dp", 1)
    x_high, x_low, s_high, s_low = halves(embeddings, other)
    early_half, late_half = gather(comp_variances, [x_high], lambda: [])
    n_early, n_late = n * len(early_half), n * len(late_half)

    def quad_scores(group, name):
        comps = n * len(group)
        operands = (*group, s_high, s_low)
        body = functools.partial(quad_kernel, n)
        return score_call(body, [(comps, 2 * rows)], [(2 * comps, width)], name, *operands)[0]

    quad = quad_scores(early_half, "early_quad")
    early_linear, late_linear = gather(
        coefficients(comp_means, comp_variances, comp_mass), [x_high], lambda: [quad]
    )
    early, early_stats = score_call(
        functools.partial(early_kernel, n),
        [(n_early, 2 * rows), (2, 2 * rows)],
        [(2 * n_early, width)],
        "early_scores",
        *early_linear,
        x_high,
        x_low,
        quad,
    )
    last, stats = score_call(
        functools.partial(last_kernel, n),
        [(n_late, 2 * rows), (2, 2, rows)],
        [(2 * n_late, width)],
        "last_scores",
        *late_linear,
        x_high,
        x_low,
        quad_scores(late_half, "late_quad"),
        early_stats,
    )
    stats = merge([stats, swap(stats, "dp", 1)[::-1]])
    stats = merge([stats] + [swap(stats, "comp", q) for q in range(1, lax.axis_size("comp"))])

    *first, resp = first_moments(early, last, stats, x_high, x_low, n)
    second = second_moments(resp, s_high, s_low, n)
    sums = scatter(first, second)

    total_comps = n * lax.axis_size("dp") * lax.axis_size("comp")
    total_rows = embeddings.shape[0] * lax.axis_size("dp")
    scale = 0.6 * (total_comps / total_rows)
    return update(scale, comp_means, comp_variances, comp_mass, *sums)


def solution(mesh):
    placed = (P("dp", None), P(("comp", "dp"), None), P(("comp", "dp"), None), P(("comp", "dp")))
    return jax.shard_map(
        per_device,
        mesh=mesh,
        in_specs=placed,
        out_specs=(P(("comp", "dp"), None), P(("comp", "dp"), None), P(("comp", "dp"))),
        check_vma=False,
    )
```

```python
import functools

import jax
import jax.numpy as jnp
from jax import lax
from jax.experimental import pallas as pl
from jax.experimental.pallas import tpu as pltpu
from jax.sharding import PartitionSpec as P

F32 = jnp.float32
BF16 = jnp.bfloat16
LANES = 128
HEAVY = pl.CostEstimate(flops=10**10, bytes_accessed=10**8, transcendentals=0)
LIGHT = pl.CostEstimate(flops=10**8, bytes_accessed=10**6, transcendentals=0)
ACROSS = (((1,), (1,)), ((), ()))
WITHIN = (((1,), (0,)), ((), ()))


def params(megabytes):
    return pltpu.CompilerParams(vmem_limit_bytes=megabytes * 1024 * 1024)


def split(value):
    high = value.astype(BF16)
    return high, (value - high.astype(F32)).astype(BF16)


def diagonal(rows, columns):
    shape = (rows, columns)
    return lax.broadcasted_iota(jnp.int32, shape, 0) == lax.broadcasted_iota(jnp.int32, shape, 1)


def to_row(column, lanes):
    return jnp.sum(jnp.where(diagonal(column.shape[0], lanes), column, 0.0), axis=0, keepdims=True)


def to_column(row, rows):
    return jnp.sum(jnp.where(diagonal(rows, row.shape[1]), row, 0.0), axis=1, keepdims=True)


def coefficient_kernel(
    means_hbm, variances_hbm, mass_hbm, pack_ref, means_ref, variances_ref, mass_ref, sems
):
    sources = (variances_hbm, means_hbm, mass_hbm)
    targets = (variances_ref, means_ref, mass_ref)
    copies = [pltpu.make_async_copy(s, t, sems.at[i]) for i, (s, t) in enumerate(zip(sources, targets))]
    for copy in copies:
        copy.start()
    for copy in copies:
        copy.wait()
    n, width = means_ref.shape
    means, variances = means_ref[...], variances_ref[...]
    mean_prec = means * (1.0 / variances)
    sums = jnp.sum(jnp.log(variances) + means * mean_prec, axis=1, keepdims=True)
    offset = to_column(jnp.log(mass_ref[...]), n) - 0.5 * sums
    for c in range(width // LANES):
        pack_ref[c * n : (c + 1) * n, :] = mean_prec[:, c * LANES : (c + 1) * LANES]
    pack_ref[width // LANES * n :, :] = jnp.broadcast_to(to_row(offset, LANES), (8, LANES))


def coefficients(means, variances, mass):
    n, width = means.shape
    operands = (means, variances, mass.reshape(1, n))
    return pl.pallas_call(
        coefficient_kernel,
        in_specs=[pl.BlockSpec(memory_space=pl.ANY)] * 3,
        out_shape=jax.ShapeDtypeStruct((width // LANES * n + 8, LANES), F32),
        scratch_shapes=[
            pltpu.VMEM((n, width), F32),
            pltpu.VMEM((n, width), F32),
            pltpu.VMEM((1, n), F32),
            pltpu.SemaphoreType.DMA((3,)),
        ],
        cost_estimate=HEAVY,
        compiler_params=params(16),
        name="coefficients",
    )(*(pltpu.with_memory_space_constraint(x, pltpu.HBM) for x in operands))


def halves_kernel(own_ref, other_ref, xh_ref, xl_ref, sh_ref, sl_ref):
    def put(block):
        xh_ref[...], xl_ref[...] = split(block)
        sh_ref[...], sl_ref[...] = split(block * block)

    first = pl.program_id(0) < pl.num_programs(0) // 2

    @pl.when(first)
    def _():
        put(own_ref[...])

    @pl.when(jnp.logical_not(first))
    def _():
        put(other_ref[...])


def halves(own, other):
    rows, width = own.shape
    tile = min(256, rows)
    steps = rows // tile
    out = jax.ShapeDtypeStruct((2 * rows, width), BF16)
    return pl.pallas_call(
        halves_kernel,
        grid=(2 * steps,),
        in_specs=[
            pl.BlockSpec((tile, width), lambda i: (jnp.minimum(i, steps - 1), 0)),
            pl.BlockSpec((tile, width), lambda i: (jnp.maximum(i - steps, 0), 0)),
        ],
        out_specs=[pl.BlockSpec((tile, width), lambda i: (i, 0))] * 4,
        out_shape=[out] * 4,
        cost_estimate=HEAVY,
        compiler_params=params(16),
        name="halves",
    )(own, other)


def load_packs(packs, weights, n):
    comps, tiles = n * len(packs), weights.shape[1] // LANES
    for q, pack in enumerate(packs):
        for c in range(tiles):
            lanes = slice(c * LANES, (c + 1) * LANES)
            high, low = split(pack[c * n : (c + 1) * n, :])
            weights[q * n : (q + 1) * n, lanes] = high
            weights[comps + q * n : comps + (q + 1) * n, lanes] = low
    if packs[0].shape[0] == tiles * n:
        return None
    return jnp.concatenate([to_column(pack[tiles * n : tiles * n + 1, :], n) for pack in packs])


def load_variances(variances, weights, n):
    comps = n * len(variances)
    for q, ref in enumerate(variances):
        high, low = split(-0.5 * (1.0 / ref[...]))
        weights[q * n : (q + 1) * n, :] = high
        weights[comps + q * n : comps + (q + 1) * n, :] = low


def product(weights, high, low, dims):
    comps = weights.shape[0] // 2
    both = lax.dot_general(weights, high, dims, preferred_element_type=F32)
    rest = lax.dot_general(weights[:comps], low, dims, preferred_element_type=F32)
    return both[:comps] + (both[comps:] + rest)


def row_tiles(rows, tile=256):
    tile = min(tile, rows)
    return [slice(i, i + tile) for i in range(0, rows, tile)]


def quad_kernel(n, *refs):
    *variances, high_ref, low_ref, out_ref, weights = refs
    load_variances(variances, weights, n)
    for tile in row_tiles(high_ref.shape[0]):
        out_ref[:, tile] = product(weights[...], high_ref[tile, :], low_ref[tile, :], ACROSS)


def stats_of(scores):
    peak = jnp.max(scores, axis=0, keepdims=True)
    return peak, jnp.sum(jnp.exp(scores - peak), axis=0, keepdims=True)


def joined(one, other):
    peak = jnp.maximum(one[0], other[0])
    return peak, one[1] * jnp.exp(one[0] - peak) + other[1] * jnp.exp(other[0] - peak)


def early_kernel(n, *refs):
    *linear, high_ref, low_ref, quad_ref, out_ref, stats_ref, weights = refs
    offset = load_packs(linear, weights, n)
    for tile in row_tiles(high_ref.shape[0]):
        scores = product(weights[...], high_ref[tile, :], low_ref[tile, :], ACROSS)
        scores = quad_ref[:, tile] + scores + offset
        out_ref[:, tile] = scores
        stats_ref[0:1, tile], stats_ref[1:2, tile] = stats_of(scores)


def half_tiles(half):
    for block in range(2):
        for part in row_tiles(half):
            yield slice(block * half + part.start, block * half + part.stop), block, part


def head_kernel(n, *refs):
    *linear, high_ref, low_ref, quad_ref, out_ref, weights = refs
    load_packs(linear, weights, n)
    columns = slice(0, weights.shape[1])
    for tile in row_tiles(high_ref.shape[0]):
        scores = product(weights[...], high_ref[tile, columns], low_ref[tile, columns], ACROSS)
        out_ref[:, tile] = quad_ref[:, tile] + scores


def last_kernel(n, *refs):
    *linear, high_ref, low_ref, quad_ref, early_ref, out_ref, stats_ref, weights = refs
    offset = load_packs(linear, weights, n)
    columns = slice(high_ref.shape[1] - weights.shape[1], high_ref.shape[1])
    for tile, block, part in half_tiles(stats_ref.shape[2]):
        scores = product(weights[...], high_ref[tile, columns], low_ref[tile, columns], ACROSS)
        scores = quad_ref[:, tile] + scores + offset
        out_ref[:, tile] = scores
        early = early_ref[0:1, tile], early_ref[1:2, tile]
        peak, total = joined(stats_of(scores), early)
        stats_ref[block, 0:1, part] = peak
        stats_ref[block, 1:2, part] = total


def score_call(body, out_shape, scratch, name, *operands, cost=None):
    return pl.pallas_call(
        body,
        out_shape=[jax.ShapeDtypeStruct(shape, F32) for shape in out_shape],
        scratch_shapes=[pltpu.VMEM(shape, BF16) for shape in scratch],
        cost_estimate=cost or HEAVY,
        compiler_params=params(24),
        name=name,
    )(*operands)


def moment_tiles(resp_ref, high_ref, low_ref, packs, n):
    for c in range(0, high_ref.shape[1], 2 * LANES):
        columns = slice(c, c + 2 * LANES)
        total = product(resp_ref[...], high_ref[:, columns], low_ref[:, columns], WITHIN)
        for q, pack in enumerate(packs):
            for k in range(2):
                place = (c // LANES + k) * n
                pack[place : place + n, :] = total[q * n : (q + 1) * n, k * LANES : (k + 1) * LANES]


def first_kernel(n, early_ref, late_ref, stats_ref, high_ref, low_ref, *refs):
    *packs, resp_ref = refs
    comps = resp_ref.shape[0] // 2
    counts = jnp.zeros((comps, LANES), F32)
    for tile, block, part in half_tiles(stats_ref.shape[2]):
        peak, total = stats_ref[block, 0:1, part], stats_ref[block, 1:2, part]
        scores = jnp.concatenate([early_ref[:, tile], late_ref[:, tile]])
        resp = jnp.exp(scores - peak) * (1.0 / total)
        resp_ref[:comps, tile], resp_ref[comps:, tile] = split(resp)
        counts += sum(resp[:, c : c + LANES] for c in range(0, resp.shape[1], LANES))
    moment_tiles(resp_ref, high_ref, low_ref, packs, n)
    column = jnp.sum(counts, axis=1, keepdims=True)
    for q, pack in enumerate(packs):
        row = to_row(column[q * n : (q + 1) * n], LANES)
        pack[-8:, :] = jnp.broadcast_to(row, (8, LANES))


def first_moments(early, late, stats, high, low, n):
    rows, width = high.shape
    comps = early.shape[0] + late.shape[0]
    pack = jax.ShapeDtypeStruct((width // LANES * n + 8, LANES), F32)
    return pl.pallas_call(
        functools.partial(first_kernel, n),
        out_shape=[pack] * (comps // n) + [jax.ShapeDtypeStruct((2 * comps, rows), BF16)],
        cost_estimate=HEAVY,
        compiler_params=params(24),
        name="first_moments",
    )(early, late, stats, high, low)


def second_kernel(n, resp_ref, high_ref, low_ref, *packs):
    moment_tiles(resp_ref, high_ref, low_ref, packs, n)


def second_moments(resp, high, low, n):
    pack = jax.ShapeDtypeStruct((high.shape[1] // LANES * n, LANES), F32)
    return pl.pallas_call(
        functools.partial(second_kernel, n),
        out_shape=[pack] * (resp.shape[0] // 2 // n),
        cost_estimate=HEAVY,
        compiler_params=params(24),
        name="second_moments",
    )(resp, high, low)


def update_kernel(
    scale,
    means_ref,
    variances_ref,
    mass_ref,
    first_ref,
    second_ref,
    near_first_ref,
    near_second_ref,
    new_means_ref,
    new_variances_ref,
    new_mass_ref,
):
    n, width = means_ref.shape
    tiles = width // LANES * n
    row = first_ref[tiles : tiles + 1, :n] + near_first_ref[tiles : tiles + 1, :n]
    new_row = 0.4 * mass_ref[...] + scale * row
    new_mass_ref[...] = new_row
    inverse = 1.0 / to_column(new_row, n)
    kept = 0.4 * to_column(mass_ref[...], n)
    for c in range(width // LANES):
        lanes, tile = slice(c * LANES, (c + 1) * LANES), slice(c * n, (c + 1) * n)
        means, variances = means_ref[:, lanes], variances_ref[:, lanes]
        first = first_ref[tile, :] + near_first_ref[tile, :]
        second = second_ref[tile, :] + near_second_ref[tile, :]
        new_means = (kept * means + scale * first) * inverse
        new_means_ref[:, lanes] = new_means
        second_moment = kept * (variances + means * means) + scale * second
        new_variances_ref[:, lanes] = second_moment * inverse - new_means * new_means


def update(scale, means, variances, mass, *sums):
    n = mass.shape[0]
    block = jax.ShapeDtypeStruct(means.shape, F32)
    new_means, new_variances, new_mass = pl.pallas_call(
        functools.partial(update_kernel, scale),
        out_shape=(block, block, jax.ShapeDtypeStruct((1, n), F32)),
        cost_estimate=HEAVY,
        compiler_params=params(16),
        name="update",
    )(means, variances, mass.reshape(1, n), *sums)
    return new_means, new_variances, new_mass.reshape(n)


def swap(value, axis, bit):
    size = lax.axis_size(axis)
    return lax.ppermute(value, axis, [(i, i ^ bit) for i in range(size)])


def vmem(value):
    return pltpu.with_memory_space_constraint(value, pltpu.VMEM)


def after(value, *others):
    return lax.optimization_barrier((value, *others))[0]


def gather_early(piece):
    bit = lax.axis_size("dp") // 4
    held = {0: piece}
    while bit > 1:
        held.update({q ^ bit: swap(value, "dp", 2 * bit) for q, value in held.items()})
        bit //= 2
    held[1] = swap(piece, "dp", 2)
    return held


def scatter_planes(first, second):
    held = [dict(enumerate(parts)) for parts in (first, second)]
    totals, near = [[parts.pop(0)] for parts in held], []
    planes, bit = len(first), 1
    while bit < planes:
        ready = []
        for parts in held:
            for q in sorted((q for q in parts if q & bit and q != bit), reverse=True):
                parts[q ^ bit] = parts[q ^ bit] + swap(after(parts.pop(q), *ready), "dp", 2 * bit)
                ready = [parts[q ^ bit]]
        for total, parts in zip(totals, held):
            part = swap(after(parts.pop(bit), *ready), "dp", 2 * bit)
            (near if bit == 1 else total).append(part)
        bit *= 2
    return *lax.optimization_barrier(tuple(sum(t[1:], t[0]) for t in totals)), *near


def merge(stats):
    peak = functools.reduce(jnp.maximum, [s[:, 0] for s in stats])
    total = sum(s[:, 1] * jnp.exp(s[:, 0] - peak) for s in stats)
    return jnp.stack([peak, total], axis=1)


def per_device(embeddings, comp_means, comp_variances, comp_mass):
    n = comp_means.shape[0]
    rows, width = embeddings.shape
    planes = lax.axis_size("dp") // 2
    variances = gather_early(comp_variances)
    linear = gather_early(coefficients(comp_means, comp_variances, comp_mass))
    other = swap(embeddings, "dp", 1)
    order = sorted(linear)
    late = [q for q in range(planes) if q not in linear]
    x_high, x_low, s_high, s_low = halves(embeddings, other)
    for q in late:
        variances[q] = swap(after(variances[q ^ 1], x_high), "dp", 2)
    n_early, n_late = n * len(order), n * len(late)

    def quad_scores(group, name, cost=None):
        comps = n * len(group)
        operands = (*(vmem(variances[q]) for q in group), s_high, s_low)
        body = functools.partial(quad_kernel, n)
        return score_call(body, [(comps, 2 * rows)], [(2 * comps, width)], name, *operands, cost=cost)[0]

    quad = quad_scores(order, "early_quad")
    head = width // LANES * 2 // 3
    heads, tails = [], []
    for q in late:
        source = after(linear[q ^ 1], quad)
        heads.append(vmem(swap(source[: head * n], "dp", 2)))
        tails.append(source[head * n :])
    early, early_stats = score_call(
        functools.partial(early_kernel, n),
        [(n_early, 2 * rows), (2, 2 * rows)],
        [(2 * n_early, width)],
        "early_scores",
        *(vmem(linear[q]) for q in order),
        x_high,
        x_low,
        quad,
        cost=LIGHT,
    )
    tails = [vmem(swap(after(tail, early), "dp", 2)) for tail in tails]
    (part,) = score_call(
        functools.partial(head_kernel, n),
        [(n_late, 2 * rows)],
        [(2 * n_late, head * LANES)],
        "late_head",
        *heads,
        x_high,
        x_low,
        quad_scores(late, "late_quad", LIGHT),
        cost=LIGHT,
    )
    last, stats = score_call(
        functools.partial(last_kernel, n),
        [(n_late, 2 * rows), (2, 2, rows)],
        [(2 * n_late, width - head * LANES)],
        "last_scores",
        *tails,
        x_high,
        x_low,
        part,
        early_stats,
    )
    stats = merge([stats, swap(stats, "dp", 1)[::-1]])
    stats = merge([stats] + [swap(stats, "comp", q) for q in range(1, lax.axis_size("comp"))])

    *first, resp = first_moments(early, last, stats, x_high, x_low, n)
    second = second_moments(resp, s_high, s_low, n)
    place = {q: i for i, q in enumerate(order + late)}
    first, second = ([parts[place[q]] for q in range(planes)] for parts in (first, second))
    sums = scatter_planes(first, second)

    total_comps = n * lax.axis_size("dp") * lax.axis_size("comp")
    total_rows = embeddings.shape[0] * lax.axis_size("dp")
    scale = 0.6 * (total_comps / total_rows)
    return update(scale, comp_means, comp_variances, comp_mass, *sums)


def solution(mesh):
    placed = (P("dp", None), P(("comp", "dp"), None), P(("comp", "dp"), None), P(("comp", "dp")))
    return jax.shard_map(
        per_device,
        mesh=mesh,
        in_specs=placed,
        out_specs=(P(("comp", "dp"), None), P(("comp", "dp"), None), P(("comp", "dp"))),
        check_vma=False,
    )
```

```python
import functools

import jax
import jax.numpy as jnp
from jax import lax
from jax.experimental import pallas as pl
from jax.experimental.pallas import tpu as pltpu
from jax.sharding import PartitionSpec as P

F32 = jnp.float32
BF16 = jnp.bfloat16
LANES = 128
HEAVY = pl.CostEstimate(flops=10**10, bytes_accessed=10**8, transcendentals=0)
LIGHT = pl.CostEstimate(flops=10**8, bytes_accessed=10**6, transcendentals=0)
ACROSS = (((1,), (1,)), ((), ()))
WITHIN = (((1,), (0,)), ((), ()))


def params(megabytes):
    return pltpu.CompilerParams(vmem_limit_bytes=megabytes * 1024 * 1024)


def split(value):
    high = value.astype(BF16)
    return high, (value - high.astype(F32)).astype(BF16)


def diagonal(rows, columns):
    shape = (rows, columns)
    return lax.broadcasted_iota(jnp.int32, shape, 0) == lax.broadcasted_iota(jnp.int32, shape, 1)


def to_row(column, lanes):
    return jnp.sum(jnp.where(diagonal(column.shape[0], lanes), column, 0.0), axis=0, keepdims=True)


def to_column(row, rows):
    return jnp.sum(jnp.where(diagonal(rows, row.shape[1]), row, 0.0), axis=1, keepdims=True)


def coefficient_kernel(
    means_hbm, variances_hbm, mass_hbm, pack_ref, means_ref, variances_ref, mass_ref, sems
):
    sources = (variances_hbm, means_hbm, mass_hbm)
    targets = (variances_ref, means_ref, mass_ref)
    copies = [pltpu.make_async_copy(s, t, sems.at[i]) for i, (s, t) in enumerate(zip(sources, targets))]
    for copy in copies:
        copy.start()
    for copy in copies:
        copy.wait()
    n, width = means_ref.shape
    means, variances = means_ref[...], variances_ref[...]
    mean_prec = means * (1.0 / variances)
    sums = jnp.sum(jnp.log(variances) + means * mean_prec, axis=1, keepdims=True)
    offset = to_column(jnp.log(mass_ref[...]), n) - 0.5 * sums
    for c in range(width // LANES):
        pack_ref[c * n : (c + 1) * n, :] = mean_prec[:, c * LANES : (c + 1) * LANES]
    pack_ref[width // LANES * n :, :] = jnp.broadcast_to(to_row(offset, LANES), (8, LANES))


def coefficients(means, variances, mass):
    n, width = means.shape
    operands = (means, variances, mass.reshape(1, n))
    return pl.pallas_call(
        coefficient_kernel,
        in_specs=[pl.BlockSpec(memory_space=pl.ANY)] * 3,
        out_shape=jax.ShapeDtypeStruct((width // LANES * n + 8, LANES), F32),
        scratch_shapes=[
            pltpu.VMEM((n, width), F32),
            pltpu.VMEM((n, width), F32),
            pltpu.VMEM((1, n), F32),
            pltpu.SemaphoreType.DMA((3,)),
        ],
        cost_estimate=HEAVY,
        compiler_params=params(16),
        name="coefficients",
    )(*(pltpu.with_memory_space_constraint(x, pltpu.HBM) for x in operands))


def halves_kernel(own_ref, other_ref, xh_ref, xl_ref, sh_ref, sl_ref):
    def put(block):
        xh_ref[...], xl_ref[...] = split(block)
        sh_ref[...], sl_ref[...] = split(block * block)

    first = pl.program_id(0) < pl.num_programs(0) // 2

    @pl.when(first)
    def _():
        put(own_ref[...])

    @pl.when(jnp.logical_not(first))
    def _():
        put(other_ref[...])


def halves(own, other):
    rows, width = own.shape
    tile = min(256, rows)
    steps = rows // tile
    out = jax.ShapeDtypeStruct((2 * rows, width), BF16)
    return pl.pallas_call(
        halves_kernel,
        grid=(2 * steps,),
        in_specs=[
            pl.BlockSpec((tile, width), lambda i: (jnp.minimum(i, steps - 1), 0)),
            pl.BlockSpec((tile, width), lambda i: (jnp.maximum(i - steps, 0), 0)),
        ],
        out_specs=[pl.BlockSpec((tile, width), lambda i: (i, 0))] * 4,
        out_shape=[out] * 4,
        cost_estimate=HEAVY,
        compiler_params=params(16),
        name="halves",
    )(own, other)


def load_packs(packs, weights, n):
    comps, tiles = n * len(packs), weights.shape[1] // LANES
    for q, pack in enumerate(packs):
        for c in range(tiles):
            lanes = slice(c * LANES, (c + 1) * LANES)
            high, low = split(pack[c * n : (c + 1) * n, :])
            weights[q * n : (q + 1) * n, lanes] = high
            weights[comps + q * n : comps + (q + 1) * n, lanes] = low
    if packs[0].shape[0] == tiles * n:
        return None
    return jnp.concatenate([to_column(pack[tiles * n : tiles * n + 1, :], n) for pack in packs])


def load_variances(variances, weights, n):
    comps = n * len(variances)
    for q, ref in enumerate(variances):
        high, low = split(-0.5 * (1.0 / ref[...]))
        weights[q * n : (q + 1) * n, :] = high
        weights[comps + q * n : comps + (q + 1) * n, :] = low


def product(weights, high, low, dims):
    comps = weights.shape[0] // 2
    both = lax.dot_general(weights, high, dims, preferred_element_type=F32)
    rest = lax.dot_general(weights[:comps], low, dims, preferred_element_type=F32)
    return both[:comps] + (both[comps:] + rest)


def row_tiles(rows, tile=256):
    tile = min(tile, rows)
    return [slice(i, i + tile) for i in range(0, rows, tile)]


def quad_kernel(n, *refs):
    *variances, high_ref, low_ref, out_ref, weights = refs
    load_variances(variances, weights, n)
    for tile in row_tiles(high_ref.shape[0]):
        out_ref[:, tile] = product(weights[...], high_ref[tile, :], low_ref[tile, :], ACROSS)


def stats_of(scores):
    peak = jnp.max(scores, axis=0, keepdims=True)
    return peak, jnp.sum(jnp.exp(scores - peak), axis=0, keepdims=True)


def joined(one, other):
    peak = jnp.maximum(one[0], other[0])
    return peak, one[1] * jnp.exp(one[0] - peak) + other[1] * jnp.exp(other[0] - peak)


def early_kernel(n, *refs):
    *linear, high_ref, low_ref, quad_ref, out_ref, stats_ref, weights = refs
    offset = load_packs(linear, weights, n)
    for tile in row_tiles(high_ref.shape[0]):
        scores = product(weights[...], high_ref[tile, :], low_ref[tile, :], ACROSS)
        scores = quad_ref[:, tile] + scores + offset
        out_ref[:, tile] = scores
        stats_ref[0:1, tile], stats_ref[1:2, tile] = stats_of(scores)


def half_tiles(half):
    for block in range(2):
        for part in row_tiles(half):
            yield slice(block * half + part.start, block * half + part.stop), block, part


def head_kernel(n, *refs):
    *linear, high_ref, low_ref, quad_ref, out_ref, weights = refs
    load_packs(linear, weights, n)
    columns = slice(0, weights.shape[1])
    for tile in row_tiles(high_ref.shape[0]):
        scores = product(weights[...], high_ref[tile, columns], low_ref[tile, columns], ACROSS)
        out_ref[:, tile] = quad_ref[:, tile] + scores


def last_kernel(n, *refs):
    *linear, high_ref, low_ref, quad_ref, early_ref, out_ref, stats_ref, weights = refs
    offset = load_packs(linear, weights, n)
    columns = slice(high_ref.shape[1] - weights.shape[1], high_ref.shape[1])
    for tile, block, part in half_tiles(stats_ref.shape[2]):
        scores = product(weights[...], high_ref[tile, columns], low_ref[tile, columns], ACROSS)
        scores = quad_ref[:, tile] + scores + offset
        out_ref[:, tile] = scores
        early = early_ref[0:1, tile], early_ref[1:2, tile]
        peak, total = joined(stats_of(scores), early)
        stats_ref[block, 0:1, part] = peak
        stats_ref[block, 1:2, part] = total


def score_call(body, out_shape, scratch, name, *operands, cost=None):
    return pl.pallas_call(
        body,
        out_shape=[jax.ShapeDtypeStruct(shape, F32) for shape in out_shape],
        scratch_shapes=[pltpu.VMEM(shape, BF16) for shape in scratch],
        cost_estimate=cost or HEAVY,
        compiler_params=params(24),
        name=name,
    )(*operands)


def moment_tiles(resp_ref, high_ref, low_ref, packs, n):
    for c in range(0, high_ref.shape[1], 2 * LANES):
        columns = slice(c, c + 2 * LANES)
        total = product(resp_ref[...], high_ref[:, columns], low_ref[:, columns], WITHIN)
        for q, pack in enumerate(packs):
            for k in range(2):
                place = (c // LANES + k) * n
                pack[place : place + n, :] = total[q * n : (q + 1) * n, k * LANES : (k + 1) * LANES]


def first_kernel(n, early_ref, late_ref, stats_ref, high_ref, low_ref, *refs):
    *packs, resp_ref = refs
    comps = resp_ref.shape[0] // 2
    counts = jnp.zeros((comps, LANES), F32)
    for tile, block, part in half_tiles(stats_ref.shape[2]):
        peak, total = stats_ref[block, 0:1, part], stats_ref[block, 1:2, part]
        scores = jnp.concatenate([early_ref[:, tile], late_ref[:, tile]])
        resp = jnp.exp(scores - peak) * (1.0 / total)
        resp_ref[:comps, tile], resp_ref[comps:, tile] = split(resp)
        counts += sum(resp[:, c : c + LANES] for c in range(0, resp.shape[1], LANES))
    moment_tiles(resp_ref, high_ref, low_ref, packs, n)
    column = jnp.sum(counts, axis=1, keepdims=True)
    for q, pack in enumerate(packs):
        row = to_row(column[q * n : (q + 1) * n], LANES)
        pack[-8:, :] = jnp.broadcast_to(row, (8, LANES))


def first_moments(early, late, stats, high, low, n):
    rows, width = high.shape
    comps = early.shape[0] + late.shape[0]
    pack = jax.ShapeDtypeStruct((width // LANES * n + 8, LANES), F32)
    return pl.pallas_call(
        functools.partial(first_kernel, n),
        out_shape=[pack] * (comps // n) + [jax.ShapeDtypeStruct((2 * comps, rows), BF16)],
        cost_estimate=HEAVY,
        compiler_params=params(24),
        name="first_moments",
    )(early, late, stats, high, low)


def second_kernel(n, resp_ref, high_ref, low_ref, *packs):
    moment_tiles(resp_ref, high_ref, low_ref, packs, n)


def second_moments(resp, high, low, n):
    pack = jax.ShapeDtypeStruct((high.shape[1] // LANES * n, LANES), F32)
    return pl.pallas_call(
        functools.partial(second_kernel, n),
        out_shape=[pack] * (resp.shape[0] // 2 // n),
        cost_estimate=HEAVY,
        compiler_params=params(24),
        name="second_moments",
    )(resp, high, low)


def update_kernel(
    scale,
    means_ref,
    variances_ref,
    mass_ref,
    first_ref,
    second_ref,
    near_first_ref,
    near_second_ref,
    new_means_ref,
    new_variances_ref,
    new_mass_ref,
):
    n, width = means_ref.shape
    tiles = width // LANES * n
    row = first_ref[tiles : tiles + 1, :n] + near_first_ref[tiles : tiles + 1, :n]
    new_row = 0.4 * mass_ref[...] + scale * row
    new_mass_ref[...] = new_row
    inverse = 1.0 / to_column(new_row, n)
    kept = 0.4 * to_column(mass_ref[...], n)
    for c in range(width // LANES):
        lanes, tile = slice(c * LANES, (c + 1) * LANES), slice(c * n, (c + 1) * n)
        means, variances = means_ref[:, lanes], variances_ref[:, lanes]
        first = first_ref[tile, :] + near_first_ref[tile, :]
        second = second_ref[tile, :] + near_second_ref[tile, :]
        new_means = (kept * means + scale * first) * inverse
        new_means_ref[:, lanes] = new_means
        second_moment = kept * (variances + means * means) + scale * second
        new_variances_ref[:, lanes] = second_moment * inverse - new_means * new_means


def update(scale, means, variances, mass, *sums):
    n = mass.shape[0]
    block = jax.ShapeDtypeStruct(means.shape, F32)
    new_means, new_variances, new_mass = pl.pallas_call(
        functools.partial(update_kernel, scale),
        out_shape=(block, block, jax.ShapeDtypeStruct((1, n), F32)),
        cost_estimate=HEAVY,
        compiler_params=params(16),
        name="update",
    )(means, variances, mass.reshape(1, n), *sums)
    return new_means, new_variances, new_mass.reshape(n)


def swap(value, axis, bit):
    size = lax.axis_size(axis)
    return lax.ppermute(value, axis, [(i, i ^ bit) for i in range(size)])


def vmem(value):
    return pltpu.with_memory_space_constraint(value, pltpu.VMEM)


def after(value, *others):
    return lax.optimization_barrier((value, *others))[0]


def gather_early(piece):
    bit = lax.axis_size("dp") // 4
    held = {0: piece}
    while bit > 1:
        held.update({q ^ bit: swap(value, "dp", 2 * bit) for q, value in held.items()})
        bit //= 2
    held[1] = swap(piece, "dp", 2)
    return held


def scatter_planes(first, second):
    held = [dict(enumerate(parts)) for parts in (first, second)]
    totals, near = [[parts.pop(0)] for parts in held], []
    planes, bit = len(first), 1
    while bit < planes:
        ready = []
        for parts in held:
            for q in sorted((q for q in parts if q & bit and q != bit), reverse=True):
                parts[q ^ bit] = parts[q ^ bit] + swap(after(parts.pop(q), *ready), "dp", 2 * bit)
                ready = [parts[q ^ bit]]
        for total, parts in zip(totals, held):
            part = swap(after(parts.pop(bit), *ready), "dp", 2 * bit)
            (near if bit == 1 else total).append(part)
        bit *= 2
    one, other, *near = lax.optimization_barrier((sum(totals[0][1:], totals[0][0]), totals[1][0], *near))
    return one, sum(totals[1][1:], other), *near


def merge(stats):
    peak = functools.reduce(jnp.maximum, [s[:, 0] for s in stats])
    total = sum(s[:, 1] * jnp.exp(s[:, 0] - peak) for s in stats)
    return jnp.stack([peak, total], axis=1)


def per_device(embeddings, comp_means, comp_variances, comp_mass):
    n = comp_means.shape[0]
    rows, width = embeddings.shape
    planes = lax.axis_size("dp") // 2
    variances = gather_early(comp_variances)
    linear = gather_early(coefficients(comp_means, comp_variances, comp_mass))
    other = swap(embeddings, "dp", 1)
    order = sorted(linear)
    late = [q for q in range(planes) if q not in linear]
    x_high, x_low, s_high, s_low = halves(embeddings, other)
    for q in late:
        variances[q] = swap(after(variances[q ^ 1], x_high), "dp", 2)
    n_early, n_late = n * len(order), n * len(late)

    def quad_scores(group, name, cost=None):
        comps = n * len(group)
        operands = (*(vmem(variances[q]) for q in group), s_high, s_low)
        body = functools.partial(quad_kernel, n)
        return score_call(body, [(comps, 2 * rows)], [(2 * comps, width)], name, *operands, cost=cost)[0]

    quad = quad_scores(order, "early_quad")
    head = width // LANES * 2 // 3
    heads, tails = [], []
    for q in late:
        source = after(linear[q ^ 1], quad)
        heads.append(vmem(swap(source[: head * n], "dp", 2)))
        tails.append(source[head * n :])
    early, early_stats = score_call(
        functools.partial(early_kernel, n),
        [(n_early, 2 * rows), (2, 2 * rows)],
        [(2 * n_early, width)],
        "early_scores",
        *(vmem(linear[q]) for q in order),
        x_high,
        x_low,
        quad,
        cost=LIGHT,
    )
    tails = [vmem(swap(after(tail, early), "dp", 2)) for tail in tails]
    (part,) = score_call(
        functools.partial(head_kernel, n),
        [(n_late, 2 * rows)],
        [(2 * n_late, head * LANES)],
        "late_head",
        *heads,
        x_high,
        x_low,
        quad_scores(late, "late_quad", LIGHT),
        cost=LIGHT,
    )
    last, stats = score_call(
        functools.partial(last_kernel, n),
        [(n_late, 2 * rows), (2, 2, rows)],
        [(2 * n_late, width - head * LANES)],
        "last_scores",
        *tails,
        x_high,
        x_low,
        part,
        early_stats,
    )
    stats = merge([stats, swap(stats, "dp", 1)[::-1]])
    stats = merge([stats] + [swap(stats, "comp", q) for q in range(1, lax.axis_size("comp"))])

    *first, resp = first_moments(early, last, stats, x_high, x_low, n)
    second = second_moments(resp, s_high, s_low, n)
    place = {q: i for i, q in enumerate(order + late)}
    first, second = ([parts[place[q]] for q in range(planes)] for parts in (first, second))
    sums = scatter_planes(first, second)

    total_comps = n * lax.axis_size("dp") * lax.axis_size("comp")
    total_rows = embeddings.shape[0] * lax.axis_size("dp")
    scale = 0.6 * (total_comps / total_rows)
    return update(scale, comp_means, comp_variances, comp_mass, *sums)


def solution(mesh):
    placed = (P("dp", None), P(("comp", "dp"), None), P(("comp", "dp"), None), P(("comp", "dp")))
    return jax.shard_map(
        per_device,
        mesh=mesh,
        in_specs=placed,
        out_specs=(P(("comp", "dp"), None), P(("comp", "dp"), None), P(("comp", "dp"))),
        check_vma=False,
    )
```

```python
import functools

import jax
import jax.numpy as jnp
from jax import lax
from jax.experimental import pallas as pl
from jax.experimental.pallas import tpu as pltpu
from jax.sharding import PartitionSpec as P

F32 = jnp.float32
BF16 = jnp.bfloat16
LANES = 128
HEAVY = pl.CostEstimate(flops=10**10, bytes_accessed=10**8, transcendentals=0)
LIGHT = pl.CostEstimate(flops=10**8, bytes_accessed=10**6, transcendentals=0)
ACROSS = (((1,), (1,)), ((), ()))
WITHIN = (((1,), (0,)), ((), ()))


def params(megabytes):
    return pltpu.CompilerParams(vmem_limit_bytes=megabytes * 1024 * 1024)


def split(value):
    high = value.astype(BF16)
    return high, (value - high.astype(F32)).astype(BF16)


def diagonal(rows, columns):
    shape = (rows, columns)
    return lax.broadcasted_iota(jnp.int32, shape, 0) == lax.broadcasted_iota(jnp.int32, shape, 1)


def to_row(column, lanes):
    return jnp.sum(jnp.where(diagonal(column.shape[0], lanes), column, 0.0), axis=0, keepdims=True)


def to_column(row, rows):
    return jnp.sum(jnp.where(diagonal(rows, row.shape[1]), row, 0.0), axis=1, keepdims=True)


def coefficient_kernel(
    means_hbm, variances_hbm, mass_hbm, pack_ref, means_ref, variances_ref, mass_ref, sems
):
    sources = (variances_hbm, means_hbm, mass_hbm)
    targets = (variances_ref, means_ref, mass_ref)
    copies = [pltpu.make_async_copy(s, t, sems.at[i]) for i, (s, t) in enumerate(zip(sources, targets))]
    for copy in copies:
        copy.start()
    for copy in copies:
        copy.wait()
    n, width = means_ref.shape
    means, variances = means_ref[...], variances_ref[...]
    mean_prec = means * (1.0 / variances)
    sums = jnp.sum(jnp.log(variances) + means * mean_prec, axis=1, keepdims=True)
    offset = to_column(jnp.log(mass_ref[...]), n) - 0.5 * sums
    for c in range(width // LANES):
        pack_ref[c * n : (c + 1) * n, :] = mean_prec[:, c * LANES : (c + 1) * LANES]
    pack_ref[width // LANES * n :, :] = jnp.broadcast_to(to_row(offset, LANES), (8, LANES))


def coefficients(means, variances, mass):
    n, width = means.shape
    operands = (means, variances, mass.reshape(1, n))
    return pl.pallas_call(
        coefficient_kernel,
        in_specs=[pl.BlockSpec(memory_space=pl.ANY)] * 3,
        out_shape=jax.ShapeDtypeStruct((width // LANES * n + 8, LANES), F32),
        scratch_shapes=[
            pltpu.VMEM((n, width), F32),
            pltpu.VMEM((n, width), F32),
            pltpu.VMEM((1, n), F32),
            pltpu.SemaphoreType.DMA((3,)),
        ],
        cost_estimate=HEAVY,
        compiler_params=params(16),
        name="coefficients",
    )(*(pltpu.with_memory_space_constraint(x, pltpu.HBM) for x in operands))


def halves_kernel(own_ref, other_ref, xh_ref, xl_ref, sh_ref, sl_ref):
    def put(block):
        xh_ref[...], xl_ref[...] = split(block)
        sh_ref[...], sl_ref[...] = split(block * block)

    first = pl.program_id(0) < pl.num_programs(0) // 2

    @pl.when(first)
    def _():
        put(own_ref[...])

    @pl.when(jnp.logical_not(first))
    def _():
        put(other_ref[...])


def halves(own, other):
    rows, width = own.shape
    tile = min(256, rows)
    steps = rows // tile
    out = jax.ShapeDtypeStruct((2 * rows, width), BF16)
    return pl.pallas_call(
        halves_kernel,
        grid=(2 * steps,),
        in_specs=[
            pl.BlockSpec((tile, width), lambda i: (jnp.minimum(i, steps - 1), 0)),
            pl.BlockSpec((tile, width), lambda i: (jnp.maximum(i - steps, 0), 0)),
        ],
        out_specs=[pl.BlockSpec((tile, width), lambda i: (i, 0))] * 4,
        out_shape=[out] * 4,
        cost_estimate=HEAVY,
        compiler_params=params(16),
        name="halves",
    )(own, other)


def load_packs(packs, weights, n):
    comps, tiles = n * len(packs), weights.shape[1] // LANES
    for q, pack in enumerate(packs):
        for c in range(tiles):
            lanes = slice(c * LANES, (c + 1) * LANES)
            high, low = split(pack[c * n : (c + 1) * n, :])
            weights[q * n : (q + 1) * n, lanes] = high
            weights[comps + q * n : comps + (q + 1) * n, lanes] = low
    if packs[0].shape[0] == tiles * n:
        return None
    return jnp.concatenate([to_column(pack[tiles * n : tiles * n + 1, :], n) for pack in packs])


def load_variances(variances, weights, n):
    comps = n * len(variances)
    for q, ref in enumerate(variances):
        high, low = split(-0.5 * (1.0 / ref[...]))
        weights[q * n : (q + 1) * n, :] = high
        weights[comps + q * n : comps + (q + 1) * n, :] = low


def product(weights, high, low, dims):
    comps = weights.shape[0] // 2
    both = lax.dot_general(weights, high, dims, preferred_element_type=F32)
    rest = lax.dot_general(weights[:comps], low, dims, preferred_element_type=F32)
    return both[:comps] + (both[comps:] + rest)


def row_tiles(rows, tile=256):
    tile = min(tile, rows)
    return [slice(i, i + tile) for i in range(0, rows, tile)]


def quad_kernel(n, *refs):
    *variances, high_ref, low_ref, out_ref, weights = refs
    load_variances(variances, weights, n)
    for tile in row_tiles(high_ref.shape[0]):
        out_ref[:, tile] = product(weights[...], high_ref[tile, :], low_ref[tile, :], ACROSS)


def stats_of(scores):
    peak = jnp.max(scores, axis=0, keepdims=True)
    return peak, jnp.sum(jnp.exp(scores - peak), axis=0, keepdims=True)


def joined(one, other):
    peak = jnp.maximum(one[0], other[0])
    return peak, one[1] * jnp.exp(one[0] - peak) + other[1] * jnp.exp(other[0] - peak)


def early_kernel(n, *refs):
    *linear, high_ref, low_ref, quad_ref, out_ref, stats_ref, weights = refs
    offset = load_packs(linear, weights, n)
    for tile in row_tiles(high_ref.shape[0]):
        scores = product(weights[...], high_ref[tile, :], low_ref[tile, :], ACROSS)
        scores = quad_ref[:, tile] + scores + offset
        out_ref[:, tile] = scores
        stats_ref[0:1, tile], stats_ref[1:2, tile] = stats_of(scores)


def half_tiles(half):
    for block in range(2):
        for part in row_tiles(half):
            yield slice(block * half + part.start, block * half + part.stop), block, part


def head_kernel(n, *refs):
    *linear, high_ref, low_ref, quad_ref, out_ref, weights = refs
    load_packs(linear, weights, n)
    columns = slice(0, weights.shape[1])
    for tile in row_tiles(high_ref.shape[0]):
        scores = product(weights[...], high_ref[tile, columns], low_ref[tile, columns], ACROSS)
        out_ref[:, tile] = quad_ref[:, tile] + scores


def last_kernel(n, *refs):
    *linear, high_ref, low_ref, quad_ref, early_ref, out_ref, stats_ref, weights = refs
    offset = load_packs(linear, weights, n)
    columns = slice(high_ref.shape[1] - weights.shape[1], high_ref.shape[1])
    for tile, block, part in half_tiles(stats_ref.shape[2]):
        scores = product(weights[...], high_ref[tile, columns], low_ref[tile, columns], ACROSS)
        scores = quad_ref[:, tile] + scores + offset
        out_ref[:, tile] = scores
        early = early_ref[0:1, tile], early_ref[1:2, tile]
        peak, total = joined(stats_of(scores), early)
        stats_ref[block, 0:1, part] = peak
        stats_ref[block, 1:2, part] = total


def score_call(body, out_shape, scratch, name, *operands, cost=None):
    return pl.pallas_call(
        body,
        out_shape=[jax.ShapeDtypeStruct(shape, F32) for shape in out_shape],
        scratch_shapes=[pltpu.VMEM(shape, BF16) for shape in scratch],
        cost_estimate=cost or HEAVY,
        compiler_params=params(24),
        name=name,
    )(*operands)


def moment_tiles(resp_ref, high_ref, low_ref, packs, n):
    for c in range(0, high_ref.shape[1], 2 * LANES):
        columns = slice(c, c + 2 * LANES)
        total = product(resp_ref[...], high_ref[:, columns], low_ref[:, columns], WITHIN)
        for q, pack in enumerate(packs):
            for k in range(2):
                place = (c // LANES + k) * n
                pack[place : place + n, :] = total[q * n : (q + 1) * n, k * LANES : (k + 1) * LANES]


def first_kernel(n, early_ref, late_ref, stats_ref, high_ref, low_ref, *refs):
    *packs, resp_ref = refs
    comps = resp_ref.shape[0] // 2
    counts = jnp.zeros((comps, LANES), F32)
    for tile, block, part in half_tiles(stats_ref.shape[2]):
        peak, total = stats_ref[block, 0:1, part], stats_ref[block, 1:2, part]
        scores = jnp.concatenate([early_ref[:, tile], late_ref[:, tile]])
        resp = jnp.exp(scores - peak) * (1.0 / total)
        resp_ref[:comps, tile], resp_ref[comps:, tile] = split(resp)
        counts += sum(resp[:, c : c + LANES] for c in range(0, resp.shape[1], LANES))
    moment_tiles(resp_ref, high_ref, low_ref, packs, n)
    column = jnp.sum(counts, axis=1, keepdims=True)
    for q, pack in enumerate(packs):
        row = to_row(column[q * n : (q + 1) * n], LANES)
        pack[-8:, :] = jnp.broadcast_to(row, (8, LANES))


def first_moments(early, late, stats, high, low, n):
    rows, width = high.shape
    comps = early.shape[0] + late.shape[0]
    pack = jax.ShapeDtypeStruct((width // LANES * n + 8, LANES), F32)
    return pl.pallas_call(
        functools.partial(first_kernel, n),
        out_shape=[pack] * (comps // n) + [jax.ShapeDtypeStruct((2 * comps, rows), BF16)],
        cost_estimate=HEAVY,
        compiler_params=params(24),
        name="first_moments",
    )(early, late, stats, high, low)


def second_kernel(n, resp_ref, high_ref, low_ref, *packs):
    moment_tiles(resp_ref, high_ref, low_ref, packs, n)


def second_moments(resp, high, low, n):
    pack = jax.ShapeDtypeStruct((high.shape[1] // LANES * n, LANES), F32)
    return pl.pallas_call(
        functools.partial(second_kernel, n),
        out_shape=[pack] * (resp.shape[0] // 2 // n),
        cost_estimate=HEAVY,
        compiler_params=params(24),
        name="second_moments",
    )(resp, high, low)


def update_kernel(
    scale,
    means_ref,
    variances_ref,
    mass_ref,
    first_ref,
    second_ref,
    near_first_ref,
    near_second_ref,
    new_means_ref,
    new_variances_ref,
    new_mass_ref,
):
    n, width = means_ref.shape
    tiles = width // LANES * n
    row = first_ref[tiles : tiles + 1, :n] + near_first_ref[tiles : tiles + 1, :n]
    new_row = 0.4 * mass_ref[...] + scale * row
    new_mass_ref[...] = new_row
    inverse = 1.0 / to_column(new_row, n)
    kept = 0.4 * to_column(mass_ref[...], n)
    for c in range(width // LANES):
        lanes, tile = slice(c * LANES, (c + 1) * LANES), slice(c * n, (c + 1) * n)
        means, variances = means_ref[:, lanes], variances_ref[:, lanes]
        first = first_ref[tile, :] + near_first_ref[tile, :]
        second = second_ref[tile, :] + near_second_ref[tile, :]
        new_means = (kept * means + scale * first) * inverse
        new_means_ref[:, lanes] = new_means
        second_moment = kept * (variances + means * means) + scale * second
        new_variances_ref[:, lanes] = second_moment * inverse - new_means * new_means


def update(scale, means, variances, mass, *sums):
    n = mass.shape[0]
    block = jax.ShapeDtypeStruct(means.shape, F32)
    new_means, new_variances, new_mass = pl.pallas_call(
        functools.partial(update_kernel, scale),
        out_shape=(block, block, jax.ShapeDtypeStruct((1, n), F32)),
        cost_estimate=HEAVY,
        compiler_params=params(16),
        name="update",
    )(means, variances, mass.reshape(1, n), *sums)
    return new_means, new_variances, new_mass.reshape(n)


def swap(value, axis, bit):
    size = lax.axis_size(axis)
    return lax.ppermute(value, axis, [(i, i ^ bit) for i in range(size)])


def after(value, *others):
    return lax.optimization_barrier((value, *others))[0]


def gather_even(piece):
    bit = lax.axis_size("dp") // 4
    held = {0: piece}
    while bit > 1:
        held.update({q ^ bit: swap(value, "dp", 2 * bit) for q, value in held.items()})
        bit //= 2
    return held


def scatter_planes(first, second):
    held = [dict(enumerate(parts)) for parts in (first, second)]
    totals, near = [[parts.pop(0)] for parts in held], []
    planes, bit = len(first), 1
    while bit < planes:
        ready = []
        for parts in held:
            for q in sorted((q for q in parts if q & bit and q != bit), reverse=True):
                parts[q ^ bit] = parts[q ^ bit] + swap(after(parts.pop(q), *ready), "dp", 2 * bit)
                ready = [parts[q ^ bit]]
        for total, parts in zip(totals, held):
            part = swap(after(parts.pop(bit), *ready), "dp", 2 * bit)
            (near if bit == 1 else total).append(part)
        bit *= 2
    one, other, *near = lax.optimization_barrier((sum(totals[0][1:], totals[0][0]), totals[1][0], *near))
    return one, sum(totals[1][1:], other), *near


def merge(stats):
    peak = functools.reduce(jnp.maximum, [s[:, 0] for s in stats])
    total = sum(s[:, 1] * jnp.exp(s[:, 0] - peak) for s in stats)
    return jnp.stack([peak, total], axis=1)


def per_device(embeddings, comp_means, comp_variances, comp_mass):
    n = comp_means.shape[0]
    rows, width = embeddings.shape
    planes = lax.axis_size("dp") // 2
    variances = gather_even(comp_variances)
    near = swap(comp_variances, "dp", 2)
    pack = coefficients(comp_means, comp_variances, comp_mass)
    linear = [pack] + [swap(pack, "dp", 2 * q) for q in reversed(range(2, planes))][::-1]
    other = swap(embeddings, "dp", 1)
    x_high, x_low, s_high, s_low = halves(embeddings, other)
    far = {q ^ 1: swap(after(variances[q], x_high), "dp", 2) for q in sorted(variances) if q}
    variances = [{**variances, **far}[q] for q in range(planes) if q != 1]
    n_early = n * len(linear)

    def quad_scores(group, name):
        comps = n * len(group)
        body = functools.partial(quad_kernel, n)
        shapes = [(comps, 2 * rows)], [(2 * comps, width)]
        return score_call(body, *shapes, name, *group, s_high, s_low)[0]

    head = width // LANES * 2 // 3
    late_head = swap(pack[: head * n], "dp", 2)
    late_quad = quad_scores([near], "late_quad")
    late_tail = swap(after(pack[head * n :], late_quad), "dp", 2)
    early, early_stats = score_call(
        functools.partial(early_kernel, n),
        [(n_early, 2 * rows), (2, 2 * rows)],
        [(2 * n_early, width)],
        "early_scores",
        *linear,
        x_high,
        x_low,
        quad_scores(variances, "early_quad"),
        cost=LIGHT,
    )
    (part,) = score_call(
        functools.partial(head_kernel, n),
        [(n, 2 * rows)],
        [(2 * n, head * LANES)],
        "late_head",
        late_head,
        x_high,
        x_low,
        late_quad,
        cost=LIGHT,
    )
    last, stats = score_call(
        functools.partial(last_kernel, n),
        [(n, 2 * rows), (2, 2, rows)],
        [(2 * n, width - head * LANES)],
        "last_scores",
        late_tail,
        x_high,
        x_low,
        part,
        early_stats,
    )
    stats = merge([stats, swap(stats, "dp", 1)[::-1]])
    stats = merge([stats] + [swap(stats, "comp", q) for q in range(1, lax.axis_size("comp"))])

    *first, resp = first_moments(early, last, stats, x_high, x_low, n)
    second = second_moments(resp, s_high, s_low, n)
    place = {q: i for i, q in enumerate([0, *range(2, planes), 1])}
    first, second = ([parts[place[q]] for q in range(planes)] for parts in (first, second))
    sums = scatter_planes(first, second)

    total_comps = n * lax.axis_size("dp") * lax.axis_size("comp")
    total_rows = embeddings.shape[0] * lax.axis_size("dp")
    scale = 0.6 * (total_comps / total_rows)
    return update(scale, comp_means, comp_variances, comp_mass, *sums)


def solution(mesh):
    placed = (P("dp", None), P(("comp", "dp"), None), P(("comp", "dp"), None), P(("comp", "dp")))
    return jax.shard_map(
        per_device,
        mesh=mesh,
        in_specs=placed,
        out_specs=(P(("comp", "dp"), None), P(("comp", "dp"), None), P(("comp", "dp"))),
        check_vma=False,
    )
```

```python
import functools

import jax
import jax.numpy as jnp
from jax import lax
from jax.experimental import pallas as pl
from jax.experimental.pallas import tpu as pltpu
from jax.sharding import PartitionSpec as P

F32 = jnp.float32
BF16 = jnp.bfloat16
LANES = 128
HEAVY = pl.CostEstimate(flops=10**10, bytes_accessed=10**8, transcendentals=0)
LIGHT = pl.CostEstimate(flops=10**8, bytes_accessed=10**6, transcendentals=0)
ACROSS = (((1,), (1,)), ((), ()))
WITHIN = (((1,), (0,)), ((), ()))


def params(megabytes):
    return pltpu.CompilerParams(vmem_limit_bytes=megabytes * 1024 * 1024)


def split(value):
    high = value.astype(BF16)
    return high, (value - high.astype(F32)).astype(BF16)


def diagonal(rows, columns):
    shape = (rows, columns)
    return lax.broadcasted_iota(jnp.int32, shape, 0) == lax.broadcasted_iota(jnp.int32, shape, 1)


def to_row(column, lanes):
    return jnp.sum(jnp.where(diagonal(column.shape[0], lanes), column, 0.0), axis=0, keepdims=True)


def to_column(row, rows):
    return jnp.sum(jnp.where(diagonal(rows, row.shape[1]), row, 0.0), axis=1, keepdims=True)


def coefficient_kernel(
    means_hbm, variances_hbm, mass_hbm, pack_ref, means_ref, variances_ref, mass_ref, sems
):
    sources = (variances_hbm, means_hbm, mass_hbm)
    targets = (variances_ref, means_ref, mass_ref)
    copies = [pltpu.make_async_copy(s, t, sems.at[i]) for i, (s, t) in enumerate(zip(sources, targets))]
    for copy in copies:
        copy.start()
    for copy in copies:
        copy.wait()
    n, width = means_ref.shape
    means, variances = means_ref[...], variances_ref[...]
    mean_prec = means * (1.0 / variances)
    sums = jnp.sum(jnp.log(variances) + means * mean_prec, axis=1, keepdims=True)
    offset = to_column(jnp.log(mass_ref[...]), n) - 0.5 * sums
    for c in range(width // LANES):
        pack_ref[c * n : (c + 1) * n, :] = mean_prec[:, c * LANES : (c + 1) * LANES]
    pack_ref[width // LANES * n :, :] = jnp.broadcast_to(to_row(offset, LANES), (8, LANES))


def coefficients(means, variances, mass):
    n, width = means.shape
    operands = (means, variances, mass.reshape(1, n))
    return pl.pallas_call(
        coefficient_kernel,
        in_specs=[pl.BlockSpec(memory_space=pl.ANY)] * 3,
        out_shape=jax.ShapeDtypeStruct((width // LANES * n + 8, LANES), F32),
        scratch_shapes=[
            pltpu.VMEM((n, width), F32),
            pltpu.VMEM((n, width), F32),
            pltpu.VMEM((1, n), F32),
            pltpu.SemaphoreType.DMA((3,)),
        ],
        cost_estimate=HEAVY,
        compiler_params=params(16),
        name="coefficients",
    )(*(pltpu.with_memory_space_constraint(x, pltpu.HBM) for x in operands))


def halves_kernel(own_ref, other_ref, xh_ref, xl_ref, sh_ref, sl_ref):
    def put(block):
        xh_ref[...], xl_ref[...] = split(block)
        sh_ref[...], sl_ref[...] = split(block * block)

    first = pl.program_id(0) < pl.num_programs(0) // 2

    @pl.when(first)
    def _():
        put(own_ref[...])

    @pl.when(jnp.logical_not(first))
    def _():
        put(other_ref[...])


def halves(own, other):
    rows, width = own.shape
    tile = min(256, rows)
    steps = rows // tile
    out = jax.ShapeDtypeStruct((2 * rows, width), BF16)
    return pl.pallas_call(
        halves_kernel,
        grid=(2 * steps,),
        in_specs=[
            pl.BlockSpec((tile, width), lambda i: (jnp.minimum(i, steps - 1), 0)),
            pl.BlockSpec((tile, width), lambda i: (jnp.maximum(i - steps, 0), 0)),
        ],
        out_specs=[pl.BlockSpec((tile, width), lambda i: (i, 0))] * 4,
        out_shape=[out] * 4,
        cost_estimate=HEAVY,
        compiler_params=params(16),
        name="halves",
    )(own, other)


def load_packs(packs, weights, n):
    comps, tiles = n * len(packs), weights.shape[1] // LANES
    for q, pack in enumerate(packs):
        for c in range(tiles):
            lanes = slice(c * LANES, (c + 1) * LANES)
            high, low = split(pack[c * n : (c + 1) * n, :])
            weights[q * n : (q + 1) * n, lanes] = high
            weights[comps + q * n : comps + (q + 1) * n, lanes] = low
    return jnp.concatenate([to_column(pack[tiles * n : tiles * n + 1, :], n) for pack in packs])


def load_variances(variances, weights, n):
    comps = n * len(variances)
    for q, ref in enumerate(variances):
        high, low = split(-0.5 * (1.0 / ref[...]))
        weights[q * n : (q + 1) * n, :] = high
        weights[comps + q * n : comps + (q + 1) * n, :] = low


def product(weights, high, low, dims):
    comps = weights.shape[0] // 2
    both = lax.dot_general(weights, high, dims, preferred_element_type=F32)
    rest = lax.dot_general(weights[:comps], low, dims, preferred_element_type=F32)
    return both[:comps] + (both[comps:] + rest)


def row_tiles(rows, tile=256):
    tile = min(tile, rows)
    return [slice(i, i + tile) for i in range(0, rows, tile)]


def quad_kernel(n, *refs):
    *variances, high_ref, low_ref, out_ref, weights = refs
    load_variances(variances, weights, n)
    for tile in row_tiles(high_ref.shape[0]):
        out_ref[:, tile] = product(weights[...], high_ref[tile, :], low_ref[tile, :], ACROSS)


def linear_kernel(n, *refs):
    *linear, high_ref, low_ref, out_ref, weights = refs
    offset = load_packs(linear, weights, n)
    for tile in row_tiles(high_ref.shape[0]):
        out_ref[:, tile] = product(weights[...], high_ref[tile, :], low_ref[tile, :], ACROSS) + offset


def stats_of(scores):
    peak = jnp.max(scores, axis=0, keepdims=True)
    return peak, jnp.sum(jnp.exp(scores - peak), axis=0, keepdims=True)


def joined(one, other):
    peak = jnp.maximum(one[0], other[0])
    return peak, one[1] * jnp.exp(one[0] - peak) + other[1] * jnp.exp(other[0] - peak)


def early_kernel(n, *refs):
    *linear, high_ref, low_ref, quad_ref, out_ref, stats_ref, weights = refs
    offset = load_packs(linear, weights, n)
    for tile in row_tiles(high_ref.shape[0]):
        scores = product(weights[...], high_ref[tile, :], low_ref[tile, :], ACROSS)
        scores = quad_ref[:, tile] + scores + offset
        out_ref[:, tile] = scores
        stats_ref[0:1, tile], stats_ref[1:2, tile] = stats_of(scores)


def half_tiles(half):
    for block in range(2):
        for part in row_tiles(half):
            yield slice(block * half + part.start, block * half + part.stop), block, part


def head_kernel(n, *refs):
    *variances, high_ref, low_ref, linear_ref, out_ref, weights = refs
    load_variances(variances, weights, n)
    columns = slice(0, weights.shape[1])
    for tile in row_tiles(high_ref.shape[0]):
        scores = product(weights[...], high_ref[tile, columns], low_ref[tile, columns], ACROSS)
        out_ref[:, tile] = linear_ref[:, tile] + scores


def last_kernel(n, *refs):
    *variances, high_ref, low_ref, rest_ref, early_ref, out_ref, stats_ref, weights = refs
    load_variances(variances, weights, n)
    columns = slice(high_ref.shape[1] - weights.shape[1], high_ref.shape[1])
    for tile, block, part in half_tiles(stats_ref.shape[2]):
        scores = product(weights[...], high_ref[tile, columns], low_ref[tile, columns], ACROSS)
        scores = rest_ref[:, tile] + scores
        out_ref[:, tile] = scores
        early = early_ref[0:1, tile], early_ref[1:2, tile]
        peak, total = joined(stats_of(scores), early)
        stats_ref[block, 0:1, part] = peak
        stats_ref[block, 1:2, part] = total


def score_call(body, out_shape, scratch, name, *operands, cost=None):
    return pl.pallas_call(
        body,
        out_shape=[jax.ShapeDtypeStruct(shape, F32) for shape in out_shape],
        scratch_shapes=[pltpu.VMEM(shape, BF16) for shape in scratch],
        cost_estimate=cost or HEAVY,
        compiler_params=params(24),
        name=name,
    )(*operands)


def moment_tiles(resp_ref, high_ref, low_ref, packs, n):
    for c in range(0, high_ref.shape[1], 2 * LANES):
        columns = slice(c, c + 2 * LANES)
        total = product(resp_ref[...], high_ref[:, columns], low_ref[:, columns], WITHIN)
        for q, pack in enumerate(packs):
            for k in range(2):
                place = (c // LANES + k) * n
                pack[place : place + n, :] = total[q * n : (q + 1) * n, k * LANES : (k + 1) * LANES]


def first_kernel(n, early_ref, late_ref, stats_ref, high_ref, low_ref, *refs):
    *packs, resp_ref = refs
    comps = resp_ref.shape[0] // 2
    counts = jnp.zeros((comps, LANES), F32)
    for tile, block, part in half_tiles(stats_ref.shape[2]):
        peak, total = stats_ref[block, 0:1, part], stats_ref[block, 1:2, part]
        scores = jnp.concatenate([early_ref[:, tile], late_ref[:, tile]])
        resp = jnp.exp(scores - peak) * (1.0 / total)
        resp_ref[:comps, tile], resp_ref[comps:, tile] = split(resp)
        counts += sum(resp[:, c : c + LANES] for c in range(0, resp.shape[1], LANES))
    moment_tiles(resp_ref, high_ref, low_ref, packs, n)
    column = jnp.sum(counts, axis=1, keepdims=True)
    for q, pack in enumerate(packs):
        row = to_row(column[q * n : (q + 1) * n], LANES)
        pack[-8:, :] = jnp.broadcast_to(row, (8, LANES))


def first_moments(early, late, stats, high, low, n):
    rows, width = high.shape
    comps = early.shape[0] + late.shape[0]
    pack = jax.ShapeDtypeStruct((width // LANES * n + 8, LANES), F32)
    return pl.pallas_call(
        functools.partial(first_kernel, n),
        out_shape=[pack] * (comps // n) + [jax.ShapeDtypeStruct((2 * comps, rows), BF16)],
        cost_estimate=HEAVY,
        compiler_params=params(24),
        name="first_moments",
    )(early, late, stats, high, low)


def second_kernel(n, resp_ref, high_ref, low_ref, *packs):
    moment_tiles(resp_ref, high_ref, low_ref, packs, n)


def second_moments(resp, high, low, n):
    pack = jax.ShapeDtypeStruct((high.shape[1] // LANES * n, LANES), F32)
    return pl.pallas_call(
        functools.partial(second_kernel, n),
        out_shape=[pack] * (resp.shape[0] // 2 // n),
        cost_estimate=HEAVY,
        compiler_params=params(24),
        name="second_moments",
    )(resp, high, low)


def update_kernel(
    scale,
    means_ref,
    variances_ref,
    mass_ref,
    first_ref,
    second_ref,
    near_first_ref,
    near_second_ref,
    new_means_ref,
    new_variances_ref,
    new_mass_ref,
):
    n, width = means_ref.shape
    tiles = width // LANES * n
    row = first_ref[tiles : tiles + 1, :n] + near_first_ref[tiles : tiles + 1, :n]
    new_row = 0.4 * mass_ref[...] + scale * row
    new_mass_ref[...] = new_row
    inverse = 1.0 / to_column(new_row, n)
    kept = 0.4 * to_column(mass_ref[...], n)
    for c in range(width // LANES):
        lanes, tile = slice(c * LANES, (c + 1) * LANES), slice(c * n, (c + 1) * n)
        means, variances = means_ref[:, lanes], variances_ref[:, lanes]
        first = first_ref[tile, :] + near_first_ref[tile, :]
        second = second_ref[tile, :] + near_second_ref[tile, :]
        new_means = (kept * means + scale * first) * inverse
        new_means_ref[:, lanes] = new_means
        second_moment = kept * (variances + means * means) + scale * second
        new_variances_ref[:, lanes] = second_moment * inverse - new_means * new_means


def update(scale, means, variances, mass, *sums):
    n = mass.shape[0]
    block = jax.ShapeDtypeStruct(means.shape, F32)
    new_means, new_variances, new_mass = pl.pallas_call(
        functools.partial(update_kernel, scale),
        out_shape=(block, block, jax.ShapeDtypeStruct((1, n), F32)),
        cost_estimate=HEAVY,
        compiler_params=params(16),
        name="update",
    )(means, variances, mass.reshape(1, n), *sums)
    return new_means, new_variances, new_mass.reshape(n)


def swap(value, axis, bit):
    size = lax.axis_size(axis)
    return lax.ppermute(value, axis, [(i, i ^ bit) for i in range(size)])


def after(value, *others):
    return lax.optimization_barrier((value, *others))[0]


def gather_even(piece):
    bit = lax.axis_size("dp") // 4
    held = {0: piece}
    while bit > 1:
        held.update({q ^ bit: swap(value, "dp", 2 * bit) for q, value in held.items()})
        bit //= 2
    return held


def scatter_planes(first, second):
    held = [dict(enumerate(parts)) for parts in (first, second)]
    totals, near = [[parts.pop(0)] for parts in held], []
    planes, bit = len(first), 1
    while bit < planes:
        ready = []
        for parts in held:
            for q in sorted((q for q in parts if q & bit and q != bit), reverse=True):
                parts[q ^ bit] = parts[q ^ bit] + swap(after(parts.pop(q), *ready), "dp", 2 * bit)
                ready = [parts[q ^ bit]]
        for total, parts in zip(totals, held):
            part = swap(after(parts.pop(bit), *ready), "dp", 2 * bit)
            (near if bit == 1 else total).append(part)
        bit *= 2
    one, other, *near = lax.optimization_barrier((sum(totals[0][1:], totals[0][0]), totals[1][0], *near))
    return one, sum(totals[1][1:], other), *near


def merge(stats):
    peak = functools.reduce(jnp.maximum, [s[:, 0] for s in stats])
    total = sum(s[:, 1] * jnp.exp(s[:, 0] - peak) for s in stats)
    return jnp.stack([peak, total], axis=1)


def per_device(embeddings, comp_means, comp_variances, comp_mass):
    n = comp_means.shape[0]
    rows, width = embeddings.shape
    planes = lax.axis_size("dp") // 2
    variances = gather_even(comp_variances)
    variances[1] = swap(comp_variances, "dp", 2)
    pack = coefficients(comp_means, comp_variances, comp_mass)
    linear = {q: swap(pack, "dp", 2 * q) for q in range(planes - 1, 0, -1)} | {0: pack}
    other = swap(embeddings, "dp", 1)
    x_high, x_low, s_high, s_low = halves(embeddings, other)
    order = sorted(variances)
    late = [q for q in range(planes) if q not in variances]
    n_early, n_late = n * len(order), n * len(late)
    head = width // LANES * 2 // 3 * LANES
    sources = [after(variances[q ^ 1], x_high) for q in late]
    heads = [swap(source[:, :head], "dp", 2) for source in sources]
    (quad,) = score_call(
        functools.partial(quad_kernel, n),
        [(n_early, 2 * rows)],
        [(2 * n_early, width)],
        "early_quad",
        *(variances[q] for q in order),
        s_high,
        s_low,
    )
    tails = [swap(after(source[:, head:], quad), "dp", 2) for source in sources]
    early, early_stats = score_call(
        functools.partial(early_kernel, n),
        [(n_early, 2 * rows), (2, 2 * rows)],
        [(2 * n_early, width)],
        "early_scores",
        *(linear[q] for q in order),
        x_high,
        x_low,
        quad,
        cost=LIGHT,
    )
    (part,) = score_call(
        functools.partial(linear_kernel, n),
        [(n_late, 2 * rows)],
        [(2 * n_late, width)],
        "late_linear",
        *(linear[q] for q in late),
        x_high,
        x_low,
        cost=LIGHT,
    )
    (part,) = score_call(
        functools.partial(head_kernel, n),
        [(n_late, 2 * rows)],
        [(2 * n_late, head)],
        "late_head",
        *heads,
        s_high,
        s_low,
        part,
        cost=LIGHT,
    )
    last, stats = score_call(
        functools.partial(last_kernel, n),
        [(n_late, 2 * rows), (2, 2, rows)],
        [(2 * n_late, width - head)],
        "last_scores",
        *tails,
        s_high,
        s_low,
        part,
        early_stats,
    )
    stats = merge([stats, swap(stats, "dp", 1)[::-1]])
    stats = merge([stats] + [swap(stats, "comp", q) for q in range(1, lax.axis_size("comp"))])

    *first, resp = first_moments(early, last, stats, x_high, x_low, n)
    second = second_moments(resp, s_high, s_low, n)
    place = {q: i for i, q in enumerate(order + late)}
    first, second = ([parts[place[q]] for q in range(planes)] for parts in (first, second))
    sums = scatter_planes(first, second)

    total_comps = n * lax.axis_size("dp") * lax.axis_size("comp")
    total_rows = embeddings.shape[0] * lax.axis_size("dp")
    scale = 0.6 * (total_comps / total_rows)
    return update(scale, comp_means, comp_variances, comp_mass, *sums)


def solution(mesh):
    placed = (P("dp", None), P(("comp", "dp"), None), P(("comp", "dp"), None), P(("comp", "dp")))
    return jax.shard_map(
        per_device,
        mesh=mesh,
        in_specs=placed,
        out_specs=(P(("comp", "dp"), None), P(("comp", "dp"), None), P(("comp", "dp"))),
        check_vma=False,
    )
```

```python
import functools

import jax
import jax.numpy as jnp
from jax import lax
from jax.experimental import pallas as pl
from jax.experimental.pallas import tpu as pltpu
from jax.sharding import PartitionSpec as P

F32 = jnp.float32
BF16 = jnp.bfloat16
LANES = 128
HEAVY = pl.CostEstimate(flops=10**10, bytes_accessed=10**8, transcendentals=0)
LIGHT = pl.CostEstimate(flops=10**8, bytes_accessed=10**6, transcendentals=0)
ACROSS = (((1,), (1,)), ((), ()))
WITHIN = (((1,), (0,)), ((), ()))


def params(megabytes):
    return pltpu.CompilerParams(vmem_limit_bytes=megabytes * 1024 * 1024)


def split(value):
    high = value.astype(BF16)
    return high, (value - high.astype(F32)).astype(BF16)


def diagonal(rows, columns):
    shape = (rows, columns)
    return lax.broadcasted_iota(jnp.int32, shape, 0) == lax.broadcasted_iota(jnp.int32, shape, 1)


def to_row(column, lanes):
    return jnp.sum(jnp.where(diagonal(column.shape[0], lanes), column, 0.0), axis=0, keepdims=True)


def to_column(row, rows):
    return jnp.sum(jnp.where(diagonal(rows, row.shape[1]), row, 0.0), axis=1, keepdims=True)


def coefficient_kernel(
    means_hbm, variances_hbm, mass_hbm, pack_ref, means_ref, variances_ref, mass_ref, sems
):
    sources = (variances_hbm, means_hbm, mass_hbm)
    targets = (variances_ref, means_ref, mass_ref)
    copies = [pltpu.make_async_copy(s, t, sems.at[i]) for i, (s, t) in enumerate(zip(sources, targets))]
    for copy in copies:
        copy.start()
    for copy in copies:
        copy.wait()
    n, width = means_ref.shape
    means, variances = means_ref[...], variances_ref[...]
    mean_prec = means * (1.0 / variances)
    sums = jnp.sum(jnp.log(variances) + means * mean_prec, axis=1, keepdims=True)
    offset = to_column(jnp.log(mass_ref[...]), n) - 0.5 * sums
    for c in range(width // LANES):
        pack_ref[c * n : (c + 1) * n, :] = mean_prec[:, c * LANES : (c + 1) * LANES]
    pack_ref[width // LANES * n :, :] = jnp.broadcast_to(to_row(offset, LANES), (8, LANES))


def coefficients(means, variances, mass):
    n, width = means.shape
    operands = (means, variances, mass.reshape(1, n))
    return pl.pallas_call(
        coefficient_kernel,
        in_specs=[pl.BlockSpec(memory_space=pl.ANY)] * 3,
        out_shape=jax.ShapeDtypeStruct((width // LANES * n + 8, LANES), F32),
        scratch_shapes=[
            pltpu.VMEM((n, width), F32),
            pltpu.VMEM((n, width), F32),
            pltpu.VMEM((1, n), F32),
            pltpu.SemaphoreType.DMA((3,)),
        ],
        cost_estimate=HEAVY,
        compiler_params=params(16),
        name="coefficients",
    )(*(pltpu.with_memory_space_constraint(x, pltpu.HBM) for x in operands))


def halves_kernel(own_ref, other_ref, xh_ref, xl_ref, sh_ref, sl_ref):
    def put(block):
        xh_ref[...], xl_ref[...] = split(block)
        sh_ref[...], sl_ref[...] = split(block * block)

    first = pl.program_id(0) < pl.num_programs(0) // 2

    @pl.when(first)
    def _():
        put(own_ref[...])

    @pl.when(jnp.logical_not(first))
    def _():
        put(other_ref[...])


def halves(own, other):
    rows, width = own.shape
    tile = min(256, rows)
    steps = rows // tile
    out = jax.ShapeDtypeStruct((2 * rows, width), BF16)
    return pl.pallas_call(
        halves_kernel,
        grid=(2 * steps,),
        in_specs=[
            pl.BlockSpec((tile, width), lambda i: (jnp.minimum(i, steps - 1), 0)),
            pl.BlockSpec((tile, width), lambda i: (jnp.maximum(i - steps, 0), 0)),
        ],
        out_specs=[pl.BlockSpec((tile, width), lambda i: (i, 0))] * 4,
        out_shape=[out] * 4,
        cost_estimate=HEAVY,
        compiler_params=params(16),
        name="halves",
    )(own, other)


def load_packs(packs, weights, n):
    comps, tiles = n * len(packs), weights.shape[1] // LANES
    for q, pack in enumerate(packs):
        for c in range(tiles):
            lanes = slice(c * LANES, (c + 1) * LANES)
            high, low = split(pack[c * n : (c + 1) * n, :])
            weights[q * n : (q + 1) * n, lanes] = high
            weights[comps + q * n : comps + (q + 1) * n, lanes] = low
    if packs[0].shape[0] == tiles * n:
        return None
    return jnp.concatenate([to_column(pack[tiles * n : tiles * n + 1, :], n) for pack in packs])


def load_variances(variances, weights, n):
    comps = n * len(variances)
    for q, ref in enumerate(variances):
        high, low = split(-0.5 * (1.0 / ref[...]))
        weights[q * n : (q + 1) * n, :] = high
        weights[comps + q * n : comps + (q + 1) * n, :] = low


def product(weights, high, low, dims):
    comps = weights.shape[0] // 2
    both = lax.dot_general(weights, high, dims, preferred_element_type=F32)
    rest = lax.dot_general(weights[:comps], low, dims, preferred_element_type=F32)
    return both[:comps] + (both[comps:] + rest)


def row_tiles(rows, tile=256):
    tile = min(tile, rows)
    return [slice(i, i + tile) for i in range(0, rows, tile)]


def quad_kernel(n, *refs):
    *variances, high_ref, low_ref, out_ref, weights = refs
    load_variances(variances, weights, n)
    for tile in row_tiles(high_ref.shape[0]):
        out_ref[:, tile] = product(weights[...], high_ref[tile, :], low_ref[tile, :], ACROSS)


def stats_of(scores):
    peak = jnp.max(scores, axis=0, keepdims=True)
    return peak, jnp.sum(jnp.exp(scores - peak), axis=0, keepdims=True)


def joined(one, other):
    peak = jnp.maximum(one[0], other[0])
    return peak, one[1] * jnp.exp(one[0] - peak) + other[1] * jnp.exp(other[0] - peak)


def early_kernel(n, *refs):
    *linear, high_ref, low_ref, quad_ref, out_ref, stats_ref, weights = refs
    offset = load_packs(linear, weights, n)
    for tile in row_tiles(high_ref.shape[0]):
        scores = product(weights[...], high_ref[tile, :], low_ref[tile, :], ACROSS)
        scores = quad_ref[:, tile] + scores + offset
        out_ref[:, tile] = scores
        stats_ref[0:1, tile], stats_ref[1:2, tile] = stats_of(scores)


def half_tiles(half):
    for block in range(2):
        for part in row_tiles(half):
            yield slice(block * half + part.start, block * half + part.stop), block, part


def head_kernel(n, *refs):
    *linear, high_ref, low_ref, quad_ref, out_ref, weights = refs
    load_packs(linear, weights, n)
    columns = slice(0, weights.shape[1])
    for tile in row_tiles(high_ref.shape[0]):
        scores = product(weights[...], high_ref[tile, columns], low_ref[tile, columns], ACROSS)
        out_ref[:, tile] = quad_ref[:, tile] + scores


def last_kernel(n, *refs):
    *linear, high_ref, low_ref, quad_ref, early_ref, out_ref, stats_ref, weights = refs
    offset = load_packs(linear, weights, n)
    columns = slice(high_ref.shape[1] - weights.shape[1], high_ref.shape[1])
    for tile, block, part in half_tiles(stats_ref.shape[2]):
        scores = product(weights[...], high_ref[tile, columns], low_ref[tile, columns], ACROSS)
        scores = quad_ref[:, tile] + scores + offset
        out_ref[:, tile] = scores
        early = early_ref[0:1, tile], early_ref[1:2, tile]
        peak, total = joined(stats_of(scores), early)
        stats_ref[block, 0:1, part] = peak
        stats_ref[block, 1:2, part] = total


def score_call(body, out_shape, scratch, name, *operands, cost=None):
    return pl.pallas_call(
        body,
        out_shape=[jax.ShapeDtypeStruct(shape, F32) for shape in out_shape],
        scratch_shapes=[pltpu.VMEM(shape, BF16) for shape in scratch],
        cost_estimate=cost or HEAVY,
        compiler_params=params(24),
        name=name,
    )(*operands)


def moment_tiles(resp_ref, high_ref, low_ref, packs, n):
    for c in range(0, high_ref.shape[1], 2 * LANES):
        columns = slice(c, c + 2 * LANES)
        total = product(resp_ref[...], high_ref[:, columns], low_ref[:, columns], WITHIN)
        for q, pack in enumerate(packs):
            for k in range(2):
                place = (c // LANES + k) * n
                pack[place : place + n, :] = total[q * n : (q + 1) * n, k * LANES : (k + 1) * LANES]


def first_kernel(n, early_ref, late_ref, stats_ref, high_ref, low_ref, *refs):
    *packs, resp_ref = refs
    comps = resp_ref.shape[0] // 2
    counts = jnp.zeros((comps, LANES), F32)
    for tile, block, part in half_tiles(stats_ref.shape[2]):
        peak, total = stats_ref[block, 0:1, part], stats_ref[block, 1:2, part]
        scores = jnp.concatenate([early_ref[:, tile], late_ref[:, tile]])
        resp = jnp.exp(scores - peak) * (1.0 / total)
        resp_ref[:comps, tile], resp_ref[comps:, tile] = split(resp)
        counts += sum(resp[:, c : c + LANES] for c in range(0, resp.shape[1], LANES))
    moment_tiles(resp_ref, high_ref, low_ref, packs, n)
    column = jnp.sum(counts, axis=1, keepdims=True)
    for q, pack in enumerate(packs):
        row = to_row(column[q * n : (q + 1) * n], LANES)
        pack[-8:, :] = jnp.broadcast_to(row, (8, LANES))


def first_moments(early, late, stats, high, low, n):
    rows, width = high.shape
    comps = early.shape[0] + late.shape[0]
    pack = jax.ShapeDtypeStruct((width // LANES * n + 8, LANES), F32)
    return pl.pallas_call(
        functools.partial(first_kernel, n),
        out_shape=[pack] * (comps // n) + [jax.ShapeDtypeStruct((2 * comps, rows), BF16)],
        cost_estimate=HEAVY,
        compiler_params=params(24),
        name="first_moments",
    )(early, late, stats, high, low)


def second_kernel(n, resp_ref, high_ref, low_ref, *packs):
    moment_tiles(resp_ref, high_ref, low_ref, packs, n)


def second_moments(resp, high, low, n):
    pack = jax.ShapeDtypeStruct((high.shape[1] // LANES * n, LANES), F32)
    return pl.pallas_call(
        functools.partial(second_kernel, n),
        out_shape=[pack] * (resp.shape[0] // 2 // n),
        cost_estimate=HEAVY,
        compiler_params=params(24),
        name="second_moments",
    )(resp, high, low)


def update_kernel(
    scale,
    means_ref,
    variances_ref,
    mass_ref,
    first_ref,
    second_ref,
    near_first_ref,
    near_second_ref,
    new_means_ref,
    new_variances_ref,
    new_mass_ref,
):
    n, width = means_ref.shape
    tiles = width // LANES * n
    row = first_ref[tiles : tiles + 1, :n] + near_first_ref[tiles : tiles + 1, :n]
    new_row = 0.4 * mass_ref[...] + scale * row
    new_mass_ref[...] = new_row
    inverse = 1.0 / to_column(new_row, n)
    kept = 0.4 * to_column(mass_ref[...], n)
    for c in range(width // LANES):
        lanes, tile = slice(c * LANES, (c + 1) * LANES), slice(c * n, (c + 1) * n)
        means, variances = means_ref[:, lanes], variances_ref[:, lanes]
        first = first_ref[tile, :] + near_first_ref[tile, :]
        second = second_ref[tile, :] + near_second_ref[tile, :]
        new_means = (kept * means + scale * first) * inverse
        new_means_ref[:, lanes] = new_means
        second_moment = kept * (variances + means * means) + scale * second
        new_variances_ref[:, lanes] = second_moment * inverse - new_means * new_means


def update(scale, means, variances, mass, *sums):
    n = mass.shape[0]
    block = jax.ShapeDtypeStruct(means.shape, F32)
    new_means, new_variances, new_mass = pl.pallas_call(
        functools.partial(update_kernel, scale),
        out_shape=(block, block, jax.ShapeDtypeStruct((1, n), F32)),
        cost_estimate=HEAVY,
        compiler_params=params(16),
        name="update",
    )(means, variances, mass.reshape(1, n), *sums)
    return new_means, new_variances, new_mass.reshape(n)


def swap(value, axis, bit):
    size = lax.axis_size(axis)
    return lax.ppermute(value, axis, [(i, i ^ bit) for i in range(size)])


def vmem(value):
    return pltpu.with_memory_space_constraint(value, pltpu.VMEM)


def after(value, *others):
    return lax.optimization_barrier((value, *others))[0]


def gather_early(piece):
    bit = lax.axis_size("dp") // 4
    held = {0: piece}
    while bit > 1:
        held.update({q ^ bit: swap(value, "dp", 2 * bit) for q, value in held.items()})
        bit //= 2
    held[1] = swap(piece, "dp", 2)
    return held


def scatter_planes(first, second):
    held = [dict(enumerate(parts)) for parts in (first, second)]
    totals, near = [[parts.pop(0)] for parts in held], []
    near = [swap(after(held[0].pop(1), second[0]), "dp", 2)]
    planes, bit = len(first), 1
    while bit < planes:
        ready = []
        for parts in held:
            for q in sorted((q for q in parts if q & bit and q != bit), reverse=True):
                parts[q ^ bit] = parts[q ^ bit] + swap(after(parts.pop(q), *ready), "dp", 2 * bit)
                ready = [parts[q ^ bit]]
        if bit == 1:
            near.append(swap(after(held[1].pop(1), *ready), "dp", 2))
            held[1] = {q: after(part, near[0]) for q, part in held[1].items()}
        else:
            for total, parts in zip(totals, held):
                total.append(swap(after(parts.pop(bit), *ready), "dp", 2 * bit))
        bit *= 2
    return *lax.optimization_barrier(tuple(sum(t[1:], t[0]) for t in totals)), *near


def merge(stats):
    peak = functools.reduce(jnp.maximum, [s[:, 0] for s in stats])
    total = sum(s[:, 1] * jnp.exp(s[:, 0] - peak) for s in stats)
    return jnp.stack([peak, total], axis=1)


def per_device(embeddings, comp_means, comp_variances, comp_mass):
    n = comp_means.shape[0]
    rows, width = embeddings.shape
    planes = lax.axis_size("dp") // 2
    variances = gather_early(comp_variances)
    linear = gather_early(coefficients(comp_means, comp_variances, comp_mass))
    other = swap(embeddings, "dp", 1)
    order = sorted(linear)
    late = [q for q in range(planes) if q not in linear]
    x_high, x_low, s_high, s_low = halves(embeddings, other)
    for q in late:
        variances[q] = swap(after(variances[q ^ 1], x_high), "dp", 2)
    n_early, n_late = n * len(order), n * len(late)

    def quad_scores(group, name, cost=None):
        comps = n * len(group)
        operands = (*(vmem(variances[q]) for q in group), s_high, s_low)
        body = functools.partial(quad_kernel, n)
        return score_call(body, [(comps, 2 * rows)], [(2 * comps, width)], name, *operands, cost=cost)[0]

    quad = quad_scores(order, "early_quad")
    head = width // LANES * 2 // 3
    heads, tails = [], []
    for q in late:
        source = after(linear[q ^ 1], quad)
        heads.append(vmem(swap(source[: head * n], "dp", 2)))
        tails.append(source[head * n :])
    early, early_stats = score_call(
        functools.partial(early_kernel, n),
        [(n_early, 2 * rows), (2, 2 * rows)],
        [(2 * n_early, width)],
        "early_scores",
        *(vmem(linear[q]) for q in order),
        x_high,
        x_low,
        quad,
        cost=LIGHT,
    )
    tails = [vmem(swap(after(tail, early), "dp", 2)) for tail in tails]
    (part,) = score_call(
        functools.partial(head_kernel, n),
        [(n_late, 2 * rows)],
        [(2 * n_late, head * LANES)],
        "late_head",
        *heads,
        x_high,
        x_low,
        quad_scores(late, "late_quad", LIGHT),
        cost=LIGHT,
    )
    last, stats = score_call(
        functools.partial(last_kernel, n),
        [(n_late, 2 * rows), (2, 2, rows)],
        [(2 * n_late, width - head * LANES)],
        "last_scores",
        *tails,
        x_high,
        x_low,
        part,
        early_stats,
    )
    stats = merge([stats, swap(stats, "dp", 1)[::-1]])
    stats = merge([stats] + [swap(stats, "comp", q) for q in range(1, lax.axis_size("comp"))])

    *first, resp = first_moments(early, last, stats, x_high, x_low, n)
    second = second_moments(resp, s_high, s_low, n)
    place = {q: i for i, q in enumerate(order + late)}
    first, second = ([parts[place[q]] for q in range(planes)] for parts in (first, second))
    sums = scatter_planes(first, second)

    total_comps = n * lax.axis_size("dp") * lax.axis_size("comp")
    total_rows = embeddings.shape[0] * lax.axis_size("dp")
    scale = 0.6 * (total_comps / total_rows)
    return update(scale, comp_means, comp_variances, comp_mass, *sums)


def solution(mesh):
    placed = (P("dp", None), P(("comp", "dp"), None), P(("comp", "dp"), None), P(("comp", "dp")))
    return jax.shard_map(
        per_device,
        mesh=mesh,
        in_specs=placed,
        out_specs=(P(("comp", "dp"), None), P(("comp", "dp"), None), P(("comp", "dp"))),
        check_vma=False,
    )
```

```python
import functools

import jax
import jax.numpy as jnp
from jax import lax
from jax.experimental import pallas as pl
from jax.experimental.pallas import tpu as pltpu
from jax.sharding import PartitionSpec as P

F32 = jnp.float32
BF16 = jnp.bfloat16
LANES = 128
HEAVY = pl.CostEstimate(flops=10**10, bytes_accessed=10**8, transcendentals=0)
LIGHT = pl.CostEstimate(flops=10**8, bytes_accessed=10**6, transcendentals=0)
ACROSS = (((1,), (1,)), ((), ()))
WITHIN = (((1,), (0,)), ((), ()))


def params(megabytes):
    return pltpu.CompilerParams(vmem_limit_bytes=megabytes * 1024 * 1024)


def split(value):
    high = value.astype(BF16)
    return high, (value - high.astype(F32)).astype(BF16)


def diagonal(rows, columns):
    shape = (rows, columns)
    return lax.broadcasted_iota(jnp.int32, shape, 0) == lax.broadcasted_iota(jnp.int32, shape, 1)


def to_row(column, lanes):
    return jnp.sum(jnp.where(diagonal(column.shape[0], lanes), column, 0.0), axis=0, keepdims=True)


def to_column(row, rows):
    return jnp.sum(jnp.where(diagonal(rows, row.shape[1]), row, 0.0), axis=1, keepdims=True)


def coefficient_kernel(
    means_hbm, variances_hbm, mass_hbm, pack_ref, means_ref, variances_ref, mass_ref, sems
):
    sources = (variances_hbm, means_hbm, mass_hbm)
    targets = (variances_ref, means_ref, mass_ref)
    copies = [pltpu.make_async_copy(s, t, sems.at[i]) for i, (s, t) in enumerate(zip(sources, targets))]
    for copy in copies:
        copy.start()
    for copy in copies:
        copy.wait()
    n, width = means_ref.shape
    means, variances = means_ref[...], variances_ref[...]
    mean_prec = means * (1.0 / variances)
    sums = jnp.sum(jnp.log(variances) + means * mean_prec, axis=1, keepdims=True)
    offset = to_column(jnp.log(mass_ref[...]), n) - 0.5 * sums
    for c in range(width // LANES):
        pack_ref[c * n : (c + 1) * n, :] = mean_prec[:, c * LANES : (c + 1) * LANES]
    pack_ref[width // LANES * n :, :] = jnp.broadcast_to(to_row(offset, LANES), (8, LANES))


def coefficients(means, variances, mass):
    n, width = means.shape
    operands = (means, variances, mass.reshape(1, n))
    return pl.pallas_call(
        coefficient_kernel,
        in_specs=[pl.BlockSpec(memory_space=pl.ANY)] * 3,
        out_shape=jax.ShapeDtypeStruct((width // LANES * n + 8, LANES), F32),
        scratch_shapes=[
            pltpu.VMEM((n, width), F32),
            pltpu.VMEM((n, width), F32),
            pltpu.VMEM((1, n), F32),
            pltpu.SemaphoreType.DMA((3,)),
        ],
        cost_estimate=HEAVY,
        compiler_params=params(16),
        name="coefficients",
    )(*(pltpu.with_memory_space_constraint(x, pltpu.HBM) for x in operands))


def halves_kernel(own_ref, other_ref, xh_ref, xl_ref, sh_ref, sl_ref):
    def put(block):
        xh_ref[...], xl_ref[...] = split(block)
        sh_ref[...], sl_ref[...] = split(block * block)

    first = pl.program_id(0) < pl.num_programs(0) // 2

    @pl.when(first)
    def _():
        put(own_ref[...])

    @pl.when(jnp.logical_not(first))
    def _():
        put(other_ref[...])


def halves(own, other):
    rows, width = own.shape
    tile = min(256, rows)
    steps = rows // tile
    out = jax.ShapeDtypeStruct((2 * rows, width), BF16)
    return pl.pallas_call(
        halves_kernel,
        grid=(2 * steps,),
        in_specs=[
            pl.BlockSpec((tile, width), lambda i: (jnp.minimum(i, steps - 1), 0)),
            pl.BlockSpec((tile, width), lambda i: (jnp.maximum(i - steps, 0), 0)),
        ],
        out_specs=[pl.BlockSpec((tile, width), lambda i: (i, 0))] * 4,
        out_shape=[out] * 4,
        cost_estimate=HEAVY,
        compiler_params=params(16),
        name="halves",
    )(own, other)


def load_packs(packs, weights, n):
    comps, tiles = n * len(packs), weights.shape[1] // LANES
    for q, pack in enumerate(packs):
        for c in range(tiles):
            lanes = slice(c * LANES, (c + 1) * LANES)
            high, low = split(pack[c * n : (c + 1) * n, :])
            weights[q * n : (q + 1) * n, lanes] = high
            weights[comps + q * n : comps + (q + 1) * n, lanes] = low
    if packs[0].shape[0] == tiles * n:
        return None
    return jnp.concatenate([to_column(pack[tiles * n : tiles * n + 1, :], n) for pack in packs])


def load_variances(variances, weights, n):
    comps = n * len(variances)
    for q, ref in enumerate(variances):
        high, low = split(-0.5 * (1.0 / ref[...]))
        weights[q * n : (q + 1) * n, :] = high
        weights[comps + q * n : comps + (q + 1) * n, :] = low


def product(weights, high, low, dims):
    comps = weights.shape[0] // 2
    both = lax.dot_general(weights, high, dims, preferred_element_type=F32)
    rest = lax.dot_general(weights[:comps], low, dims, preferred_element_type=F32)
    return both[:comps] + (both[comps:] + rest)


def row_tiles(rows, tile=256):
    tile = min(tile, rows)
    return [slice(i, i + tile) for i in range(0, rows, tile)]


def quad_kernel(n, *refs):
    *variances, high_ref, low_ref, out_ref, weights = refs
    load_variances(variances, weights, n)
    for tile in row_tiles(high_ref.shape[0]):
        out_ref[:, tile] = product(weights[...], high_ref[tile, :], low_ref[tile, :], ACROSS)


def stats_of(scores):
    peak = jnp.max(scores, axis=0, keepdims=True)
    return peak, jnp.sum(jnp.exp(scores - peak), axis=0, keepdims=True)


def joined(one, other):
    peak = jnp.maximum(one[0], other[0])
    return peak, one[1] * jnp.exp(one[0] - peak) + other[1] * jnp.exp(other[0] - peak)


def early_kernel(n, *refs):
    *linear, high_ref, low_ref, quad_ref, out_ref, stats_ref, weights = refs
    offset = load_packs(linear, weights, n)
    for tile in row_tiles(high_ref.shape[0]):
        scores = product(weights[...], high_ref[tile, :], low_ref[tile, :], ACROSS)
        scores = quad_ref[:, tile] + scores + offset
        out_ref[:, tile] = scores
        stats_ref[0:1, tile], stats_ref[1:2, tile] = stats_of(scores)


def half_tiles(half):
    for block in range(2):
        for part in row_tiles(half):
            yield slice(block * half + part.start, block * half + part.stop), block, part


def head_kernel(n, *refs):
    *linear, high_ref, low_ref, quad_ref, out_ref, weights = refs
    load_packs(linear, weights, n)
    columns = slice(0, weights.shape[1])
    for tile in row_tiles(high_ref.shape[0]):
        scores = product(weights[...], high_ref[tile, columns], low_ref[tile, columns], ACROSS)
        out_ref[:, tile] = quad_ref[:, tile] + scores


def last_kernel(n, *refs):
    *linear, high_ref, low_ref, quad_ref, early_ref, out_ref, stats_ref, weights = refs
    offset = load_packs(linear, weights, n)
    columns = slice(high_ref.shape[1] - weights.shape[1], high_ref.shape[1])
    for tile, block, part in half_tiles(stats_ref.shape[2]):
        scores = product(weights[...], high_ref[tile, columns], low_ref[tile, columns], ACROSS)
        scores = quad_ref[:, tile] + scores + offset
        out_ref[:, tile] = scores
        early = early_ref[0:1, tile], early_ref[1:2, tile]
        peak, total = joined(stats_of(scores), early)
        stats_ref[block, 0:1, part] = peak
        stats_ref[block, 1:2, part] = total


def score_call(body, out_shape, scratch, name, *operands, cost=None):
    return pl.pallas_call(
        body,
        out_shape=[jax.ShapeDtypeStruct(shape, F32) for shape in out_shape],
        scratch_shapes=[pltpu.VMEM(shape, BF16) for shape in scratch],
        cost_estimate=cost or HEAVY,
        compiler_params=params(24),
        name=name,
    )(*operands)


def moment_tiles(resp_ref, high_ref, low_ref, packs, n):
    for c in range(0, high_ref.shape[1], 2 * LANES):
        columns = slice(c, c + 2 * LANES)
        total = product(resp_ref[...], high_ref[:, columns], low_ref[:, columns], WITHIN)
        for q, pack in enumerate(packs):
            for k in range(2):
                place = (c // LANES + k) * n
                pack[place : place + n, :] = total[q * n : (q + 1) * n, k * LANES : (k + 1) * LANES]


def first_kernel(n, early_ref, late_ref, stats_ref, high_ref, low_ref, *refs):
    *packs, resp_ref = refs
    comps = resp_ref.shape[0] // 2
    counts = jnp.zeros((comps, LANES), F32)
    for tile, block, part in half_tiles(stats_ref.shape[2]):
        peak, total = stats_ref[block, 0:1, part], stats_ref[block, 1:2, part]
        scores = jnp.concatenate([early_ref[:, tile], late_ref[:, tile]])
        resp = jnp.exp(scores - peak) * (1.0 / total)
        resp_ref[:comps, tile], resp_ref[comps:, tile] = split(resp)
        counts += sum(resp[:, c : c + LANES] for c in range(0, resp.shape[1], LANES))
    moment_tiles(resp_ref, high_ref, low_ref, packs, n)
    column = jnp.sum(counts, axis=1, keepdims=True)
    for q, pack in enumerate(packs):
        row = to_row(column[q * n : (q + 1) * n], LANES)
        pack[-8:, :] = jnp.broadcast_to(row, (8, LANES))


def first_moments(early, late, stats, high, low, n):
    rows, width = high.shape
    comps = early.shape[0] + late.shape[0]
    pack = jax.ShapeDtypeStruct((width // LANES * n + 8, LANES), F32)
    return pl.pallas_call(
        functools.partial(first_kernel, n),
        out_shape=[pack] * (comps // n) + [jax.ShapeDtypeStruct((2 * comps, rows), BF16)],
        cost_estimate=HEAVY,
        compiler_params=params(24),
        name="first_moments",
    )(early, late, stats, high, low)


def second_kernel(n, resp_ref, high_ref, low_ref, *packs):
    moment_tiles(resp_ref, high_ref, low_ref, packs, n)


def second_moments(resp, high, low, n):
    pack = jax.ShapeDtypeStruct((high.shape[1] // LANES * n, LANES), F32)
    return pl.pallas_call(
        functools.partial(second_kernel, n),
        out_shape=[pack] * (resp.shape[0] // 2 // n),
        cost_estimate=HEAVY,
        compiler_params=params(24),
        name="second_moments",
    )(resp, high, low)


def update_kernel(
    scale,
    means_ref,
    variances_ref,
    mass_ref,
    first_ref,
    second_ref,
    near_first_ref,
    near_second_ref,
    new_means_ref,
    new_variances_ref,
    new_mass_ref,
):
    n, width = means_ref.shape
    tiles = width // LANES * n
    row = first_ref[tiles : tiles + 1, :n] + near_first_ref[tiles : tiles + 1, :n]
    new_row = 0.4 * mass_ref[...] + scale * row
    new_mass_ref[...] = new_row
    inverse = 1.0 / to_column(new_row, n)
    kept = 0.4 * to_column(mass_ref[...], n)
    for c in range(width // LANES):
        lanes, tile = slice(c * LANES, (c + 1) * LANES), slice(c * n, (c + 1) * n)
        means, variances = means_ref[:, lanes], variances_ref[:, lanes]
        first = first_ref[tile, :] + near_first_ref[tile, :]
        second = second_ref[tile, :] + near_second_ref[tile, :]
        new_means = (kept * means + scale * first) * inverse
        new_means_ref[:, lanes] = new_means
        second_moment = kept * (variances + means * means) + scale * second
        new_variances_ref[:, lanes] = second_moment * inverse - new_means * new_means


def update(scale, means, variances, mass, *sums):
    n = mass.shape[0]
    block = jax.ShapeDtypeStruct(means.shape, F32)
    new_means, new_variances, new_mass = pl.pallas_call(
        functools.partial(update_kernel, scale),
        out_shape=(block, block, jax.ShapeDtypeStruct((1, n), F32)),
        cost_estimate=HEAVY,
        compiler_params=params(16),
        name="update",
    )(means, variances, mass.reshape(1, n), *sums)
    return new_means, new_variances, new_mass.reshape(n)


def swap(value, axis, bit):
    size = lax.axis_size(axis)
    return lax.ppermute(value, axis, [(i, i ^ bit) for i in range(size)])


def vmem(value):
    return pltpu.with_memory_space_constraint(value, pltpu.VMEM)


def after(value, *others):
    return lax.optimization_barrier((value, *others))[0]


def gather_early(piece):
    bit = lax.axis_size("dp") // 4
    held = {0: piece}
    while bit > 1:
        held.update({q ^ bit: swap(value, "dp", 2 * bit) for q, value in held.items()})
        bit //= 2
    held[1] = swap(piece, "dp", 2)
    return held


def scatter_planes(first, second):
    held = [dict(enumerate(parts)) for parts in (first, second)]
    totals, near = [[parts.pop(0)] for parts in held], []
    planes, bit = len(first), 1
    while bit < planes:
        ready = []
        for parts in held:
            for q in sorted((q for q in parts if q & bit and q != bit), reverse=True):
                parts[q ^ bit] = after(parts[q ^ bit], *ready) + swap(parts.pop(q), "dp", 2 * bit)
                ready = [parts[q ^ bit]]
        for total, parts in zip(totals, held):
            part = swap(after(parts.pop(bit), *ready), "dp", 2 * bit)
            (near if bit == 1 else total).append(part)
        bit *= 2
    one, other, *near = lax.optimization_barrier((sum(totals[0][1:], totals[0][0]), totals[1][0], *near))
    return one, sum(totals[1][1:], other), *near


def merge(stats):
    peak = functools.reduce(jnp.maximum, [s[:, 0] for s in stats])
    total = sum(s[:, 1] * jnp.exp(s[:, 0] - peak) for s in stats)
    return jnp.stack([peak, total], axis=1)


def per_device(embeddings, comp_means, comp_variances, comp_mass):
    n = comp_means.shape[0]
    rows, width = embeddings.shape
    planes = lax.axis_size("dp") // 2
    variances = gather_early(comp_variances)
    linear = gather_early(coefficients(comp_means, comp_variances, comp_mass))
    other = swap(embeddings, "dp", 1)
    order = sorted(linear)
    late = [q for q in range(planes) if q not in linear]
    x_high, x_low, s_high, s_low = halves(embeddings, other)
    for q in late:
        variances[q] = swap(after(variances[q ^ 1], x_high), "dp", 2)
    n_early, n_late = n * len(order), n * len(late)

    def quad_scores(group, name, cost=None):
        comps = n * len(group)
        operands = (*(vmem(variances[q]) for q in group), s_high, s_low)
        body = functools.partial(quad_kernel, n)
        return score_call(body, [(comps, 2 * rows)], [(2 * comps, width)], name, *operands, cost=cost)[0]

    quad = quad_scores(order, "early_quad")
    head = width // LANES * 2 // 3
    heads, tails = [], []
    for q in late:
        source = after(linear[q ^ 1], quad)
        heads.append(vmem(swap(source[: head * n], "dp", 2)))
        tails.append(source[head * n :])
    early, early_stats = score_call(
        functools.partial(early_kernel, n),
        [(n_early, 2 * rows), (2, 2 * rows)],
        [(2 * n_early, width)],
        "early_scores",
        *(vmem(linear[q]) for q in order),
        x_high,
        x_low,
        quad,
        cost=LIGHT,
    )
    tails = [vmem(swap(after(tail, early), "dp", 2)) for tail in tails]
    (part,) = score_call(
        functools.partial(head_kernel, n),
        [(n_late, 2 * rows)],
        [(2 * n_late, head * LANES)],
        "late_head",
        *heads,
        x_high,
        x_low,
        quad_scores(late, "late_quad", LIGHT),
        cost=LIGHT,
    )
    last, stats = score_call(
        functools.partial(last_kernel, n),
        [(n_late, 2 * rows), (2, 2, rows)],
        [(2 * n_late, width - head * LANES)],
        "last_scores",
        *tails,
        x_high,
        x_low,
        part,
        early_stats,
    )
    stats = merge([stats, swap(stats, "dp", 1)[::-1]])
    stats = merge([stats] + [swap(stats, "comp", q) for q in range(1, lax.axis_size("comp"))])

    *first, resp = first_moments(early, last, stats, x_high, x_low, n)
    second = second_moments(resp, s_high, s_low, n)
    place = {q: i for i, q in enumerate(order + late)}
    first, second = ([parts[place[q]] for q in range(planes)] for parts in (first, second))
    sums = scatter_planes(first, second)

    total_comps = n * lax.axis_size("dp") * lax.axis_size("comp")
    total_rows = embeddings.shape[0] * lax.axis_size("dp")
    scale = 0.6 * (total_comps / total_rows)
    return update(scale, comp_means, comp_variances, comp_mass, *sums)


def solution(mesh):
    placed = (P("dp", None), P(("comp", "dp"), None), P(("comp", "dp"), None), P(("comp", "dp")))
    return jax.shard_map(
        per_device,
        mesh=mesh,
        in_specs=placed,
        out_specs=(P(("comp", "dp"), None), P(("comp", "dp"), None), P(("comp", "dp"))),
        check_vma=False,
    )
```

```python
import functools

import jax
import jax.numpy as jnp
from jax import lax
from jax.experimental import pallas as pl
from jax.experimental.pallas import tpu as pltpu
from jax.sharding import PartitionSpec as P

F32 = jnp.float32
BF16 = jnp.bfloat16
LANES = 128
HEAVY = pl.CostEstimate(flops=10**10, bytes_accessed=10**8, transcendentals=0)
LIGHT = pl.CostEstimate(flops=10**8, bytes_accessed=10**6, transcendentals=0)
ACROSS = (((1,), (1,)), ((), ()))
WITHIN = (((1,), (0,)), ((), ()))


def params(megabytes):
    return pltpu.CompilerParams(vmem_limit_bytes=megabytes * 1024 * 1024)


def split(value):
    high = value.astype(BF16)
    return high, (value - high.astype(F32)).astype(BF16)


def diagonal(rows, columns):
    shape = (rows, columns)
    return lax.broadcasted_iota(jnp.int32, shape, 0) == lax.broadcasted_iota(jnp.int32, shape, 1)


def to_row(column, lanes):
    return jnp.sum(jnp.where(diagonal(column.shape[0], lanes), column, 0.0), axis=0, keepdims=True)


def to_column(row, rows):
    return jnp.sum(jnp.where(diagonal(rows, row.shape[1]), row, 0.0), axis=1, keepdims=True)


def coefficient_kernel(
    means_hbm, variances_hbm, mass_hbm, pack_ref, means_ref, variances_ref, mass_ref, sems
):
    sources = (variances_hbm, means_hbm, mass_hbm)
    targets = (variances_ref, means_ref, mass_ref)
    copies = [pltpu.make_async_copy(s, t, sems.at[i]) for i, (s, t) in enumerate(zip(sources, targets))]
    for copy in copies:
        copy.start()
    for copy in copies:
        copy.wait()
    n, width = means_ref.shape
    means, variances = means_ref[...], variances_ref[...]
    mean_prec = means * (1.0 / variances)
    sums = jnp.sum(jnp.log(variances) + means * mean_prec, axis=1, keepdims=True)
    offset = to_column(jnp.log(mass_ref[...]), n) - 0.5 * sums
    for c in range(width // LANES):
        pack_ref[c * n : (c + 1) * n, :] = mean_prec[:, c * LANES : (c + 1) * LANES]
    pack_ref[width // LANES * n :, :] = jnp.broadcast_to(to_row(offset, LANES), (8, LANES))


def coefficients(means, variances, mass):
    n, width = means.shape
    operands = (means, variances, mass.reshape(1, n))
    return pl.pallas_call(
        coefficient_kernel,
        in_specs=[pl.BlockSpec(memory_space=pl.ANY)] * 3,
        out_shape=jax.ShapeDtypeStruct((width // LANES * n + 8, LANES), F32),
        scratch_shapes=[
            pltpu.VMEM((n, width), F32),
            pltpu.VMEM((n, width), F32),
            pltpu.VMEM((1, n), F32),
            pltpu.SemaphoreType.DMA((3,)),
        ],
        cost_estimate=HEAVY,
        compiler_params=params(16),
        name="coefficients",
    )(*(pltpu.with_memory_space_constraint(x, pltpu.HBM) for x in operands))


def halves_kernel(own_ref, other_ref, xh_ref, xl_ref, sh_ref, sl_ref):
    def put(block):
        xh_ref[...], xl_ref[...] = split(block)
        sh_ref[...], sl_ref[...] = split(block * block)

    first = pl.program_id(0) < pl.num_programs(0) // 2

    @pl.when(first)
    def _():
        put(own_ref[...])

    @pl.when(jnp.logical_not(first))
    def _():
        put(other_ref[...])


def halves(own, other):
    rows, width = own.shape
    tile = min(256, rows)
    steps = rows // tile
    out = jax.ShapeDtypeStruct((2 * rows, width), BF16)
    return pl.pallas_call(
        halves_kernel,
        grid=(2 * steps,),
        in_specs=[
            pl.BlockSpec((tile, width), lambda i: (jnp.minimum(i, steps - 1), 0)),
            pl.BlockSpec((tile, width), lambda i: (jnp.maximum(i - steps, 0), 0)),
        ],
        out_specs=[pl.BlockSpec((tile, width), lambda i: (i, 0))] * 4,
        out_shape=[out] * 4,
        cost_estimate=HEAVY,
        compiler_params=params(16),
        name="halves",
    )(own, other)


def load_packs(packs, weights, n):
    comps, tiles = n * len(packs), weights.shape[1] // LANES
    for q, pack in enumerate(packs):
        for c in range(tiles):
            lanes = slice(c * LANES, (c + 1) * LANES)
            high, low = split(pack[c * n : (c + 1) * n, :])
            weights[q * n : (q + 1) * n, lanes] = high
            weights[comps + q * n : comps + (q + 1) * n, lanes] = low
    if packs[0].shape[0] == tiles * n:
        return None
    return jnp.concatenate([to_column(pack[tiles * n : tiles * n + 1, :], n) for pack in packs])


def load_variances(variances, weights, n):
    comps = n * len(variances)
    for q, ref in enumerate(variances):
        high, low = split(-0.5 * (1.0 / ref[...]))
        weights[q * n : (q + 1) * n, :] = high
        weights[comps + q * n : comps + (q + 1) * n, :] = low


def product(weights, high, low, dims):
    comps = weights.shape[0] // 2
    both = lax.dot_general(weights, high, dims, preferred_element_type=F32)
    rest = lax.dot_general(weights[:comps], low, dims, preferred_element_type=F32)
    return both[:comps] + (both[comps:] + rest)


def row_tiles(rows, tile=256):
    tile = min(tile, rows)
    return [slice(i, i + tile) for i in range(0, rows, tile)]


def quad_kernel(n, *refs):
    *variances, high_ref, low_ref, out_ref, weights = refs
    load_variances(variances, weights, n)
    for tile in row_tiles(high_ref.shape[0]):
        out_ref[:, tile] = product(weights[...], high_ref[tile, :], low_ref[tile, :], ACROSS)


def stats_of(scores):
    peak = jnp.max(scores, axis=0, keepdims=True)
    return peak, jnp.sum(jnp.exp(scores - peak), axis=0, keepdims=True)


def joined(one, other):
    peak = jnp.maximum(one[0], other[0])
    return peak, one[1] * jnp.exp(one[0] - peak) + other[1] * jnp.exp(other[0] - peak)


def early_kernel(n, *refs):
    *linear, high_ref, low_ref, quad_ref, out_ref, stats_ref, weights = refs
    offset = load_packs(linear, weights, n)
    for tile in row_tiles(high_ref.shape[0]):
        scores = product(weights[...], high_ref[tile, :], low_ref[tile, :], ACROSS)
        scores = quad_ref[:, tile] + scores + offset
        out_ref[:, tile] = scores
        stats_ref[0:1, tile], stats_ref[1:2, tile] = stats_of(scores)


def half_tiles(half):
    for block in range(2):
        for part in row_tiles(half):
            yield slice(block * half + part.start, block * half + part.stop), block, part


def head_kernel(n, *refs):
    *linear, high_ref, low_ref, quad_ref, out_ref, weights = refs
    load_packs(linear, weights, n)
    columns = slice(0, weights.shape[1])
    for tile in row_tiles(high_ref.shape[0]):
        scores = product(weights[...], high_ref[tile, columns], low_ref[tile, columns], ACROSS)
        out_ref[:, tile] = quad_ref[:, tile] + scores


def last_kernel(n, *refs):
    *linear, high_ref, low_ref, quad_ref, early_ref, out_ref, stats_ref, weights = refs
    offset = load_packs(linear, weights, n)
    columns = slice(high_ref.shape[1] - weights.shape[1], high_ref.shape[1])
    for tile, block, part in half_tiles(stats_ref.shape[2]):
        scores = product(weights[...], high_ref[tile, columns], low_ref[tile, columns], ACROSS)
        scores = quad_ref[:, tile] + scores + offset
        out_ref[:, tile] = scores
        early = early_ref[0:1, tile], early_ref[1:2, tile]
        peak, total = joined(stats_of(scores), early)
        stats_ref[block, 0:1, part] = peak
        stats_ref[block, 1:2, part] = total


def score_call(body, out_shape, scratch, name, *operands, cost=None):
    return pl.pallas_call(
        body,
        out_shape=[jax.ShapeDtypeStruct(shape, F32) for shape in out_shape],
        scratch_shapes=[pltpu.VMEM(shape, BF16) for shape in scratch],
        cost_estimate=cost or HEAVY,
        compiler_params=params(24),
        name=name,
    )(*operands)


def moment_tiles(resp_ref, high_ref, low_ref, packs, n, rows=slice(None), add=False):
    for c in range(0, high_ref.shape[1], 2 * LANES):
        columns = slice(c, c + 2 * LANES)
        total = product(resp_ref[:, rows], high_ref[rows, columns], low_ref[rows, columns], WITHIN)
        for q, pack in enumerate(packs):
            for k in range(2):
                tile = slice((c // LANES + k) * n, (c // LANES + k + 1) * n)
                part = total[q * n : (q + 1) * n, k * LANES : (k + 1) * LANES]
                pack[tile, :] = pack[tile, :] + part if add else part


def first_kernel(n, sets, early_ref, late_ref, *refs):
    stats, (high_ref, low_ref, *packs, resp_ref) = refs[:sets], refs[sets:]
    comps = resp_ref.shape[0] // 2
    half = stats[0].shape[2]
    counts = jnp.zeros((comps, LANES), F32)
    for block in range(2):
        for part in row_tiles(half):
            tile = slice(block * half + part.start, block * half + part.stop)
            parts = [(ref[block, 0:1, part], ref[block, 1:2, part]) for ref in stats]
            peak = functools.reduce(jnp.maximum, [p for p, _ in parts])
            total = sum(t * jnp.exp(p - peak) for p, t in parts)
            scores = jnp.concatenate([early_ref[:, tile], late_ref[:, tile]])
            resp = jnp.exp(scores - peak) * (1.0 / total)
            resp_ref[:comps, tile], resp_ref[comps:, tile] = split(resp)
            counts += sum(resp[:, c : c + LANES] for c in range(0, resp.shape[1], LANES))
        rows = slice(block * half, (block + 1) * half)
        moment_tiles(resp_ref, high_ref, low_ref, packs, n, rows, block == 1)
    column = jnp.sum(counts, axis=1, keepdims=True)
    for q, pack in enumerate(packs):
        row = to_row(column[q * n : (q + 1) * n], LANES)
        pack[-8:, :] = jnp.broadcast_to(row, (8, LANES))


def first_moments(early, late, stats, high, low, n):
    rows, width = high.shape
    comps = early.shape[0] + late.shape[0]
    pack = jax.ShapeDtypeStruct((width // LANES * n + 8, LANES), F32)
    return pl.pallas_call(
        functools.partial(first_kernel, n, len(stats)),
        out_shape=[pack] * (comps // n) + [jax.ShapeDtypeStruct((2 * comps, rows), BF16)],
        cost_estimate=HEAVY,
        compiler_params=params(24),
        name="first_moments",
    )(early, late, *stats, high, low)


def second_kernel(n, resp_ref, high_ref, low_ref, *packs):
    moment_tiles(resp_ref, high_ref, low_ref, packs, n)


def second_moments(resp, high, low, n):
    pack = jax.ShapeDtypeStruct((high.shape[1] // LANES * n, LANES), F32)
    return pl.pallas_call(
        functools.partial(second_kernel, n),
        out_shape=[pack] * (resp.shape[0] // 2 // n),
        cost_estimate=HEAVY,
        compiler_params=params(24),
        name="second_moments",
    )(resp, high, low)


def update_kernel(
    scale,
    means_ref,
    variances_ref,
    mass_ref,
    first_ref,
    second_ref,
    near_first_ref,
    near_second_ref,
    new_means_ref,
    new_variances_ref,
    new_mass_ref,
):
    n, width = means_ref.shape
    tiles = width // LANES * n
    row = first_ref[tiles : tiles + 1, :n] + near_first_ref[tiles : tiles + 1, :n]
    new_row = 0.4 * mass_ref[...] + scale * row
    new_mass_ref[...] = new_row
    inverse = 1.0 / to_column(new_row, n)
    kept = 0.4 * to_column(mass_ref[...], n)
    for c in range(width // LANES):
        lanes, tile = slice(c * LANES, (c + 1) * LANES), slice(c * n, (c + 1) * n)
        means, variances = means_ref[:, lanes], variances_ref[:, lanes]
        first = first_ref[tile, :] + near_first_ref[tile, :]
        second = second_ref[tile, :] + near_second_ref[tile, :]
        new_means = (kept * means + scale * first) * inverse
        new_means_ref[:, lanes] = new_means
        second_moment = kept * (variances + means * means) + scale * second
        new_variances_ref[:, lanes] = second_moment * inverse - new_means * new_means


def update(scale, means, variances, mass, *sums):
    n = mass.shape[0]
    block = jax.ShapeDtypeStruct(means.shape, F32)
    new_means, new_variances, new_mass = pl.pallas_call(
        functools.partial(update_kernel, scale),
        out_shape=(block, block, jax.ShapeDtypeStruct((1, n), F32)),
        cost_estimate=HEAVY,
        compiler_params=params(16),
        name="update",
    )(means, variances, mass.reshape(1, n), *sums)
    return new_means, new_variances, new_mass.reshape(n)


def swap(value, axis, bit):
    size = lax.axis_size(axis)
    return lax.ppermute(value, axis, [(i, i ^ bit) for i in range(size)])


def vmem(value):
    return pltpu.with_memory_space_constraint(value, pltpu.VMEM)


def after(value, *others):
    return lax.optimization_barrier((value, *others))[0]


def gather_early(piece):
    bit = lax.axis_size("dp") // 4
    held = {0: piece}
    while bit > 1:
        held.update({q ^ bit: swap(value, "dp", 2 * bit) for q, value in held.items()})
        bit //= 2
    held[1] = swap(piece, "dp", 2)
    return held


def scatter_planes(first, second):
    held = [dict(enumerate(parts)) for parts in (first, second)]
    totals, near = [[parts.pop(0)] for parts in held], []
    planes, bit = len(first), 1
    while bit < planes:
        ready = []
        for parts in held:
            for q in sorted((q for q in parts if q & bit and q != bit), reverse=True):
                parts[q ^ bit] = parts[q ^ bit] + swap(after(parts.pop(q), *ready), "dp", 2 * bit)
                ready = [parts[q ^ bit]]
        for total, parts in zip(totals, held):
            part = swap(after(parts.pop(bit), *ready), "dp", 2 * bit)
            (near if bit == 1 else total).append(part)
        bit *= 2
    return *lax.optimization_barrier(tuple(sum(t[1:], t[0]) for t in totals)), *near


def merge(stats):
    peak = functools.reduce(jnp.maximum, [s[:, 0] for s in stats])
    total = sum(s[:, 1] * jnp.exp(s[:, 0] - peak) for s in stats)
    return jnp.stack([peak, total], axis=1)


def per_device(embeddings, comp_means, comp_variances, comp_mass):
    n = comp_means.shape[0]
    rows, width = embeddings.shape
    planes = lax.axis_size("dp") // 2
    variances = gather_early(comp_variances)
    linear = gather_early(coefficients(comp_means, comp_variances, comp_mass))
    other = swap(embeddings, "dp", 1)
    order = sorted(linear)
    late = [q for q in range(planes) if q not in linear]
    x_high, x_low, s_high, s_low = halves(embeddings, other)
    for q in late:
        variances[q] = swap(after(variances[q ^ 1], x_high), "dp", 2)
    n_early, n_late = n * len(order), n * len(late)

    def quad_scores(group, name, cost=None):
        comps = n * len(group)
        operands = (*(vmem(variances[q]) for q in group), s_high, s_low)
        body = functools.partial(quad_kernel, n)
        return score_call(body, [(comps, 2 * rows)], [(2 * comps, width)], name, *operands, cost=cost)[0]

    quad = quad_scores(order, "early_quad")
    head = width // LANES * 2 // 3
    heads, tails = [], []
    for q in late:
        source = after(linear[q ^ 1], quad)
        heads.append(vmem(swap(source[: head * n], "dp", 2)))
        tails.append(source[head * n :])
    early, early_stats = score_call(
        functools.partial(early_kernel, n),
        [(n_early, 2 * rows), (2, 2 * rows)],
        [(2 * n_early, width)],
        "early_scores",
        *(vmem(linear[q]) for q in order),
        x_high,
        x_low,
        quad,
        cost=LIGHT,
    )
    tails = [vmem(swap(after(tail, early), "dp", 2)) for tail in tails]
    (part,) = score_call(
        functools.partial(head_kernel, n),
        [(n_late, 2 * rows)],
        [(2 * n_late, head * LANES)],
        "late_head",
        *heads,
        x_high,
        x_low,
        quad_scores(late, "late_quad", LIGHT),
        cost=LIGHT,
    )
    last, stats = score_call(
        functools.partial(last_kernel, n),
        [(n_late, 2 * rows), (2, 2, rows)],
        [(2 * n_late, width - head * LANES)],
        "last_scores",
        *tails,
        x_high,
        x_low,
        part,
        early_stats,
    )
    stats = merge([stats, swap(stats, "dp", 1)[::-1]])
    stats = [stats] + [swap(stats, "comp", q) for q in range(1, lax.axis_size("comp"))]

    *first, resp = first_moments(early, last, stats, x_high, x_low, n)
    second = second_moments(resp, s_high, s_low, n)
    place = {q: i for i, q in enumerate(order + late)}
    first, second = ([parts[place[q]] for q in range(planes)] for parts in (first, second))
    sums = scatter_planes(first, second)

    total_comps = n * lax.axis_size("dp") * lax.axis_size("comp")
    total_rows = embeddings.shape[0] * lax.axis_size("dp")
    scale = 0.6 * (total_comps / total_rows)
    return update(scale, comp_means, comp_variances, comp_mass, *sums)


def solution(mesh):
    placed = (P("dp", None), P(("comp", "dp"), None), P(("comp", "dp"), None), P(("comp", "dp")))
    return jax.shard_map(
        per_device,
        mesh=mesh,
        in_specs=placed,
        out_specs=(P(("comp", "dp"), None), P(("comp", "dp"), None), P(("comp", "dp"))),
        check_vma=False,
    )
```

```python
import functools

import jax
import jax.numpy as jnp
from jax import lax
from jax.experimental import pallas as pl
from jax.experimental.pallas import tpu as pltpu
from jax.sharding import PartitionSpec as P

F32 = jnp.float32
BF16 = jnp.bfloat16
LANES = 128
HEAVY = pl.CostEstimate(flops=10**10, bytes_accessed=10**8, transcendentals=0)
LIGHT = pl.CostEstimate(flops=10**8, bytes_accessed=10**6, transcendentals=0)
ACROSS = (((1,), (1,)), ((), ()))
WITHIN = (((1,), (0,)), ((), ()))


def params(megabytes):
    return pltpu.CompilerParams(vmem_limit_bytes=megabytes * 1024 * 1024)


def split(value):
    high = value.astype(BF16)
    return high, (value - high.astype(F32)).astype(BF16)


def diagonal(rows, columns):
    shape = (rows, columns)
    return lax.broadcasted_iota(jnp.int32, shape, 0) == lax.broadcasted_iota(jnp.int32, shape, 1)


def to_row(column, lanes):
    return jnp.sum(jnp.where(diagonal(column.shape[0], lanes), column, 0.0), axis=0, keepdims=True)


def to_column(row, rows):
    return jnp.sum(jnp.where(diagonal(rows, row.shape[1]), row, 0.0), axis=1, keepdims=True)


def coefficient_kernel(
    means_hbm, variances_hbm, mass_hbm, pack_ref, means_ref, variances_ref, mass_ref, sems
):
    sources = (variances_hbm, means_hbm, mass_hbm)
    targets = (variances_ref, means_ref, mass_ref)
    copies = [pltpu.make_async_copy(s, t, sems.at[i]) for i, (s, t) in enumerate(zip(sources, targets))]
    for copy in copies:
        copy.start()
    for copy in copies:
        copy.wait()
    n, width = means_ref.shape
    means, variances = means_ref[...], variances_ref[...]
    mean_prec = means * (1.0 / variances)
    sums = jnp.sum(jnp.log(variances) + means * mean_prec, axis=1, keepdims=True)
    offset = to_column(jnp.log(mass_ref[...]), n) - 0.5 * sums
    for c in range(width // LANES):
        pack_ref[c * n : (c + 1) * n, :] = mean_prec[:, c * LANES : (c + 1) * LANES]
    pack_ref[width // LANES * n :, :] = jnp.broadcast_to(to_row(offset, LANES), (8, LANES))


def coefficients(means, variances, mass):
    n, width = means.shape
    operands = (means, variances, mass.reshape(1, n))
    return pl.pallas_call(
        coefficient_kernel,
        in_specs=[pl.BlockSpec(memory_space=pl.ANY)] * 3,
        out_shape=jax.ShapeDtypeStruct((width // LANES * n + 8, LANES), F32),
        scratch_shapes=[
            pltpu.VMEM((n, width), F32),
            pltpu.VMEM((n, width), F32),
            pltpu.VMEM((1, n), F32),
            pltpu.SemaphoreType.DMA((3,)),
        ],
        cost_estimate=HEAVY,
        compiler_params=params(16),
        name="coefficients",
    )(*(pltpu.with_memory_space_constraint(x, pltpu.HBM) for x in operands))


def halves_kernel(own_ref, other_ref, xh_ref, xl_ref, sh_ref, sl_ref):
    def put(block):
        xh_ref[...], xl_ref[...] = split(block)
        sh_ref[...], sl_ref[...] = split(block * block)

    first = pl.program_id(0) < pl.num_programs(0) // 2

    @pl.when(first)
    def _():
        put(own_ref[...])

    @pl.when(jnp.logical_not(first))
    def _():
        put(other_ref[...])


def halves(own, other):
    rows, width = own.shape
    tile = min(256, rows)
    steps = rows // tile
    out = jax.ShapeDtypeStruct((2 * rows, width), BF16)
    return pl.pallas_call(
        halves_kernel,
        grid=(2 * steps,),
        in_specs=[
            pl.BlockSpec((tile, width), lambda i: (jnp.minimum(i, steps - 1), 0)),
            pl.BlockSpec((tile, width), lambda i: (jnp.maximum(i - steps, 0), 0)),
        ],
        out_specs=[pl.BlockSpec((tile, width), lambda i: (i, 0))] * 4,
        out_shape=[out] * 4,
        cost_estimate=HEAVY,
        compiler_params=params(16),
        name="halves",
    )(own, other)


def load_packs(packs, weights, n):
    comps, tiles = n * len(packs), weights.shape[1] // LANES
    for q, pack in enumerate(packs):
        for c in range(tiles):
            lanes = slice(c * LANES, (c + 1) * LANES)
            high, low = split(pack[c * n : (c + 1) * n, :])
            weights[q * n : (q + 1) * n, lanes] = high
            weights[comps + q * n : comps + (q + 1) * n, lanes] = low
    if packs[0].shape[0] == tiles * n:
        return None
    return jnp.concatenate([to_column(pack[tiles * n : tiles * n + 1, :], n) for pack in packs])


def load_variances(variances, weights, n):
    comps = n * len(variances)
    for q, ref in enumerate(variances):
        high, low = split(-0.5 * (1.0 / ref[...]))
        weights[q * n : (q + 1) * n, :] = high
        weights[comps + q * n : comps + (q + 1) * n, :] = low


def product(weights, high, low, dims):
    comps = weights.shape[0] // 2
    both = lax.dot_general(weights, high, dims, preferred_element_type=F32)
    rest = lax.dot_general(weights[:comps], low, dims, preferred_element_type=F32)
    return both[:comps] + (both[comps:] + rest)


def row_tiles(rows, tile=256):
    tile = min(tile, rows)
    return [slice(i, i + tile) for i in range(0, rows, tile)]


def quad_kernel(n, *refs):
    *variances, high_ref, low_ref, out_ref, weights = refs
    load_variances(variances, weights, n)
    for tile in row_tiles(high_ref.shape[0]):
        out_ref[:, tile] = product(weights[...], high_ref[tile, :], low_ref[tile, :], ACROSS)


def stats_of(scores):
    peak = jnp.max(scores, axis=0, keepdims=True)
    return peak, jnp.sum(jnp.exp(scores - peak), axis=0, keepdims=True)


def joined(one, other):
    peak = jnp.maximum(one[0], other[0])
    return peak, one[1] * jnp.exp(one[0] - peak) + other[1] * jnp.exp(other[0] - peak)


def early_kernel(n, *refs):
    *linear, high_ref, low_ref, quad_ref, out_ref, stats_ref, weights = refs
    offset = load_packs(linear, weights, n)
    for tile in row_tiles(high_ref.shape[0]):
        scores = product(weights[...], high_ref[tile, :], low_ref[tile, :], ACROSS)
        scores = quad_ref[:, tile] + scores + offset
        out_ref[:, tile] = scores
        stats_ref[0:1, tile], stats_ref[1:2, tile] = stats_of(scores)


def half_tiles(half):
    for block in range(2):
        for part in row_tiles(half):
            yield slice(block * half + part.start, block * half + part.stop), block, part


def head_kernel(n, *refs):
    *linear, high_ref, low_ref, quad_ref, out_ref, weights = refs
    load_packs(linear, weights, n)
    columns = slice(0, weights.shape[1])
    for tile in row_tiles(high_ref.shape[0]):
        scores = product(weights[...], high_ref[tile, columns], low_ref[tile, columns], ACROSS)
        out_ref[:, tile] = quad_ref[:, tile] + scores


def last_kernel(n, *refs):
    *linear, high_ref, low_ref, quad_ref, early_ref, out_ref, stats_ref, weights = refs
    offset = load_packs(linear, weights, n)
    columns = slice(high_ref.shape[1] - weights.shape[1], high_ref.shape[1])
    for tile, block, part in half_tiles(stats_ref.shape[2]):
        scores = product(weights[...], high_ref[tile, columns], low_ref[tile, columns], ACROSS)
        scores = quad_ref[:, tile] + scores + offset
        out_ref[:, tile] = scores
        early = early_ref[0:1, tile], early_ref[1:2, tile]
        peak, total = joined(stats_of(scores), early)
        stats_ref[block, 0:1, part] = peak
        stats_ref[block, 1:2, part] = total


def score_call(body, out_shape, scratch, name, *operands, cost=None):
    return pl.pallas_call(
        body,
        out_shape=[jax.ShapeDtypeStruct(shape, F32) for shape in out_shape],
        scratch_shapes=[pltpu.VMEM(shape, BF16) for shape in scratch],
        cost_estimate=cost or HEAVY,
        compiler_params=params(24),
        name=name,
    )(*operands)


def moment_tiles(resp_ref, high_ref, low_ref, packs, n, rows=slice(None), add=False):
    for c in range(0, high_ref.shape[1], 2 * LANES):
        columns = slice(c, c + 2 * LANES)
        total = product(resp_ref[:, rows], high_ref[rows, columns], low_ref[rows, columns], WITHIN)
        for q, pack in enumerate(packs):
            for k in range(2):
                tile = slice((c // LANES + k) * n, (c // LANES + k + 1) * n)
                part = total[q * n : (q + 1) * n, k * LANES : (k + 1) * LANES]
                pack[tile, :] = pack[tile, :] + part if add else part


def first_kernel(n, sets, early_ref, late_ref, *refs):
    stats, (high_ref, low_ref, *packs, resp_ref) = refs[:sets], refs[sets:]
    comps = resp_ref.shape[0] // 2
    half = stats[0].shape[2]
    counts = jnp.zeros((comps, LANES), F32)
    for block in range(2):
        for part in row_tiles(half):
            tile = slice(block * half + part.start, block * half + part.stop)
            parts = [(ref[block, 0:1, part], ref[block, 1:2, part]) for ref in stats]
            peak = functools.reduce(jnp.maximum, [p for p, _ in parts])
            total = sum(t * jnp.exp(p - peak) for p, t in parts)
            scores = jnp.concatenate([early_ref[:, tile], late_ref[:, tile]])
            resp = jnp.exp(scores - peak) * (1.0 / total)
            resp_ref[:comps, tile], resp_ref[comps:, tile] = split(resp)
            counts += sum(resp[:, c : c + LANES] for c in range(0, resp.shape[1], LANES))
        rows = slice(block * half, (block + 1) * half)
        moment_tiles(resp_ref, high_ref, low_ref, packs, n, rows, block == 1)
    column = jnp.sum(counts, axis=1, keepdims=True)
    for q, pack in enumerate(packs):
        row = to_row(column[q * n : (q + 1) * n], LANES)
        pack[-8:, :] = jnp.broadcast_to(row, (8, LANES))


def first_moments(early, late, stats, high, low, n):
    rows, width = high.shape
    comps = early.shape[0] + late.shape[0]
    pack = jax.ShapeDtypeStruct((width // LANES * n + 8, LANES), F32)
    return pl.pallas_call(
        functools.partial(first_kernel, n, len(stats)),
        out_shape=[pack] * (comps // n) + [jax.ShapeDtypeStruct((2 * comps, rows), BF16)],
        cost_estimate=HEAVY,
        compiler_params=params(24),
        name="first_moments",
    )(early, late, *stats, high, low)


def second_kernel(n, resp_ref, high_ref, low_ref, *packs):
    moment_tiles(resp_ref, high_ref, low_ref, packs, n)


def second_moments(resp, high, low, n):
    pack = jax.ShapeDtypeStruct((high.shape[1] // LANES * n, LANES), F32)
    return pl.pallas_call(
        functools.partial(second_kernel, n),
        out_shape=[pack] * (resp.shape[0] // 2 // n),
        cost_estimate=HEAVY,
        compiler_params=params(24),
        name="second_moments",
    )(resp, high, low)


def kept_kernel(
    means_hbm, variances_hbm, mass_hbm, first_ref, second_ref, means_ref, variances_ref, mass_ref, sems
):
    sources = (variances_hbm, means_hbm, mass_hbm)
    targets = (variances_ref, means_ref, mass_ref)
    copies = [pltpu.make_async_copy(s, t, sems.at[i]) for i, (s, t) in enumerate(zip(sources, targets))]
    for copy in copies:
        copy.start()
    for copy in copies:
        copy.wait()
    means = means_ref[...]
    kept = 0.4 * to_column(mass_ref[...], means.shape[0])
    first_ref[...] = kept * means
    second_ref[...] = kept * (variances_ref[...] + means * means)


def kept_moments(means, variances, mass, ready):
    n, width = means.shape
    operands = (means, variances, after(mass.reshape(1, n), ready))
    return pl.pallas_call(
        kept_kernel,
        in_specs=[pl.BlockSpec(memory_space=pl.ANY)] * 3,
        out_shape=[jax.ShapeDtypeStruct((n, width), F32)] * 2,
        scratch_shapes=[
            pltpu.VMEM((n, width), F32),
            pltpu.VMEM((n, width), F32),
            pltpu.VMEM((1, n), F32),
            pltpu.SemaphoreType.DMA((3,)),
        ],
        cost_estimate=HEAVY,
        compiler_params=params(16),
        name="kept_moments",
    )(*(pltpu.with_memory_space_constraint(x, pltpu.HBM) for x in operands))


def update_kernel(
    scale,
    kept_first_ref,
    kept_second_ref,
    mass_ref,
    first_ref,
    second_ref,
    near_first_ref,
    near_second_ref,
    new_means_ref,
    new_variances_ref,
    new_mass_ref,
):
    n, width = kept_first_ref.shape
    tiles = width // LANES * n
    row = first_ref[tiles : tiles + 1, :n] + near_first_ref[tiles : tiles + 1, :n]
    new_row = 0.4 * mass_ref[...] + scale * row
    new_mass_ref[...] = new_row
    inverse = 1.0 / to_column(new_row, n)
    for c in range(width // LANES):
        lanes, tile = slice(c * LANES, (c + 1) * LANES), slice(c * n, (c + 1) * n)
        first = first_ref[tile, :] + near_first_ref[tile, :]
        second = second_ref[tile, :] + near_second_ref[tile, :]
        new_means = (kept_first_ref[:, lanes] + scale * first) * inverse
        new_means_ref[:, lanes] = new_means
        second_moment = kept_second_ref[:, lanes] + scale * second
        new_variances_ref[:, lanes] = second_moment * inverse - new_means * new_means


def update(scale, kept, mass, *sums):
    n = mass.shape[0]
    block = jax.ShapeDtypeStruct(kept[0].shape, F32)
    new_means, new_variances, new_mass = pl.pallas_call(
        functools.partial(update_kernel, scale),
        out_shape=(block, block, jax.ShapeDtypeStruct((1, n), F32)),
        cost_estimate=HEAVY,
        compiler_params=params(16),
        name="update",
    )(*kept, mass.reshape(1, n), *sums)
    return new_means, new_variances, new_mass.reshape(n)


def swap(value, axis, bit):
    size = lax.axis_size(axis)
    return lax.ppermute(value, axis, [(i, i ^ bit) for i in range(size)])


def vmem(value):
    return pltpu.with_memory_space_constraint(value, pltpu.VMEM)


def after(value, *others):
    return lax.optimization_barrier((value, *others))[0]


def gather_early(piece):
    bit = lax.axis_size("dp") // 4
    held = {0: piece}
    while bit > 1:
        held.update({q ^ bit: swap(value, "dp", 2 * bit) for q, value in held.items()})
        bit //= 2
    held[1] = swap(piece, "dp", 2)
    return held


def scatter_planes(first, second, beside):
    held = [dict(enumerate(parts)) for parts in (first, second)]
    totals, near = [[parts.pop(0)] for parts in held], []
    planes, bit = len(first), 1
    while bit < planes:
        ready = []
        for parts in held:
            for q in sorted((q for q in parts if q & bit and q != bit), reverse=True):
                parts[q ^ bit] = parts[q ^ bit] + swap(after(parts.pop(q), *ready), "dp", 2 * bit)
                ready = [parts[q ^ bit]]
            if bit == 1 and parts is held[0]:
                made = beside(ready[0])
                held[0] = {q: after(part, made[0]) if q == 2 else part for q, part in parts.items()}
        for total, parts in zip(totals, held):
            part = swap(after(parts.pop(bit), *ready), "dp", 2 * bit)
            (near if bit == 1 else total).append(part)
        bit *= 2
    return made, *lax.optimization_barrier(tuple(sum(t[1:], t[0]) for t in totals)), *near


def merge(stats):
    peak = functools.reduce(jnp.maximum, [s[:, 0] for s in stats])
    total = sum(s[:, 1] * jnp.exp(s[:, 0] - peak) for s in stats)
    return jnp.stack([peak, total], axis=1)


def per_device(embeddings, comp_means, comp_variances, comp_mass):
    n = comp_means.shape[0]
    rows, width = embeddings.shape
    planes = lax.axis_size("dp") // 2
    variances = gather_early(comp_variances)
    linear = gather_early(coefficients(comp_means, comp_variances, comp_mass))
    other = swap(embeddings, "dp", 1)
    order = sorted(linear)
    late = [q for q in range(planes) if q not in linear]
    x_high, x_low, s_high, s_low = halves(embeddings, other)
    for q in late:
        variances[q] = swap(after(variances[q ^ 1], x_high), "dp", 2)
    n_early, n_late = n * len(order), n * len(late)

    def quad_scores(group, name, cost=None):
        comps = n * len(group)
        operands = (*(vmem(variances[q]) for q in group), s_high, s_low)
        body = functools.partial(quad_kernel, n)
        return score_call(body, [(comps, 2 * rows)], [(2 * comps, width)], name, *operands, cost=cost)[0]

    quad = quad_scores(order, "early_quad")
    head = width // LANES * 2 // 3
    heads, tails = [], []
    for q in late:
        source = after(linear[q ^ 1], quad)
        heads.append(vmem(swap(source[: head * n], "dp", 2)))
        tails.append(source[head * n :])
    early, early_stats = score_call(
        functools.partial(early_kernel, n),
        [(n_early, 2 * rows), (2, 2 * rows)],
        [(2 * n_early, width)],
        "early_scores",
        *(vmem(linear[q]) for q in order),
        x_high,
        x_low,
        quad,
        cost=LIGHT,
    )
    tails = [vmem(swap(after(tail, early), "dp", 2)) for tail in tails]
    (part,) = score_call(
        functools.partial(head_kernel, n),
        [(n_late, 2 * rows)],
        [(2 * n_late, head * LANES)],
        "late_head",
        *heads,
        x_high,
        x_low,
        quad_scores(late, "late_quad", LIGHT),
        cost=LIGHT,
    )
    last, stats = score_call(
        functools.partial(last_kernel, n),
        [(n_late, 2 * rows), (2, 2, rows)],
        [(2 * n_late, width - head * LANES)],
        "last_scores",
        *tails,
        x_high,
        x_low,
        part,
        early_stats,
    )
    stats = merge([stats, swap(stats, "dp", 1)[::-1]])
    stats = [stats] + [swap(stats, "comp", q) for q in range(1, lax.axis_size("comp"))]

    *first, resp = first_moments(early, last, stats, x_high, x_low, n)
    second = second_moments(resp, s_high, s_low, n)
    place = {q: i for i, q in enumerate(order + late)}
    first, second = ([parts[place[q]] for q in range(planes)] for parts in (first, second))
    olds = (comp_means, comp_variances, comp_mass)
    kept, *sums = scatter_planes(first, second, lambda ready: kept_moments(*olds, ready))

    total_comps = n * lax.axis_size("dp") * lax.axis_size("comp")
    total_rows = embeddings.shape[0] * lax.axis_size("dp")
    scale = 0.6 * (total_comps / total_rows)
    return update(scale, kept, comp_mass, *sums)


def solution(mesh):
    placed = (P("dp", None), P(("comp", "dp"), None), P(("comp", "dp"), None), P(("comp", "dp")))
    return jax.shard_map(
        per_device,
        mesh=mesh,
        in_specs=placed,
        out_specs=(P(("comp", "dp"), None), P(("comp", "dp"), None), P(("comp", "dp"))),
        check_vma=False,
    )
```

```python
import functools

import jax
import jax.numpy as jnp
from jax import lax
from jax.experimental import pallas as pl
from jax.experimental.pallas import tpu as pltpu
from jax.sharding import PartitionSpec as P

F32 = jnp.float32
BF16 = jnp.bfloat16
LANES = 128
HEAVY = pl.CostEstimate(flops=10**10, bytes_accessed=10**8, transcendentals=0)
LIGHT = pl.CostEstimate(flops=10**8, bytes_accessed=10**6, transcendentals=0)
ACROSS = (((1,), (1,)), ((), ()))
WITHIN = (((1,), (0,)), ((), ()))


def params(megabytes):
    return pltpu.CompilerParams(vmem_limit_bytes=megabytes * 1024 * 1024)


def split(value):
    high = value.astype(BF16)
    return high, (value - high.astype(F32)).astype(BF16)


def diagonal(rows, columns):
    shape = (rows, columns)
    return lax.broadcasted_iota(jnp.int32, shape, 0) == lax.broadcasted_iota(jnp.int32, shape, 1)


def to_row(column, lanes):
    return jnp.sum(jnp.where(diagonal(column.shape[0], lanes), column, 0.0), axis=0, keepdims=True)


def to_column(row, rows):
    return jnp.sum(jnp.where(diagonal(rows, row.shape[1]), row, 0.0), axis=1, keepdims=True)


def coefficient_kernel(
    means_hbm, variances_hbm, mass_hbm, pack_ref, means_ref, variances_ref, mass_ref, sems
):
    sources = (variances_hbm, means_hbm, mass_hbm)
    targets = (variances_ref, means_ref, mass_ref)
    copies = [pltpu.make_async_copy(s, t, sems.at[i]) for i, (s, t) in enumerate(zip(sources, targets))]
    for copy in copies:
        copy.start()
    for copy in copies:
        copy.wait()
    n, width = means_ref.shape
    means, variances = means_ref[...], variances_ref[...]
    mean_prec = means * (1.0 / variances)
    sums = jnp.sum(jnp.log(variances) + means * mean_prec, axis=1, keepdims=True)
    offset = to_column(jnp.log(mass_ref[...]), n) - 0.5 * sums
    for c in range(width // LANES):
        pack_ref[c * n : (c + 1) * n, :] = mean_prec[:, c * LANES : (c + 1) * LANES]
    pack_ref[width // LANES * n :, :] = jnp.broadcast_to(to_row(offset, LANES), (8, LANES))


def coefficients(means, variances, mass):
    n, width = means.shape
    operands = (means, variances, mass.reshape(1, n))
    return pl.pallas_call(
        coefficient_kernel,
        in_specs=[pl.BlockSpec(memory_space=pl.ANY)] * 3,
        out_shape=jax.ShapeDtypeStruct((width // LANES * n + 8, LANES), F32),
        scratch_shapes=[
            pltpu.VMEM((n, width), F32),
            pltpu.VMEM((n, width), F32),
            pltpu.VMEM((1, n), F32),
            pltpu.SemaphoreType.DMA((3,)),
        ],
        cost_estimate=HEAVY,
        compiler_params=params(16),
        name="coefficients",
    )(*(pltpu.with_memory_space_constraint(x, pltpu.HBM) for x in operands))


def halves_kernel(own_ref, other_ref, xh_ref, xl_ref, sh_ref, sl_ref):
    def put(block):
        xh_ref[...], xl_ref[...] = split(block)
        sh_ref[...], sl_ref[...] = split(block * block)

    first = pl.program_id(0) < pl.num_programs(0) // 2

    @pl.when(first)
    def _():
        put(own_ref[...])

    @pl.when(jnp.logical_not(first))
    def _():
        put(other_ref[...])


def halves(own, other):
    rows, width = own.shape
    tile = min(256, rows)
    steps = rows // tile
    out = jax.ShapeDtypeStruct((2 * rows, width), BF16)
    return pl.pallas_call(
        halves_kernel,
        grid=(2 * steps,),
        in_specs=[
            pl.BlockSpec((tile, width), lambda i: (jnp.minimum(i, steps - 1), 0)),
            pl.BlockSpec((tile, width), lambda i: (jnp.maximum(i - steps, 0), 0)),
        ],
        out_specs=[pl.BlockSpec((tile, width), lambda i: (i, 0))] * 4,
        out_shape=[out] * 4,
        cost_estimate=HEAVY,
        compiler_params=params(16),
        name="halves",
    )(own, other)


def load_packs(packs, weights, n):
    comps, tiles = n * len(packs), weights.shape[1] // LANES
    for q, pack in enumerate(packs):
        for c in range(tiles):
            lanes = slice(c * LANES, (c + 1) * LANES)
            high, low = split(pack[c * n : (c + 1) * n, :])
            weights[q * n : (q + 1) * n, lanes] = high
            weights[comps + q * n : comps + (q + 1) * n, lanes] = low
    if packs[0].shape[0] == tiles * n:
        return None
    return jnp.concatenate([to_column(pack[tiles * n : tiles * n + 1, :], n) for pack in packs])


def load_variances(variances, weights, n):
    comps = n * len(variances)
    for q, ref in enumerate(variances):
        high, low = split(-0.5 * (1.0 / ref[...]))
        weights[q * n : (q + 1) * n, :] = high
        weights[comps + q * n : comps + (q + 1) * n, :] = low


def product(weights, high, low, dims):
    comps = weights.shape[0] // 2
    both = lax.dot_general(weights, high, dims, preferred_element_type=F32)
    rest = lax.dot_general(weights[:comps], low, dims, preferred_element_type=F32)
    return both[:comps] + (both[comps:] + rest)


def row_tiles(rows, tile=256):
    tile = min(tile, rows)
    return [slice(i, i + tile) for i in range(0, rows, tile)]


def quad_kernel(n, *refs):
    *variances, high_ref, low_ref, out_ref, weights = refs
    load_variances(variances, weights, n)
    for tile in row_tiles(high_ref.shape[0]):
        out_ref[:, tile] = product(weights[...], high_ref[tile, :], low_ref[tile, :], ACROSS)


def stats_of(scores):
    peak = jnp.max(scores, axis=0, keepdims=True)
    return peak, jnp.sum(jnp.exp(scores - peak), axis=0, keepdims=True)


def joined(one, other):
    peak = jnp.maximum(one[0], other[0])
    return peak, one[1] * jnp.exp(one[0] - peak) + other[1] * jnp.exp(other[0] - peak)


def early_kernel(n, *refs):
    *linear, high_ref, low_ref, quad_ref, out_ref, stats_ref, weights = refs
    offset = load_packs(linear, weights, n)
    for tile in row_tiles(high_ref.shape[0]):
        scores = product(weights[...], high_ref[tile, :], low_ref[tile, :], ACROSS)
        scores = quad_ref[:, tile] + scores + offset
        out_ref[:, tile] = scores
        stats_ref[0:1, tile], stats_ref[1:2, tile] = stats_of(scores)


def half_tiles(half):
    for block in range(2):
        for part in row_tiles(half):
            yield slice(block * half + part.start, block * half + part.stop), block, part


def head_kernel(n, *refs):
    *linear, high_ref, low_ref, quad_ref, out_ref, weights = refs
    load_packs(linear, weights, n)
    columns = slice(0, weights.shape[1])
    for tile in row_tiles(high_ref.shape[0]):
        scores = product(weights[...], high_ref[tile, columns], low_ref[tile, columns], ACROSS)
        out_ref[:, tile] = quad_ref[:, tile] + scores


def last_kernel(n, *refs):
    *linear, high_ref, low_ref, quad_ref, early_ref, out_ref, stats_ref, weights = refs
    offset = load_packs(linear, weights, n)
    columns = slice(high_ref.shape[1] - weights.shape[1], high_ref.shape[1])
    for tile, block, part in half_tiles(stats_ref.shape[2]):
        scores = product(weights[...], high_ref[tile, columns], low_ref[tile, columns], ACROSS)
        scores = quad_ref[:, tile] + scores + offset
        out_ref[:, tile] = scores
        early = early_ref[0:1, tile], early_ref[1:2, tile]
        peak, total = joined(stats_of(scores), early)
        stats_ref[block, 0:1, part] = peak
        stats_ref[block, 1:2, part] = total


def score_call(body, out_shape, scratch, name, *operands, cost=None):
    return pl.pallas_call(
        body,
        out_shape=[jax.ShapeDtypeStruct(shape, F32) for shape in out_shape],
        scratch_shapes=[pltpu.VMEM(shape, BF16) for shape in scratch],
        cost_estimate=cost or HEAVY,
        compiler_params=params(24),
        name=name,
    )(*operands)


def moment_tiles(resp_ref, high_ref, low_ref, packs, n, rows=slice(None), add=False):
    for c in range(0, high_ref.shape[1], 2 * LANES):
        columns = slice(c, c + 2 * LANES)
        total = product(resp_ref[:, rows], high_ref[rows, columns], low_ref[rows, columns], WITHIN)
        for q, pack in enumerate(packs):
            for k in range(2):
                tile = slice((c // LANES + k) * n, (c // LANES + k + 1) * n)
                part = total[q * n : (q + 1) * n, k * LANES : (k + 1) * LANES]
                pack[tile, :] = pack[tile, :] + part if add else part


def first_kernel(n, sets, early_ref, late_ref, *refs):
    stats, (high_ref, low_ref, *packs, resp_ref) = refs[:sets], refs[sets:]
    comps = resp_ref.shape[0] // 2
    half = stats[0].shape[2]
    counts = jnp.zeros((comps, LANES), F32)
    for block in range(2):
        for part in row_tiles(half):
            tile = slice(block * half + part.start, block * half + part.stop)
            parts = [(ref[block, 0:1, part], ref[block, 1:2, part]) for ref in stats]
            peak = functools.reduce(jnp.maximum, [p for p, _ in parts])
            total = sum(t * jnp.exp(p - peak) for p, t in parts)
            scores = jnp.concatenate([early_ref[:, tile], late_ref[:, tile]])
            resp = jnp.exp(scores - peak) * (1.0 / total)
            resp_ref[:comps, tile], resp_ref[comps:, tile] = split(resp)
            counts += sum(resp[:, c : c + LANES] for c in range(0, resp.shape[1], LANES))
        rows = slice(block * half, (block + 1) * half)
        moment_tiles(resp_ref, high_ref, low_ref, packs, n, rows, block == 1)
    column = jnp.sum(counts, axis=1, keepdims=True)
    for q, pack in enumerate(packs):
        row = to_row(column[q * n : (q + 1) * n], LANES)
        pack[-8:, :] = jnp.broadcast_to(row, (8, LANES))


def first_moments(early, late, stats, high, low, n):
    rows, width = high.shape
    comps = early.shape[0] + late.shape[0]
    pack = jax.ShapeDtypeStruct((width // LANES * n + 8, LANES), F32)
    return pl.pallas_call(
        functools.partial(first_kernel, n, len(stats)),
        out_shape=[pack] * (comps // n) + [jax.ShapeDtypeStruct((2 * comps, rows), BF16)],
        cost_estimate=HEAVY,
        compiler_params=params(24),
        name="first_moments",
    )(early, late, *stats, high, low)


def second_kernel(n, resp_ref, high_ref, low_ref, *packs):
    moment_tiles(resp_ref, high_ref, low_ref, packs, n)


def second_moments(resp, high, low, n):
    pack = jax.ShapeDtypeStruct((high.shape[1] // LANES * n, LANES), F32)
    return pl.pallas_call(
        functools.partial(second_kernel, n),
        out_shape=[pack] * (resp.shape[0] // 2 // n),
        cost_estimate=HEAVY,
        compiler_params=params(24),
        name="second_moments",
    )(resp, high, low)


def kept_kernel(means_ref, variances_ref, mass_ref, first_ref, second_ref):
    means = means_ref[...]
    kept = 0.4 * to_column(mass_ref[...], means.shape[0])
    first_ref[...] = kept * means
    second_ref[...] = kept * (variances_ref[...] + means * means)


def kept_moments(means, variances, mass, ready):
    block = jax.ShapeDtypeStruct(means.shape, F32)
    return pl.pallas_call(
        kept_kernel,
        out_shape=(block, block),
        cost_estimate=HEAVY,
        compiler_params=params(16),
        name="kept_moments",
    )(means, variances, after(mass.reshape(1, -1), ready))


def update_kernel(
    scale,
    kept_first_ref,
    kept_second_ref,
    mass_ref,
    first_ref,
    second_ref,
    near_first_ref,
    near_second_ref,
    new_means_ref,
    new_variances_ref,
    new_mass_ref,
):
    n, width = kept_first_ref.shape
    tiles = width // LANES * n
    row = first_ref[tiles : tiles + 1, :n] + near_first_ref[tiles : tiles + 1, :n]
    new_row = 0.4 * mass_ref[...] + scale * row
    new_mass_ref[...] = new_row
    inverse = 1.0 / to_column(new_row, n)
    for c in range(width // LANES):
        lanes, tile = slice(c * LANES, (c + 1) * LANES), slice(c * n, (c + 1) * n)
        first = first_ref[tile, :] + near_first_ref[tile, :]
        second = second_ref[tile, :] + near_second_ref[tile, :]
        new_means = (kept_first_ref[:, lanes] + scale * first) * inverse
        new_means_ref[:, lanes] = new_means
        second_moment = kept_second_ref[:, lanes] + scale * second
        new_variances_ref[:, lanes] = second_moment * inverse - new_means * new_means


def update(scale, kept, mass, *sums):
    n = mass.shape[0]
    block = jax.ShapeDtypeStruct(kept[0].shape, F32)
    new_means, new_variances, new_mass = pl.pallas_call(
        functools.partial(update_kernel, scale),
        out_shape=(block, block, jax.ShapeDtypeStruct((1, n), F32)),
        cost_estimate=HEAVY,
        compiler_params=params(16),
        name="update",
    )(*kept, mass.reshape(1, n), *sums)
    return new_means, new_variances, new_mass.reshape(n)


def swap(value, axis, bit):
    size = lax.axis_size(axis)
    return lax.ppermute(value, axis, [(i, i ^ bit) for i in range(size)])


def vmem(value):
    return pltpu.with_memory_space_constraint(value, pltpu.VMEM)


def after(value, *others):
    return lax.optimization_barrier((value, *others))[0]


def gather_early(piece):
    bit = lax.axis_size("dp") // 4
    held = {0: piece}
    while bit > 1:
        held.update({q ^ bit: swap(value, "dp", 2 * bit) for q, value in held.items()})
        bit //= 2
    held[1] = swap(piece, "dp", 2)
    return held


def scatter_planes(first, second):
    held = [dict(enumerate(parts)) for parts in (first, second)]
    totals, near = [[parts.pop(0)] for parts in held], []
    planes, bit = len(first), 1
    while bit < planes:
        ready = []
        for parts in held:
            for q in sorted((q for q in parts if q & bit and q != bit), reverse=True):
                parts[q ^ bit] = parts[q ^ bit] + swap(after(parts.pop(q), *ready), "dp", 2 * bit)
                ready = [parts[q ^ bit]]
        for total, parts in zip(totals, held):
            part = swap(after(parts.pop(bit), *ready), "dp", 2 * bit)
            (near if bit == 1 else total).append(part)
        bit *= 2
    return *lax.optimization_barrier(tuple(sum(t[1:], t[0]) for t in totals)), *near


def merge(stats):
    peak = functools.reduce(jnp.maximum, [s[:, 0] for s in stats])
    total = sum(s[:, 1] * jnp.exp(s[:, 0] - peak) for s in stats)
    return jnp.stack([peak, total], axis=1)


def per_device(embeddings, comp_means, comp_variances, comp_mass):
    n = comp_means.shape[0]
    rows, width = embeddings.shape
    planes = lax.axis_size("dp") // 2
    variances = gather_early(comp_variances)
    linear = gather_early(coefficients(comp_means, comp_variances, comp_mass))
    other = swap(embeddings, "dp", 1)
    order = sorted(linear)
    late = [q for q in range(planes) if q not in linear]
    x_high, x_low, s_high, s_low = halves(embeddings, other)
    for q in late:
        variances[q] = swap(after(variances[q ^ 1], x_high), "dp", 2)
    n_early, n_late = n * len(order), n * len(late)

    def quad_scores(group, name, cost=None):
        comps = n * len(group)
        operands = (*(vmem(variances[q]) for q in group), s_high, s_low)
        body = functools.partial(quad_kernel, n)
        return score_call(body, [(comps, 2 * rows)], [(2 * comps, width)], name, *operands, cost=cost)[0]

    quad = quad_scores(order, "early_quad")
    head = width // LANES * 2 // 3
    heads, tails = [], []
    for q in late:
        source = after(linear[q ^ 1], quad)
        heads.append(vmem(swap(source[: head * n], "dp", 2)))
        tails.append(source[head * n :])
    early, early_stats = score_call(
        functools.partial(early_kernel, n),
        [(n_early, 2 * rows), (2, 2 * rows)],
        [(2 * n_early, width)],
        "early_scores",
        *(vmem(linear[q]) for q in order),
        x_high,
        x_low,
        quad,
        cost=LIGHT,
    )
    tails = [vmem(swap(after(tail, early), "dp", 2)) for tail in tails]
    (part,) = score_call(
        functools.partial(head_kernel, n),
        [(n_late, 2 * rows)],
        [(2 * n_late, head * LANES)],
        "late_head",
        *heads,
        x_high,
        x_low,
        quad_scores(late, "late_quad", LIGHT),
        cost=LIGHT,
    )
    last, stats = score_call(
        functools.partial(last_kernel, n),
        [(n_late, 2 * rows), (2, 2, rows)],
        [(2 * n_late, width - head * LANES)],
        "last_scores",
        *tails,
        x_high,
        x_low,
        part,
        early_stats,
    )
    stats = merge([stats, swap(stats, "dp", 1)[::-1]])
    stats = [stats] + [swap(stats, "comp", q) for q in range(1, lax.axis_size("comp"))]

    *first, resp = first_moments(early, last, stats, x_high, x_low, n)
    second = second_moments(resp, s_high, s_low, n)
    place = {q: i for i, q in enumerate(order + late)}
    first, second = ([parts[place[q]] for q in range(planes)] for parts in (first, second))
    kept = kept_moments(comp_means, comp_variances, comp_mass, resp)
    sums = scatter_planes(first, second)

    total_comps = n * lax.axis_size("dp") * lax.axis_size("comp")
    total_rows = embeddings.shape[0] * lax.axis_size("dp")
    scale = 0.6 * (total_comps / total_rows)
    return update(scale, kept, comp_mass, *sums)


def solution(mesh):
    placed = (P("dp", None), P(("comp", "dp"), None), P(("comp", "dp"), None), P(("comp", "dp")))
    return jax.shard_map(
        per_device,
        mesh=mesh,
        in_specs=placed,
        out_specs=(P(("comp", "dp"), None), P(("comp", "dp"), None), P(("comp", "dp"))),
        check_vma=False,
    )
```

```python
import functools

import jax
import jax.numpy as jnp
from jax import lax
from jax.experimental import pallas as pl
from jax.experimental.pallas import tpu as pltpu
from jax.sharding import PartitionSpec as P

F32 = jnp.float32
BF16 = jnp.bfloat16
LANES = 128
HEAVY = pl.CostEstimate(flops=10**10, bytes_accessed=10**8, transcendentals=0)
LIGHT = pl.CostEstimate(flops=10**8, bytes_accessed=10**6, transcendentals=0)
ACROSS = (((1,), (1,)), ((), ()))
WITHIN = (((1,), (0,)), ((), ()))


def params(megabytes):
    return pltpu.CompilerParams(vmem_limit_bytes=megabytes * 1024 * 1024)


def split(value):
    high = value.astype(BF16)
    return high, (value - high.astype(F32)).astype(BF16)


def diagonal(rows, columns):
    shape = (rows, columns)
    return lax.broadcasted_iota(jnp.int32, shape, 0) == lax.broadcasted_iota(jnp.int32, shape, 1)


def to_row(column, lanes):
    return jnp.sum(jnp.where(diagonal(column.shape[0], lanes), column, 0.0), axis=0, keepdims=True)


def to_column(row, rows):
    return jnp.sum(jnp.where(diagonal(rows, row.shape[1]), row, 0.0), axis=1, keepdims=True)


def coefficient_kernel(
    means_hbm, variances_hbm, mass_hbm, pack_ref, means_ref, variances_ref, mass_ref, sems
):
    sources = (variances_hbm, means_hbm, mass_hbm)
    targets = (variances_ref, means_ref, mass_ref)
    copies = [pltpu.make_async_copy(s, t, sems.at[i]) for i, (s, t) in enumerate(zip(sources, targets))]
    for copy in copies:
        copy.start()
    for copy in copies:
        copy.wait()
    n, width = means_ref.shape
    means, variances = means_ref[...], variances_ref[...]
    mean_prec = means * (1.0 / variances)
    sums = jnp.sum(jnp.log(variances) + means * mean_prec, axis=1, keepdims=True)
    offset = to_column(jnp.log(mass_ref[...]), n) - 0.5 * sums
    for c in range(width // LANES):
        pack_ref[c * n : (c + 1) * n, :] = mean_prec[:, c * LANES : (c + 1) * LANES]
    pack_ref[width // LANES * n :, :] = jnp.broadcast_to(to_row(offset, LANES), (8, LANES))


def coefficients(means, variances, mass):
    n, width = means.shape
    operands = (means, variances, mass.reshape(1, n))
    return pl.pallas_call(
        coefficient_kernel,
        in_specs=[pl.BlockSpec(memory_space=pl.ANY)] * 3,
        out_shape=jax.ShapeDtypeStruct((width // LANES * n + 8, LANES), F32),
        scratch_shapes=[
            pltpu.VMEM((n, width), F32),
            pltpu.VMEM((n, width), F32),
            pltpu.VMEM((1, n), F32),
            pltpu.SemaphoreType.DMA((3,)),
        ],
        cost_estimate=HEAVY,
        compiler_params=params(16),
        name="coefficients",
    )(*(pltpu.with_memory_space_constraint(x, pltpu.HBM) for x in operands))


def halves_kernel(own_ref, other_ref, xh_ref, xl_ref, sh_ref, sl_ref):
    def put(block):
        xh_ref[...], xl_ref[...] = split(block)
        sh_ref[...], sl_ref[...] = split(block * block)

    first = pl.program_id(0) < pl.num_programs(0) // 2

    @pl.when(first)
    def _():
        put(own_ref[...])

    @pl.when(jnp.logical_not(first))
    def _():
        put(other_ref[...])


def halves(own, other):
    rows, width = own.shape
    tile = min(256, rows)
    steps = rows // tile
    out = jax.ShapeDtypeStruct((2 * rows, width), BF16)
    return pl.pallas_call(
        halves_kernel,
        grid=(2 * steps,),
        in_specs=[
            pl.BlockSpec((tile, width), lambda i: (jnp.minimum(i, steps - 1), 0)),
            pl.BlockSpec((tile, width), lambda i: (jnp.maximum(i - steps, 0), 0)),
        ],
        out_specs=[pl.BlockSpec((tile, width), lambda i: (i, 0))] * 4,
        out_shape=[out] * 4,
        cost_estimate=HEAVY,
        compiler_params=params(16),
        name="halves",
    )(own, other)


def load_packs(packs, weights, n):
    comps, tiles = n * len(packs), weights.shape[1] // LANES
    for q, pack in enumerate(packs):
        for c in range(tiles):
            lanes = slice(c * LANES, (c + 1) * LANES)
            high, low = split(pack[c * n : (c + 1) * n, :])
            weights[q * n : (q + 1) * n, lanes] = high
            weights[comps + q * n : comps + (q + 1) * n, lanes] = low
    if packs[0].shape[0] == tiles * n:
        return None
    return jnp.concatenate([to_column(pack[tiles * n : tiles * n + 1, :], n) for pack in packs])


def load_variances(variances, weights, n):
    comps = n * len(variances)
    for q, ref in enumerate(variances):
        high, low = split(-0.5 * (1.0 / ref[...]))
        weights[q * n : (q + 1) * n, :] = high
        weights[comps + q * n : comps + (q + 1) * n, :] = low


def product(weights, high, low, dims):
    comps = weights.shape[0] // 2
    both = lax.dot_general(weights, high, dims, preferred_element_type=F32)
    rest = lax.dot_general(weights[:comps], low, dims, preferred_element_type=F32)
    return both[:comps] + (both[comps:] + rest)


def row_tiles(rows, tile=256):
    tile = min(tile, rows)
    return [slice(i, i + tile) for i in range(0, rows, tile)]


def quad_kernel(n, *refs):
    *variances, high_ref, low_ref, out_ref, weights = refs
    load_variances(variances, weights, n)
    for tile in row_tiles(high_ref.shape[0]):
        out_ref[:, tile] = product(weights[...], high_ref[tile, :], low_ref[tile, :], ACROSS)


def stats_of(scores):
    peak = jnp.max(scores, axis=0, keepdims=True)
    return peak, jnp.sum(jnp.exp(scores - peak), axis=0, keepdims=True)


def joined(one, other):
    peak = jnp.maximum(one[0], other[0])
    return peak, one[1] * jnp.exp(one[0] - peak) + other[1] * jnp.exp(other[0] - peak)


def early_kernel(n, *refs):
    *linear, high_ref, low_ref, quad_ref, out_ref, stats_ref, weights = refs
    offset = load_packs(linear, weights, n)
    for tile in row_tiles(high_ref.shape[0]):
        scores = product(weights[...], high_ref[tile, :], low_ref[tile, :], ACROSS)
        scores = quad_ref[:, tile] + scores + offset
        out_ref[:, tile] = scores
        stats_ref[0:1, tile], stats_ref[1:2, tile] = stats_of(scores)


def half_tiles(half):
    for block in range(2):
        for part in row_tiles(half):
            yield slice(block * half + part.start, block * half + part.stop), block, part


def head_kernel(n, *refs):
    *linear, high_ref, low_ref, quad_ref, out_ref, weights = refs
    load_packs(linear, weights, n)
    columns = slice(0, weights.shape[1])
    for tile in row_tiles(high_ref.shape[0]):
        scores = product(weights[...], high_ref[tile, columns], low_ref[tile, columns], ACROSS)
        out_ref[:, tile] = quad_ref[:, tile] + scores


def last_kernel(n, *refs):
    *linear, high_ref, low_ref, quad_ref, early_ref, out_ref, stats_ref, weights = refs
    offset = load_packs(linear, weights, n)
    columns = slice(high_ref.shape[1] - weights.shape[1], high_ref.shape[1])
    for tile, block, part in half_tiles(stats_ref.shape[2]):
        scores = product(weights[...], high_ref[tile, columns], low_ref[tile, columns], ACROSS)
        scores = quad_ref[:, tile] + scores + offset
        out_ref[:, tile] = scores
        early = early_ref[0:1, tile], early_ref[1:2, tile]
        peak, total = joined(stats_of(scores), early)
        stats_ref[block, 0:1, part] = peak
        stats_ref[block, 1:2, part] = total


def score_call(body, out_shape, scratch, name, *operands, cost=None):
    return pl.pallas_call(
        body,
        out_shape=[jax.ShapeDtypeStruct(shape, F32) for shape in out_shape],
        scratch_shapes=[pltpu.VMEM(shape, BF16) for shape in scratch],
        cost_estimate=cost or HEAVY,
        compiler_params=params(24),
        name=name,
    )(*operands)


def moment_tiles(resp_ref, high_ref, low_ref, packs, n, rows=slice(None), add=False):
    for c in range(0, high_ref.shape[1], 2 * LANES):
        columns = slice(c, c + 2 * LANES)
        total = product(resp_ref[:, rows], high_ref[rows, columns], low_ref[rows, columns], WITHIN)
        for q, pack in enumerate(packs):
            for k in range(2):
                tile = slice((c // LANES + k) * n, (c // LANES + k + 1) * n)
                part = total[q * n : (q + 1) * n, k * LANES : (k + 1) * LANES]
                pack[tile, :] = pack[tile, :] + part if add else part


def first_kernel(n, sets, early_ref, late_ref, *refs):
    stats, (high_ref, low_ref, *packs, resp_ref) = refs[:sets], refs[sets:]
    comps = resp_ref.shape[0] // 2
    half = stats[0].shape[2]
    counts = jnp.zeros((comps, LANES), F32)
    for block in range(2):
        for part in row_tiles(half):
            tile = slice(block * half + part.start, block * half + part.stop)
            parts = [(ref[block, 0:1, part], ref[block, 1:2, part]) for ref in stats]
            peak = functools.reduce(jnp.maximum, [p for p, _ in parts])
            total = sum(t * jnp.exp(p - peak) for p, t in parts)
            scores = jnp.concatenate([early_ref[:, tile], late_ref[:, tile]])
            resp = jnp.exp(scores - peak) * (1.0 / total)
            resp_ref[:comps, tile], resp_ref[comps:, tile] = split(resp)
            counts += sum(resp[:, c : c + LANES] for c in range(0, resp.shape[1], LANES))
        rows = slice(block * half, (block + 1) * half)
        moment_tiles(resp_ref, high_ref, low_ref, packs, n, rows, block == 1)
    column = jnp.sum(counts, axis=1, keepdims=True)
    for q, pack in enumerate(packs):
        row = to_row(column[q * n : (q + 1) * n], LANES)
        pack[-8:, :] = jnp.broadcast_to(row, (8, LANES))


def first_moments(early, late, stats, high, low, n):
    rows, width = high.shape
    comps = early.shape[0] + late.shape[0]
    pack = jax.ShapeDtypeStruct((width // LANES * n + 8, LANES), F32)
    return pl.pallas_call(
        functools.partial(first_kernel, n, len(stats)),
        out_shape=[pack] * (comps // n) + [jax.ShapeDtypeStruct((2 * comps, rows), BF16)],
        cost_estimate=HEAVY,
        compiler_params=params(24),
        name="first_moments",
    )(early, late, *stats, high, low)


def second_kernel(n, resp_ref, high_ref, low_ref, *packs):
    moment_tiles(resp_ref, high_ref, low_ref, packs, n)


def second_moments(resp, high, low, n):
    pack = jax.ShapeDtypeStruct((high.shape[1] // LANES * n, LANES), F32)
    return pl.pallas_call(
        functools.partial(second_kernel, n),
        out_shape=[pack] * (resp.shape[0] // 2 // n),
        cost_estimate=HEAVY,
        compiler_params=params(24),
        name="second_moments",
    )(resp, high, low)


def update_kernel(
    scale,
    means_ref,
    variances_ref,
    mass_ref,
    first_ref,
    second_ref,
    near_first_ref,
    near_second_ref,
    new_means_ref,
    new_variances_ref,
    new_mass_ref,
):
    n, width = means_ref.shape
    tiles = width // LANES * n
    row = first_ref[tiles : tiles + 1, :n] + near_first_ref[tiles : tiles + 1, :n]
    new_row = 0.4 * mass_ref[...] + scale * row
    new_mass_ref[...] = new_row
    inverse = 1.0 / to_column(new_row, n)
    kept = 0.4 * to_column(mass_ref[...], n)
    for c in range(width // LANES):
        lanes, tile = slice(c * LANES, (c + 1) * LANES), slice(c * n, (c + 1) * n)
        means, variances = means_ref[:, lanes], variances_ref[:, lanes]
        first = first_ref[tile, :] + near_first_ref[tile, :]
        second = second_ref[tile, :] + near_second_ref[tile, :]
        new_means = (kept * means + scale * first) * inverse
        new_means_ref[:, lanes] = new_means
        second_moment = kept * (variances + means * means) + scale * second
        new_variances_ref[:, lanes] = second_moment * inverse - new_means * new_means


def update(scale, means, variances, mass, *sums):
    n = mass.shape[0]
    block = jax.ShapeDtypeStruct(means.shape, F32)
    new_means, new_variances, new_mass = pl.pallas_call(
        functools.partial(update_kernel, scale),
        out_shape=(block, block, jax.ShapeDtypeStruct((1, n), F32)),
        cost_estimate=HEAVY,
        compiler_params=params(16),
        name="update",
    )(means, variances, mass.reshape(1, n), *sums)
    return new_means, new_variances, new_mass.reshape(n)


def swap(value, axis, bit):
    size = lax.axis_size(axis)
    return lax.ppermute(value, axis, [(i, i ^ bit) for i in range(size)])


def vmem(value):
    return pltpu.with_memory_space_constraint(value, pltpu.VMEM)


def after(value, *others):
    return lax.optimization_barrier((value, *others))[0]


def gather_early(piece):
    bit = lax.axis_size("dp") // 4
    held = {0: piece}
    while bit > 1:
        held.update({q ^ bit: swap(value, "dp", 2 * bit) for q, value in held.items()})
        bit //= 2
    held[1] = swap(piece, "dp", 2)
    return held


def scatter_planes(first, second):
    held = [dict(enumerate(parts)) for parts in (first, second)]
    totals, near = [[parts.pop(0)] for parts in held], []
    planes, bit = len(first), 1
    while bit < planes:
        ready = []
        for parts in held:
            for q in sorted((q for q in parts if q & bit and q != bit), reverse=True):
                parts[q ^ bit] = parts[q ^ bit] + swap(after(parts.pop(q), *ready), "dp", 2 * bit)
                ready = [parts[q ^ bit]]
        for total, parts in zip(totals, held):
            part = swap(after(parts.pop(bit), *ready), "dp", 2 * bit)
            (near if bit == 1 else total).append(part)
        bit *= 2
    return *lax.optimization_barrier(tuple(sum(t[1:], t[0]) for t in totals)), *near


def merge(stats):
    peak = functools.reduce(jnp.maximum, [s[:, 0] for s in stats])
    total = sum(s[:, 1] * jnp.exp(s[:, 0] - peak) for s in stats)
    return jnp.stack([peak, total], axis=1)


def per_device(embeddings, comp_means, comp_variances, comp_mass):
    n = comp_means.shape[0]
    rows, width = embeddings.shape
    planes = lax.axis_size("dp") // 2
    variances = gather_early(comp_variances)
    linear = gather_early(coefficients(comp_means, comp_variances, comp_mass))
    other = swap(embeddings, "dp", 1)
    order = sorted(linear)
    late = [q for q in range(planes) if q not in linear]
    x_high, x_low, s_high, s_low = halves(embeddings, other)
    for q in late:
        variances[q] = swap(after(variances[q ^ 1], x_high), "dp", 2)
    n_early, n_late = n * len(order), n * len(late)

    def quad_scores(group, name, cost=None):
        comps = n * len(group)
        operands = (*(vmem(variances[q]) for q in group), s_high, s_low)
        body = functools.partial(quad_kernel, n)
        return score_call(body, [(comps, 2 * rows)], [(2 * comps, width)], name, *operands, cost=cost)[0]

    quad = quad_scores(order, "early_quad")
    head = width // LANES // 2
    heads, tails = [], []
    for q in late:
        source = after(linear[q ^ 1], quad)
        heads.append(vmem(swap(source[: head * n], "dp", 2)))
        tails.append(source[head * n :])
    early, early_stats = score_call(
        functools.partial(early_kernel, n),
        [(n_early, 2 * rows), (2, 2 * rows)],
        [(2 * n_early, width)],
        "early_scores",
        *(vmem(linear[q]) for q in order),
        x_high,
        x_low,
        quad,
        cost=LIGHT,
    )
    tails = [vmem(swap(after(tail, early), "dp", 2)) for tail in tails]
    (part,) = score_call(
        functools.partial(head_kernel, n),
        [(n_late, 2 * rows)],
        [(2 * n_late, head * LANES)],
        "late_head",
        *heads,
        x_high,
        x_low,
        quad_scores(late, "late_quad", LIGHT),
        cost=LIGHT,
    )
    last, stats = score_call(
        functools.partial(last_kernel, n),
        [(n_late, 2 * rows), (2, 2, rows)],
        [(2 * n_late, width - head * LANES)],
        "last_scores",
        *tails,
        x_high,
        x_low,
        part,
        early_stats,
    )
    stats = merge([stats, swap(stats, "dp", 1)[::-1]])
    stats = [stats] + [swap(stats, "comp", q) for q in range(1, lax.axis_size("comp"))]

    *first, resp = first_moments(early, last, stats, x_high, x_low, n)
    second = second_moments(resp, s_high, s_low, n)
    place = {q: i for i, q in enumerate(order + late)}
    first, second = ([parts[place[q]] for q in range(planes)] for parts in (first, second))
    sums = scatter_planes(first, second)

    total_comps = n * lax.axis_size("dp") * lax.axis_size("comp")
    total_rows = embeddings.shape[0] * lax.axis_size("dp")
    scale = 0.6 * (total_comps / total_rows)
    return update(scale, comp_means, comp_variances, comp_mass, *sums)


def solution(mesh):
    placed = (P("dp", None), P(("comp", "dp"), None), P(("comp", "dp"), None), P(("comp", "dp")))
    return jax.shard_map(
        per_device,
        mesh=mesh,
        in_specs=placed,
        out_specs=(P(("comp", "dp"), None), P(("comp", "dp"), None), P(("comp", "dp"))),
        check_vma=False,
    )
```
